32 devices in a mesh: dp: 4 (over y, x), row: 2 (over core), col: 4 (over z).
Axes of the slice: x: 2, y: 2, z: 4, core: 2. Of those that a mesh axis runs over, the one named last changes fastest.
Arguments:
- hidden: bfloat16 [16384, 1024], P(('dp', 'row'), 'col'), may hold values from -6 to 6
- encoder: bfloat16 [16384, 1024], P(('dp', 'row'), 'col'), may hold values from -6 to 6
- cotangent: bfloat16 [16384, 1024], P(('dp', 'row'), 'col'), may hold values from -6 to 6
- answer_length: int32 [16], P('dp'), may hold values from 256 to 1024, as said below
- passage_length: int32 [16], P('dp'), may hold values from 256 to 1024, as said below
- self_input: bfloat16 [1024, 3, 1024], P('col', None, 'row'), may hold values from -0.1875 to 0.1875
- self_output: bfloat16 [1024, 1024], P('row', 'col'), may hold values from -1.5 to 1.5
- cross_query: bfloat16 [1024, 1024], P('col', 'row'), may hold values from -0.1875 to 0.1875
- cross_memory: bfloat16 [1024, 2, 1024], P('col', None, 'row'), may hold values from -0.1875 to 0.1875
- cross_output: bfloat16 [1024, 1024], P('row', 'col'), may hold values from -3 to 3
- expand_weight: bfloat16 [1024, 4096], P('col', 'row'), may hold values from -0.1875 to 0.1875
- shrink_weight: bfloat16 [4096, 1024], P('row', 'col'), may hold values from -0.09375 to 0.09375
- head_bias: float32 [4, 1024], P(None, 'row'), may hold values from -2 to 2
- expand_bias: float32 [4096], P('row'), may hold values from -2 to 2
- model_bias: float32 [3, 1024], P(None, 'col'), may hold values from -2 to 2
- norm_gain: float32 [3, 1024], P(None, 'col'), may hold values from 0.5 to 1.5
- norm_shift: float32 [3, 1024], P(None, 'col'), may hold values from -1.5 to 1.5
Outputs:
- output: float32 [16384, 1024], P(('dp', 'row'), 'col')
- grad_hidden: float32 [16384, 1024], P(('dp', 'row'), 'col')
- grad_encoder: float32 [16384, 1024], P(('dp', 'row'), 'col')
- grad_self_input: float32 [1024, 3, 1024], P('col', None, 'row')
- grad_self_output: float32 [1024, 1024], P('row', 'col')
- grad_cross_query: float32 [1024, 1024], P('col', 'row')
- grad_cross_memory: float32 [1024, 2, 1024], P('col', None, 'row')
- grad_cross_output: float32 [1024, 1024], P('row', 'col')
- grad_expand: float32 [1024, 4096], P('col', 'row')
- grad_shrink: float32 [4096, 1024], P('row', 'col')
- grad_head_bias: float32 [4, 1024], P(None, 'row')
- grad_expand_bias: float32 [4096], P('row')
- grad_model_bias: float32 [3, 1024], P(None, 'col')
- grad_norm_gain: float32 [3, 1024], P(None, 'col')
- grad_norm_shift: float32 [3, 1024], P(None, 'col')
The draws below stay inside these ranges and needn't reach their ends.
Inputs may be any that keep to these rules, and one draw needn't show every extreme that they name: `answer_length`: in every draw one sequence has 1024 live decoder tokens and one has 256. `passage_length`: in every draw one sequence has 1024 live encoder tokens and one has 256.
All inputs are finite; a program needn't handle non-finite values.
Results may differ from the reference program's by a relative error of at most 0.023.
Values may be sent and summed in bfloat16 or wider, within the bound.
No kernel may reach another device: no remote copies, remote signals or barrier semaphores. Data moves between devices by JAX's collectives and lax.ppermute only.
A program may use at most 448 MiB of HBM per device.

```python
import math
import jax
import jax.numpy as jnp
from jax import lax

D = 1024
HEADS = 16
HEAD_DIM = 64
FF = 4096
SLOT = 1024
SEQ_BLK = 1
SEQS = 16
TOKENS = 16384


def spread_lengths(key):
    first_key, second_key = jax.random.split(key)
    drawn = jax.random.randint(first_key, (SEQS,), SLOT // 4, SLOT + 1)
    order = jax.random.permutation(second_key, SEQS)
    drawn = drawn.at[order[0]].set(SLOT)
    drawn = drawn.at[order[1]].set(SLOT // 4)
    return drawn.astype(jnp.int32)


def draw_answer_length(key, part):
    return spread_lengths(jax.random.fold_in(key, 17))


def draw_passage_length(key, part):
    return spread_lengths(jax.random.fold_in(key, 29))


def steps_of(own_key, dims, pieces, smallest, largest):
    level, own = 1.0, jax.random.fold_in(own_key, 6)
    for axis_at, blocks in pieces:
        draws = jnp.exp(jax.random.uniform(jax.random.fold_in(own, axis_at), (blocks,), jnp.float32, smallest / len(pieces), largest / len(pieces)))
        level = level * jnp.repeat(draws, dims[axis_at] // blocks).reshape([-1 if axis == axis_at else 1 for axis in range(len(dims))])
    return level


def centred(key, shape, scale, most, shards=(), dtype=jnp.bfloat16):
    values = jax.random.normal(key, shape, jnp.float32) * scale
    if len(shards) > 0:
        values = steps_of(key, shape, shards, -0.22, 0.18) * values
    return jnp.clip(values, min=-most, max=most).astype(dtype)


def setup_inputs(seed: int = 0) -> dict:
    key_of = jax.random.split(jax.random.key(seed), 18)
    return {
        "hidden": centred(key_of[0], (TOKENS, D), 1.0, 6.0, ((0, 8), (1, 4))),
        "encoder": centred(key_of[1], (TOKENS, D), 1.0, 6.0, ((0, 8), (1, 4))),
        "cotangent": centred(key_of[2], (TOKENS, D), 1.0, 6.0, ((0, 8), (1, 4))),
        "answer_length": draw_answer_length(jax.random.fold_in(key_of[17], 71), 0),
        "passage_length": draw_passage_length(jax.random.fold_in(key_of[17], 71), 0),
        "self_input": centred(key_of[5], (D, 3, D), D ** -0.5, 0.1875, ((0, 4), (2, 2))),
        "self_output": centred(key_of[6], (D, D), (16 * D // SLOT) ** -0.5, 1.5, ((0, 2), (1, 4))),
        "cross_query": centred(key_of[7], (D, D), D ** -0.5, 0.1875, ((0, 4), (1, 2))),
        "cross_memory": centred(key_of[8], (D, 2, D), D ** -0.5, 0.1875, ((0, 4), (2, 2))),
        "cross_output": centred(key_of[9], (D, D), (4 * D // SLOT) ** -0.5, 3.0, ((0, 2), (1, 4))),
        "expand_weight": centred(key_of[10], (D, FF), D ** -0.5, 0.1875, ((0, 4), (1, 2))),
        "shrink_weight": centred(key_of[11], (FF, D), FF ** -0.5, 0.09375, ((0, 2), (1, 4))),
        "head_bias": centred(key_of[12], (4, D), 0.3, 2.0, ((1, 2),), jnp.float32),
        "expand_bias": centred(key_of[13], (FF,), 0.3, 2.0, ((0, 2),), jnp.float32),
        "model_bias": centred(key_of[14], (3, D), 0.3, 2.0, ((1, 4),), jnp.float32),
        "norm_gain": jnp.clip(1.0 + 0.1 * jax.random.normal(key_of[15], (3, D), jnp.float32), 0.5, 1.5),
        "norm_shift": centred(key_of[16], (3, D), 0.2, 1.5, ((1, 4),), jnp.float32),
    }


@jax.custom_vjp
def low(v):
    return lax.optimization_barrier(v.astype(jnp.bfloat16)).astype(jnp.float32)

@jax.custom_vjp
def low_back(v):
    return v

def low_keep(v):
    return (low(v), None)

def low_pass(kept, grad):
    return (grad,)

def back_keep(v):
    return (v, None)

def back_low(kept, grad):
    return (low(grad),)
low.defvjp(low_keep, low_pass)
low_back.defvjp(back_keep, back_low)

def product(left, right):
    return jnp.dot(left, right, precision=lax.Precision.HIGHEST, preferred_element_type=jnp.float32)

def both_ways(values):
    return low(low_back(values))

def normalize(residual, gain_row, shift_row):
    center = lax.optimization_barrier(jnp.mean(residual, axis=-1, keepdims=True))
    spread = lax.optimization_barrier(jnp.mean(jnp.square(residual - center), axis=-1, keepdims=True))
    return (residual - center) * lax.rsqrt(spread + 1e-05) * gain_row + shift_row

def self_mask(length_limit):
    places = jnp.arange(SLOT)
    return (places[None, :] <= places[:, None]) & (places[None, :] < length_limit)

def cross_mask(length_limit):
    places = jnp.arange(SLOT)
    return jnp.broadcast_to(places[None, :] < length_limit, (SLOT, SLOT))

def attend(query_rows, key_rows, value_rows, allowed):
    factor = 1.0 / math.sqrt(HEAD_DIM)
    scores = jnp.einsum('qhd,khd->hqk', query_rows, key_rows, precision=lax.Precision.HIGHEST) * factor
    scores = jnp.where(allowed[None], low_back(scores), -1000000000.0)
    weights = low(jax.nn.softmax(scores, axis=-1))
    return jnp.einsum('hqk,khd->qhd', weights, value_rows, precision=lax.Precision.HIGHEST)

def self_one(member):
    return attend(member[0], member[1], member[2], self_mask(member[3]))

def cross_one(member):
    return attend(member[0], member[1], member[2], cross_mask(member[3]))

def decoder_layer(params, source_rows, encoder_rows, answers, passages):
    self_input, self_output, cross_query, cross_memory, cross_output, expand_weight, shrink_weight, head_bias, expand_bias, model_bias, norm_gain, norm_shift = params
    layout = (answers.shape[0], SLOT, HEADS, HEAD_DIM)
    packed = product(source_rows, self_input.reshape(D, 3 * D)).reshape(-1, 3, D)
    query_rows = both_ways(packed[:, 0] + head_bias[0])
    key_rows = both_ways(packed[:, 1])
    value_rows = both_ways(packed[:, 2] + head_bias[1])
    mixture = lax.map(jax.checkpoint(self_one), (query_rows.reshape(layout), key_rows.reshape(layout), value_rows.reshape(layout), answers))
    mixture = both_ways(mixture.reshape(-1, D))
    residual = source_rows + low_back(product(mixture, self_output) + model_bias[0])
    first_norm = low(normalize(residual, norm_gain[0], norm_shift[0]))
    cross_rows = both_ways(product(first_norm, cross_query) + head_bias[2])
    memory = product(encoder_rows, cross_memory.reshape(D, 2 * D)).reshape(-1, 2, D)
    cross_keys = both_ways(memory[:, 0])
    cross_values = both_ways(memory[:, 1] + head_bias[3])
    recall = lax.map(jax.checkpoint(cross_one), (cross_rows.reshape(layout), cross_keys.reshape(layout), cross_values.reshape(layout), passages))
    recall = both_ways(recall.reshape(-1, D))
    residual = first_norm + low_back(product(recall, cross_output) + model_bias[1])
    second_norm = low(normalize(residual, norm_gain[1], norm_shift[1]))
    expanded = low_back(product(second_norm, expand_weight) + expand_bias)
    activated = low(jax.nn.gelu(expanded, approximate=False))
    residual = second_norm + low_back(product(activated, shrink_weight) + model_bias[2])
    result = normalize(residual, norm_gain[2], norm_shift[2])
    places = jnp.arange(SLOT)
    valid_rows = (places[None, :] < answers[:, None]).reshape(-1, 1)
    return jnp.where(valid_rows, result, 0.0)

def reference(hidden, encoder, cotangent, answer_length, passage_length, self_input, self_output, cross_query, cross_memory, cross_output, expand_weight, shrink_weight, head_bias, expand_bias, model_bias, norm_gain, norm_shift):
    params = tuple((weight.astype(jnp.float32) for weight in (self_input, self_output, cross_query, cross_memory, cross_output, expand_weight, shrink_weight, head_bias, expand_bias, model_bias, norm_gain, norm_shift)))
    groups = answer_length.shape[0] // SEQ_BLK
    group_rows = SEQ_BLK * SLOT
    stacked = (hidden.astype(jnp.float32).reshape(groups, group_rows, D), encoder.astype(jnp.float32).reshape(groups, group_rows, D), cotangent.astype(jnp.float32).reshape(groups, group_rows, D), answer_length.reshape(groups, SEQ_BLK), passage_length.reshape(groups, SEQ_BLK))

    def scan_step(totals, member):
        source, memory_rows, upstream, answers, passages = member

        def forward(weights_all, source_rows, encoder_rows):
            return decoder_layer(weights_all, source_rows, encoder_rows, answers, passages)
        result, pullback = jax.vjp(forward, params, source, memory_rows)
        weight_grads, source_grad, memory_grad = pullback(upstream)
        totals = jax.tree.map(jnp.add, totals, weight_grads)
        return (totals, (result, source_grad, memory_grad))
    zeros = jax.tree.map(jnp.zeros_like, params)
    totals, (result, source_grad, memory_grad) = lax.scan(scan_step, zeros, stacked)
    return (result.reshape(-1, D), source_grad.reshape(-1, D), memory_grad.reshape(-1, D), totals[0], totals[1], totals[2], totals[3], totals[4], totals[5], totals[6], totals[7], totals[8], totals[9], totals[10], totals[11])
```

```python
import math

import jax
import jax.numpy as jnp
from jax import lax
from jax.sharding import PartitionSpec as P

HEAD_DIM = 64
SLOT = 1024
BF = jnp.bfloat16
F32 = jnp.float32


def dot(left, right):
    return jnp.dot(left, right, preferred_element_type=F32)


def dot_flip(left, right):
    return lax.dot_general(left, right, (((1,), (1,)), ((), ())), preferred_element_type=F32)


def outer_sum(left, right):
    return lax.dot_general(left, right, (((0,), (0,)), ((), ())), preferred_element_type=F32)


class Plan:
    def __init__(self, mesh):
        self.n_row = mesh.shape["row"]
        self.n_col = mesh.shape["col"]
        self.n_dp = mesh.shape["dp"]
        self.share = SLOT // self.n_row
        self.row = lax.axis_index("row")
        self.col = lax.axis_index("col")
        self.pair = self.n_row == 2
        self.offset = self.row * self.share if self.pair else jnp.int32(0)
        self.positions = (jnp.arange(SLOT, dtype=jnp.int32) + self.offset) % SLOT
        self.own_positions = self.row * self.share + jnp.arange(self.share, dtype=jnp.int32)

    def swap(self, values):
        return lax.ppermute(values, "row", [(0, 1), (1, 0)])

    def gather_rows(self, values):
        if self.pair:
            return jnp.concatenate([values, self.swap(values)], axis=0)
        return lax.all_gather(values, "row", axis=0, tiled=True)

    def scatter_product(self, left, right, flipped=False):
        times = dot_flip if flipped else dot
        if self.pair:
            away = self.swap(times(left[self.share :], right))
            return times(left[: self.share], right) + away
        return lax.psum_scatter(times(left, right), "row", scatter_dimension=0, tiled=True)

    def spread(self, values):
        width = values.shape[1]
        if self.pair:
            seqs = self.n_col // 2
            parts = values.reshape(seqs, 2, self.share, width)
            keep = lax.dynamic_index_in_dim(parts, self.row, 1, keepdims=False)
            give = lax.dynamic_index_in_dim(parts, 1 - self.row, 1, keepdims=False)
            take = self.swap(give)
            first = self.row == 0
            ordered = jnp.concatenate(
                [jnp.where(first, keep, take), jnp.where(first, take, keep)], axis=0
            )
        else:
            whole = lax.all_gather(values, "row", axis=0, tiled=True)
            parts = whole.reshape(self.n_col, self.n_row, self.share, width)
            ordered = lax.dynamic_index_in_dim(parts, self.row, 1, keepdims=False)
        moved = lax.all_to_all(ordered, "col", 0, 2, tiled=True)
        return moved.reshape(self.share, width * self.n_col)

    def collect(self, values):
        width = values.shape[1] // self.n_col
        moved = lax.all_to_all(values.reshape(1, self.share, -1), "col", 2, 0, tiled=True)
        if self.pair:
            seqs = self.n_col // 2
            first = self.row == 0
            low, high = moved[:seqs], moved[seqs:]
            keep = jnp.where(first, low, high)
            take = self.swap(jnp.where(first, high, low))
            parts = jnp.stack(
                [jnp.where(first, keep, take), jnp.where(first, take, keep)], axis=1
            )
            return parts.reshape(-1, width)
        whole = lax.all_gather(moved, "row", axis=1, tiled=True).reshape(-1, width)
        rows = whole.shape[0] // self.n_row
        return lax.dynamic_slice_in_dim(whole, self.row * rows, rows, axis=0)


def normalize(residual, gain_row, shift_row):
    center = jnp.mean(residual, axis=-1, keepdims=True)
    moved = residual - center
    inverse = lax.rsqrt(jnp.mean(moved * moved, axis=-1, keepdims=True) + 1e-05)
    normal = moved * inverse
    return normal * gain_row + shift_row, normal, inverse


def norm_back(upstream, normal, inverse, gain_row):
    scaled = upstream * gain_row
    plain = jnp.mean(scaled, axis=-1, keepdims=True)
    cross = jnp.mean(scaled * normal, axis=-1, keepdims=True)
    return inverse * (scaled - plain - normal * cross)


def exact_gelu(values):
    return jax.nn.gelu(values, approximate=False)


def build_mask(positions, length, causal):
    allowed = jnp.broadcast_to(positions[None, :] < length, (SLOT, SLOT))
    if causal:
        allowed = allowed & (positions[None, :] <= positions[:, None])
    return allowed


def score_block(query, key, allowed):
    factor = 1.0 / math.sqrt(HEAD_DIM)
    scores = jnp.einsum("qhd,khd->hqk", query, key, preferred_element_type=F32) * factor
    return jnp.where(allowed[None], scores, -1000000000.0)


def split_heads(values):
    return values.reshape(SLOT, -1, HEAD_DIM)


def attention_forward(query, key, value, allowed):
    query, key, value = (split_heads(v) for v in (query, key, value))
    scores = score_block(query, key, allowed)
    highest = jnp.max(scores, axis=-1, keepdims=True)
    raised = jnp.exp(scores - highest)
    denominator = jnp.sum(raised, axis=-1, keepdims=True)
    weights = (raised / denominator).astype(BF)
    mixture = jnp.einsum("hqk,khd->qhd", weights, value, preferred_element_type=F32)
    return mixture.reshape(SLOT, -1).astype(BF), highest + jnp.log(denominator)


def attention_backward(query, key, value, allowed, logsum, upstream):
    query, key, value, upstream = (split_heads(v) for v in (query, key, value, upstream))
    factor = 1.0 / math.sqrt(HEAD_DIM)
    weights = jnp.exp(score_block(query, key, allowed) - logsum)
    value_grad = jnp.einsum("hqk,qhd->khd", weights.astype(BF), upstream, preferred_element_type=F32)
    weight_grad = jnp.einsum("qhd,khd->hqk", upstream, value, preferred_element_type=F32)
    inner = jnp.sum(weights * weight_grad, axis=-1, keepdims=True)
    score_grad = (weights * (weight_grad - inner)).astype(BF)
    query_grad = jnp.einsum("hqk,khd->qhd", score_grad, key, preferred_element_type=F32) * factor
    key_grad = jnp.einsum("hqk,qhd->khd", score_grad, query, preferred_element_type=F32) * factor
    return tuple(g.reshape(SLOT, -1).astype(BF) for g in (query_grad, key_grad, value_grad))


def gather_weight(piece, axis):
    return lax.all_gather(piece, "col", axis=axis, tiled=True)


def reduce_grad(grad, axis):
    part = lax.psum_scatter(grad.astype(BF), "col", scatter_dimension=axis, tiled=True)
    return lax.psum(part, "dp").astype(F32)


def layer(mesh):
    def body(
        hidden,
        encoder,
        cotangent,
        answer_length,
        passage_length,
        self_input,
        self_output,
        cross_query,
        cross_memory,
        cross_output,
        expand_weight,
        shrink_weight,
        head_bias,
        expand_bias,
        model_bias,
        norm_gain,
        norm_shift,
    ):
        plan = Plan(mesh)
        heads = self_output.shape[0]
        answers = lax.dynamic_index_in_dim(answer_length, plan.col, keepdims=False)
        passages = lax.dynamic_index_in_dim(passage_length, plan.col, keepdims=False)
        valid = (plan.own_positions < answers).astype(F32)[:, None]
        norms = lax.all_gather(
            jnp.concatenate([model_bias, norm_gain, norm_shift]), "col", axis=1, tiled=True
        )
        bias_rows, gain_rows, shift_rows = norms[:3], norms[3:6], norms[6:]

        own_x = plan.spread(hidden)
        w_self = gather_weight(self_input, 0).reshape(-1, 3 * heads)
        own_encoder = plan.spread(encoder)
        own_cotangent = plan.spread(cotangent)
        w_self_out = gather_weight(self_output, 1)
        w_query = gather_weight(cross_query, 0)
        w_memory = gather_weight(cross_memory, 0).reshape(-1, 2 * heads)
        w_cross_out = gather_weight(cross_output, 1)
        w_expand = gather_weight(expand_weight, 0)
        w_shrink = gather_weight(shrink_weight, 1)

        full_x = plan.gather_rows(own_x)
        packed = dot(full_x, w_self)
        query = (packed[:, :heads] + head_bias[0]).astype(BF)
        key = packed[:, heads : 2 * heads].astype(BF)
        value = (packed[:, 2 * heads :] + head_bias[1]).astype(BF)
        self_mask = build_mask(plan.positions, answers, True)
        mixture, self_logsum = attention_forward(query, key, value, self_mask)
        branch = plan.scatter_product(mixture, w_self_out) + bias_rows[0]
        normed, normal_one, inverse_one = normalize(own_x.astype(F32) + branch, gain_rows[0], shift_rows[0])
        own_first = normed.astype(BF)
        full_first = plan.gather_rows(own_first)
        cross_q = (dot(full_first, w_query) + head_bias[2]).astype(BF)
        full_encoder = plan.gather_rows(own_encoder)
        memory = dot(full_encoder, w_memory)
        cross_k = memory[:, :heads].astype(BF)
        cross_v = (memory[:, heads:] + head_bias[3]).astype(BF)
        cross_mask = build_mask(plan.positions, passages, False)
        recall, cross_logsum = attention_forward(cross_q, cross_k, cross_v, cross_mask)
        branch = plan.scatter_product(recall, w_cross_out) + bias_rows[1]
        normed, normal_two, inverse_two = normalize(own_first.astype(F32) + branch, gain_rows[1], shift_rows[1])
        own_second = normed.astype(BF)
        full_second = plan.gather_rows(own_second)
        expanded = dot(full_second, w_expand) + expand_bias
        gelu_value, gelu_pull = jax.vjp(exact_gelu, expanded)
        activated = gelu_value.astype(BF)
        branch = plan.scatter_product(activated, w_shrink) + bias_rows[2]
        normed, normal_three, inverse_three = normalize(
            own_second.astype(F32) + branch, gain_rows[2], shift_rows[2]
        )
        output = plan.collect((normed * valid).astype(BF)).astype(F32)

        up_three = own_cotangent.astype(F32) * valid
        resid_three = norm_back(up_three, normal_three, inverse_three, gain_rows[2])
        own_dshrink = resid_three.astype(BF)
        full_dshrink = plan.gather_rows(own_dshrink)
        g_shrink = reduce_grad(outer_sum(activated, full_dshrink), 1)
        d_expanded = gelu_pull(dot_flip(full_dshrink, w_shrink))[0].astype(BF)
        g_expand = reduce_grad(outer_sum(full_second, d_expanded), 0)
        up_two = resid_three + plan.scatter_product(d_expanded, w_expand, True)
        resid_two = norm_back(up_two, normal_two, inverse_two, gain_rows[1])
        own_dcross = resid_two.astype(BF)
        full_dcross = plan.gather_rows(own_dcross)
        d_recall = dot_flip(full_dcross, w_cross_out).astype(BF)
        g_cross_out = reduce_grad(outer_sum(recall, full_dcross), 1)
        d_cross_q, d_cross_k, d_cross_v = attention_backward(
            cross_q, cross_k, cross_v, cross_mask, cross_logsum, d_recall
        )
        up_one = resid_two + plan.scatter_product(d_cross_q, w_query, True)
        g_query = reduce_grad(outer_sum(full_first, d_cross_q), 0)
        d_memory = jnp.concatenate([d_cross_k, d_cross_v], axis=1)
        g_encoder = plan.collect(plan.scatter_product(d_memory, w_memory, True).astype(BF)).astype(F32)
        g_memory = reduce_grad(outer_sum(full_encoder, d_memory), 0)
        resid_one = norm_back(up_one, normal_one, inverse_one, gain_rows[0])
        own_dself = resid_one.astype(BF)
        full_dself = plan.gather_rows(own_dself)
        d_mixture = dot_flip(full_dself, w_self_out).astype(BF)
        g_self_out = reduce_grad(outer_sum(mixture, full_dself), 1)
        d_query, d_key, d_value = attention_backward(
            query, key, value, self_mask, self_logsum, d_mixture
        )
        d_packed = jnp.concatenate([d_query, d_key, d_value], axis=1)
        g_hidden = plan.collect(
            (resid_one + plan.scatter_product(d_packed, w_self, True)).astype(BF)
        ).astype(F32)
        g_self = reduce_grad(outer_sum(full_x, d_packed), 0)

        def rows_of(values):
            return jnp.sum(values, axis=0, dtype=F32)

        wide = jnp.stack(
            [rows_of(v) for v in (own_dself, own_dcross, own_dshrink)]
            + [rows_of(u * n) for u, n in ((up_one, normal_one), (up_two, normal_two), (up_three, normal_three))]
            + [rows_of(v) for v in (up_one, up_two, up_three)]
        )
        narrow = jnp.concatenate(
            [rows_of(v) for v in (d_query, d_value, d_cross_q, d_cross_v, d_expanded)]
        )
        wide = lax.psum(wide, ("dp", "row", "col"))
        narrow = lax.psum(narrow, ("dp", "col"))
        width = model_bias.shape[1]
        wide = lax.dynamic_slice_in_dim(wide, plan.col * width, width, axis=1)
        return (
            output,
            g_hidden,
            g_encoder,
            g_self.reshape(self_input.shape),
            g_self_out,
            g_query,
            g_memory.reshape(cross_memory.shape),
            g_cross_out,
            g_expand,
            g_shrink,
            narrow[: 4 * heads].reshape(4, heads),
            narrow[4 * heads :],
            wide[:3],
            wide[3:6],
            wide[6:],
        )

    return body


def solution(mesh):
    rows = P(("dp", "row"), "col")
    weights = (
        P("col", None, "row"),
        P("row", "col"),
        P("col", "row"),
        P("col", None, "row"),
        P("row", "col"),
        P("col", "row"),
        P("row", "col"),
        P(None, "row"),
        P("row"),
        P(None, "col"),
        P(None, "col"),
        P(None, "col"),
    )
    return jax.shard_map(
        layer(mesh),
        mesh=mesh,
        in_specs=(rows, rows, rows, P("dp"), P("dp")) + weights,
        out_specs=(rows, rows, rows) + weights,
        check_vma=False,
    )
```

```python
import functools
import math

import jax
import jax.numpy as jnp
from jax import lax
from jax.experimental import pallas as pl
from jax.experimental.pallas import tpu as pltpu
from jax.sharding import PartitionSpec as P

HEAD_DIM = 64
SLOT = 1024
BF = jnp.bfloat16
F32 = jnp.float32


def tie(*values):
    return lax.optimization_barrier(values)


def dot(left, right):
    return jnp.dot(left, right, preferred_element_type=F32)


def dot_flip(left, right):
    return lax.dot_general(left, right, (((1,), (1,)), ((), ())), preferred_element_type=F32)


def outer_sum(left, right):
    return lax.dot_general(left, right, (((0,), (0,)), ((), ())), preferred_element_type=F32)

def in_vmem(body, name, scalars, arrays, outs):
    count = len(arrays)

    def kernel(info, *refs):
        body(info, refs[:count], refs[count:])

    def spec(shape):
        return pl.BlockSpec(shape, lambda i, info: (0,) * len(shape))

    return pl.pallas_call(
        kernel,
        out_shape=outs,
        grid_spec=pltpu.PrefetchScalarGridSpec(
            num_scalar_prefetch=1,
            grid=(1,),
            in_specs=[spec(a.shape) for a in arrays],
            out_specs=[spec(o.shape) for o in outs],
        ),
        compiler_params=pltpu.CompilerParams(vmem_limit_bytes=56 * 2**20),
        cost_estimate=small_cost(),
        name=name,
    )(scalars, *arrays)


def lanes_at(start):
    return pl.ds(pl.multiple_of(start, 128), 128)


def join_columns(pieces, places):
    rows, width = pieces[0].shape

    def body(info, ins, outs):
        for i, piece in enumerate(ins):
            start = pl.multiple_of(info[i] * width, width)
            outs[0][:, pl.ds(start, width)] = piece[...]

    out = jax.ShapeDtypeStruct((rows, width * len(pieces)), pieces[0].dtype)
    return in_vmem(body, "join_columns", jnp.stack(places), pieces, [out])[0]


def join_rows(pieces, places):
    rows, width = pieces[0].shape

    def body(info, ins, outs):
        for i, piece in enumerate(ins):
            start = pl.multiple_of(info[i] * rows, rows)
            outs[0][pl.ds(start, rows), :] = piece[...].astype(F32)

    out = jax.ShapeDtypeStruct((rows * len(pieces), width), F32)
    return in_vmem(body, "join_rows", jnp.stack(places), pieces, [out])[0]


def sum_blocks(terms, axis, n_col, col):
    shape = terms[0].shape
    width = shape[axis] // n_col
    block = (shape[0], width) if axis == 1 else (width, shape[1])

    def body(info, ins, outs):
        for owner in range(n_col):
            start = pl.multiple_of(lax.rem(info[0] - owner + n_col, n_col) * width, width)
            at = (slice(None), pl.ds(start, width)) if axis == 1 else (pl.ds(start, width), slice(None))
            outs[0][owner] = sum(t[at].astype(F32) for t in ins).astype(BF)

    out = jax.ShapeDtypeStruct((n_col, *block), BF)
    return in_vmem(body, "sum_blocks", col[None], terms, [out])[0]


class Plan:
    def __init__(self, mesh):
        self.n_row = mesh.shape["row"]
        self.n_col = mesh.shape["col"]
        self.share = SLOT // self.n_row
        self.row = lax.axis_index("row")
        self.col = lax.axis_index("col")
        self.pair = self.n_row == 2
        self.offset = self.row * self.share if self.pair else jnp.int32(0)
        self.positions = (jnp.arange(SLOT, dtype=jnp.int32) + self.offset) % SLOT
        self.own_positions = self.row * self.share + jnp.arange(self.share, dtype=jnp.int32)

    def swap(self, values):
        return lax.ppermute(values, "row", [(0, 1), (1, 0)])

    def shift(self, values, k):
        n = self.n_col
        return lax.ppermute(values, "col", [(i, (i + k) % n) for i in range(n)])

    def block(self, other):
        return (self.col - other) % self.n_col

    def reorder(self, blocks):
        return jnp.stack(
            [lax.dynamic_index_in_dim(blocks, self.block(i), 0, keepdims=False) for i in range(self.n_col)]
        )

    def gather_rows(self, values):
        if self.pair:
            return jnp.concatenate([values, self.swap(values)], axis=0)
        return lax.all_gather(values, "row", axis=0, tiled=True)

    def scatter_product(self, left, right, flipped=False):
        times = dot_flip if flipped else dot
        if self.pair:
            away = self.swap(times(left[self.share :], right))
            return times(left[: self.share], right) + away
        return lax.psum_scatter(times(left, right), "row", scatter_dimension=0, tiled=True)

    def turn(self, t, back=False):
        pairs = []
        for r in range(2):
            for z in range(self.n_col):
                h, j = divmod(z ^ t, 2)
                pairs.append((r * self.n_col + z, h * self.n_col + 2 * r + j))
        return [(b, a) for a, b in pairs] if back else pairs

    def spread(self, values):
        width = values.shape[1]
        if self.pair and self.n_col == 4:
            parts = values.reshape(4, self.share, width)
            takes = []
            for t in range(4):
                h, j = (self.col ^ t) // 2, (self.col ^ t) % 2
                give = lax.dynamic_index_in_dim(parts, 2 * j + h, 0, keepdims=False)
                takes.append(lax.ppermute(give, ("row", "col"), self.turn(t)))
            return tuple(takes)
        whole = lax.all_gather(values, "row", axis=0, tiled=True)
        parts = whole.reshape(self.n_col, self.n_row, self.share, width)
        ordered = lax.dynamic_index_in_dim(parts, self.row, 1, keepdims=False)
        moved = self.reorder(lax.all_to_all(ordered, "col", 0, 0, tiled=True))
        return (jnp.transpose(moved, (1, 0, 2)).reshape(self.share, -1),)

    def spread_end(self, takes):
        if len(takes) == 1:
            return takes[0]
        seen = 2 * self.row + self.col % 2
        return join_columns(takes, [self.block(t ^ seen) for t in range(4)])

    def collect(self, values):
        width = values.shape[1] // self.n_col
        if self.pair and self.n_col == 4:
            seen = 2 * self.row + self.col % 2
            takes = []
            for t in range(4):
                give = lax.dynamic_slice_in_dim(values, self.block(t ^ seen) * width, width, axis=1)
                takes.append(lax.ppermute(give, ("row", "col"), self.turn(t, back=True)))
            return tuple(takes)
        blocks = jnp.transpose(values.reshape(self.share, self.n_col, width), (1, 0, 2))
        moved = lax.all_to_all(self.reorder(blocks), "col", 0, 0, tiled=True)
        whole = lax.all_gather(moved, "row", axis=1, tiled=True).reshape(-1, width)
        rows = whole.shape[0] // self.n_row
        return (lax.dynamic_slice_in_dim(whole, self.row * rows, rows, axis=0),)

    def collect_end(self, takes):
        if len(takes) == 1:
            return takes[0].astype(F32)
        places = [2 * ((self.col ^ t) % 2) + (self.col ^ t) // 2 for t in range(4)]
        return join_rows(takes, places)


def normalize(residual, gain_row, shift_row):
    center = jnp.mean(residual, axis=-1, keepdims=True)
    moved = residual - center
    inverse = lax.rsqrt(jnp.mean(moved * moved, axis=-1, keepdims=True) + 1e-05)
    normal = moved * inverse
    return normal * gain_row + shift_row, normal, inverse


def norm_back(upstream, normal, inverse, gain_row):
    scaled = upstream * gain_row
    plain = jnp.mean(scaled, axis=-1, keepdims=True)
    cross = jnp.mean(scaled * normal, axis=-1, keepdims=True)
    return inverse * (scaled - plain - normal * cross)


def gelu_and_slope(values):
    cdf = 0.5 + 0.5 * lax.erf(values * math.sqrt(0.5))
    density = jnp.exp(-0.5 * values * values) * (1.0 / math.sqrt(2.0 * math.pi))
    return (values * cdf).astype(BF), (cdf + values * density).astype(BF)


LANES = 2 * HEAD_DIM
SPAN = 256
NEVER = -1000000000.0


def dot_last(left, right):
    return lax.dot_general(left, right, (((1,), (1,)), ((), ())), preferred_element_type=F32)


def place_of(start, offset):
    return pl.multiple_of(lax.rem(start + offset, SLOT), SPAN)


def heads_apart(rows):
    low = lax.broadcasted_iota(jnp.int32, rows.shape, 1) < HEAD_DIM
    none = jnp.zeros_like(rows)
    return jnp.where(low, rows, none), jnp.where(low, none, rows)


def key_spans(count):
    if count == 1:
        return [(0, SPAN)]
    return [(0, (count - 1) * SPAN), ((count - 1) * SPAN, count * SPAN)]


def score_spans(keys_ref, query, count, limit):
    parts = []
    for start, stop in key_spans(count):
        scores = dot_last(keys_ref[start:stop, :], query)
        if stop == count * SPAN:
            places = lax.broadcasted_iota(jnp.int32, scores.shape, 0)
            if limit is None:
                allowed = places <= lax.broadcasted_iota(jnp.int32, scores.shape, 1)
            else:
                allowed = places < limit - start
            scores = jnp.where(allowed, scores, NEVER)
        parts.append(scores)
    return parts


def for_each_block(causal, query_length, key_length, run, skip):
    blocks = SLOT // SPAN
    if causal:
        for i in range(blocks):
            pl.when(i * SPAN < query_length)(functools.partial(run, i * SPAN, i + 1))
            pl.when(i * SPAN >= query_length)(functools.partial(skip, i * SPAN))
        return
    live = lax.div(query_length + (SPAN - 1), SPAN)
    spans = lax.div(key_length + (SPAN - 1), SPAN)
    for count in range(1, blocks + 1):

        @pl.when(spans == count)
        def _(count=count):
            @pl.loop(0, live)
            def _(i):
                run(pl.multiple_of(i * SPAN, SPAN), count)

    @pl.loop(live, blocks)
    def _(i):
        skip(pl.multiple_of(i * SPAN, SPAN))


def forward_kernel(causal, info, query_ref, key_ref, value_ref, out_ref, logsum_ref, keys, values_t):
    offset, query_length, key_length = info[0], info[1], info[2]
    half = SLOT // 2
    for start in (0, half):
        stored = place_of(start, offset)
        keys[start : start + half, :] = key_ref[pl.ds(stored, half), :]
        values_t[:, start : start + half] = value_ref[pl.ds(stored, half), :].T

    def run(start, count):
        stored = place_of(start, offset)
        scaled = query_ref[pl.ds(stored, SPAN), :] * (1.0 / math.sqrt(HEAD_DIM))
        outs = []
        for head, query in enumerate(heads_apart(scaled)):
            parts = score_spans(keys, query, count, None if causal else key_length)
            highest = functools.reduce(jnp.maximum, [jnp.max(s, axis=0, keepdims=True) for s in parts])
            raised = [jnp.exp(s - highest) for s in parts]
            below = sum(jnp.sum(e, axis=0, keepdims=True) for e in raised)
            mixed = sum(
                jnp.dot(
                    values_t[head * HEAD_DIM : (head + 1) * HEAD_DIM, a:b],
                    e.astype(BF),
                    preferred_element_type=F32,
                )
                for (a, b), e in zip(key_spans(count), raised)
            )
            outs.append(mixed * (1.0 / below))
            logsum_ref[0, head : head + 1, pl.ds(start, SPAN)] = highest + jnp.log(below)
        out_ref[pl.ds(stored, SPAN), :] = jnp.concatenate(outs, axis=0).T.astype(BF)

    def skip(start):
        out_ref[pl.ds(place_of(start, offset), SPAN), :] = jnp.zeros((SPAN, LANES), BF)

    for_each_block(causal, query_length, key_length, run, skip)


def backward_kernel(
    causal, info, query_ref, key_ref, value_ref, up_ref, logsum_ref, *refs
):
    if causal:
        packed_ref, keys, keys_t, values, key_sum, value_sum = refs
        query_out, other_out = packed_ref, packed_ref
        base = LANES
    else:
        query_out, other_out, keys, keys_t, values, key_sum, value_sum = refs
        base = 0
    offset, query_length, key_length = info[0], info[1], info[2]
    half = SLOT // 2
    for start in (0, half):
        stored = place_of(start, offset)
        block = key_ref[pl.ds(stored, half), :]
        keys[start : start + half, :] = block
        keys_t[:, start : start + half] = block.T
        values[start : start + half, :] = value_ref[pl.ds(stored, half), :]
    key_sum[...] = jnp.zeros_like(key_sum)
    value_sum[...] = jnp.zeros_like(value_sum)
    factor = 1.0 / math.sqrt(HEAD_DIM)

    def run(start, count):
        stored = place_of(start, offset)
        queries = heads_apart(query_ref[pl.ds(stored, SPAN), :] * factor)
        ups = heads_apart(up_ref[pl.ds(stored, SPAN), :])
        spans = key_spans(count)
        weights, grads, outs = [], [], []
        for head in range(2):
            logsum = logsum_ref[0, head : head + 1, pl.ds(start, SPAN)]
            parts = score_spans(keys, queries[head], count, None if causal else key_length)
            parts = [jnp.exp(s - logsum) for s in parts]
            pulls = [dot_last(values[a:b, :], ups[head]) for a, b in spans]
            inner = sum(jnp.sum(p * g, axis=0, keepdims=True) for p, g in zip(parts, pulls))
            pulls = [(p * (g - inner)).astype(BF) for p, g in zip(parts, pulls)]
            outs.append(
                sum(
                    jnp.dot(
                        keys_t[head * HEAD_DIM : (head + 1) * HEAD_DIM, a:b],
                        g,
                        preferred_element_type=F32,
                    )
                    for (a, b), g in zip(spans, pulls)
                )
            )
            weights.append([p.astype(BF) for p in parts])
            grads.append(pulls)
        query_out[pl.ds(stored, SPAN), 0:LANES] = (
            jnp.concatenate(outs, axis=0) * factor
        ).T.astype(BF)
        for at, (a, b) in enumerate(spans):
            for head in range(2):
                value_sum[a:b, :] += jnp.dot(weights[head][at], ups[head], preferred_element_type=F32)
                key_sum[a:b, :] += jnp.dot(grads[head][at], queries[head], preferred_element_type=F32)

    def skip(start):
        query_out[pl.ds(place_of(start, offset), SPAN), 0:LANES] = jnp.zeros((SPAN, LANES), BF)

    for_each_block(causal, query_length, key_length, run, skip)
    for start in (0, half):
        stored = place_of(start, offset)
        other_out[pl.ds(stored, half), base : base + LANES] = key_sum[start : start + half, :].astype(BF)
        other_out[pl.ds(stored, half), base + LANES : base + 2 * LANES] = value_sum[
            start : start + half, :
        ].astype(BF)


def column_block(width, of):
    return pl.BlockSpec((SLOT, width), lambda i, info: (0, of(i)))


LOGSUM_BLOCK = pl.BlockSpec((1, 2, SLOT), lambda i, info: (i, 0, 0))


def small_cost():
    return pl.CostEstimate(flops=0, bytes_accessed=2**16, transcendentals=0)


def attend(causal, info, query, keys, pairs):
    step = 3 if causal else 2
    first = 1 if causal else 0
    return pl.pallas_call(
        functools.partial(forward_kernel, causal),
        out_shape=(
            jax.ShapeDtypeStruct((SLOT, pairs * LANES), BF),
            jax.ShapeDtypeStruct((pairs, 2, SLOT), F32),
        ),
        grid_spec=pltpu.PrefetchScalarGridSpec(
            num_scalar_prefetch=1,
            grid=(pairs,),
            in_specs=[
                column_block(LANES, (lambda i: 3 * i) if causal else (lambda i: i)),
                column_block(LANES, lambda i: step * i + first),
                column_block(LANES, lambda i: step * i + first + 1),
            ],
            out_specs=(column_block(LANES, lambda i: i), LOGSUM_BLOCK),
            scratch_shapes=[pltpu.VMEM((SLOT, LANES), BF), pltpu.VMEM((LANES, SLOT), BF)],
        ),
        compiler_params=pltpu.CompilerParams(vmem_limit_bytes=48 * 2**20),
        cost_estimate=small_cost(),
        name="attend",
    )(info, query, keys, keys)


def attend_back(causal, info, query, keys, logsum, upstream, pairs):
    step = 3 if causal else 2
    first = 1 if causal else 0
    if causal:
        out_shape = jax.ShapeDtypeStruct((SLOT, pairs * 3 * LANES), BF)
        out_specs = column_block(3 * LANES, lambda i: i)
    else:
        out_shape = (
            jax.ShapeDtypeStruct((SLOT, pairs * LANES), BF),
            jax.ShapeDtypeStruct((SLOT, pairs * 2 * LANES), BF),
        )
        out_specs = (column_block(LANES, lambda i: i), column_block(2 * LANES, lambda i: i))
    return pl.pallas_call(
        functools.partial(backward_kernel, causal),
        out_shape=out_shape,
        grid_spec=pltpu.PrefetchScalarGridSpec(
            num_scalar_prefetch=1,
            grid=(pairs,),
            in_specs=[
                column_block(LANES, (lambda i: 3 * i) if causal else (lambda i: i)),
                column_block(LANES, lambda i: step * i + first),
                column_block(LANES, lambda i: step * i + first + 1),
                column_block(LANES, lambda i: i),
                LOGSUM_BLOCK,
            ],
            out_specs=out_specs,
            scratch_shapes=[
                pltpu.VMEM((SLOT, LANES), BF),
                pltpu.VMEM((LANES, SLOT), BF),
                pltpu.VMEM((SLOT, LANES), BF),
                pltpu.VMEM((SLOT, LANES), F32),
                pltpu.VMEM((SLOT, LANES), F32),
            ],
        ),
        compiler_params=pltpu.CompilerParams(vmem_limit_bytes=48 * 2**20),
        cost_estimate=small_cost(),
        name="attend_back",
    )(info, query, keys, keys, upstream, logsum)


def build_mask(positions, length, causal):
    allowed = jnp.broadcast_to(positions[None, :] < length, (SLOT, SLOT))
    if causal:
        allowed = allowed & (positions[None, :] <= positions[:, None])
    return allowed


def score_block(query, key, allowed):
    factor = 1.0 / math.sqrt(HEAD_DIM)
    scores = jnp.einsum("qhd,khd->hqk", query, key, preferred_element_type=F32) * factor
    return jnp.where(allowed[None], scores, -1000000000.0)


def split_heads(values):
    return values.reshape(SLOT, -1, HEAD_DIM)


def attention_forward(query, key, value, allowed):
    query, key, value = (split_heads(v) for v in (query, key, value))
    scores = score_block(query, key, allowed)
    highest = jnp.max(scores, axis=-1, keepdims=True)
    raised = jnp.exp(scores - highest)
    denominator = jnp.sum(raised, axis=-1, keepdims=True)
    weights = (raised / denominator).astype(BF)
    mixture = jnp.einsum("hqk,khd->qhd", weights, value, preferred_element_type=F32)
    return mixture.reshape(SLOT, -1).astype(BF), highest + jnp.log(denominator)


def attention_backward(query, key, value, allowed, logsum, upstream):
    query, key, value, upstream = (split_heads(v) for v in (query, key, value, upstream))
    factor = 1.0 / math.sqrt(HEAD_DIM)
    weights = jnp.exp(score_block(query, key, allowed) - logsum)
    value_grad = jnp.einsum("hqk,qhd->khd", weights.astype(BF), upstream, preferred_element_type=F32)
    weight_grad = jnp.einsum("qhd,khd->hqk", upstream, value, preferred_element_type=F32)
    inner = jnp.sum(weights * weight_grad, axis=-1, keepdims=True)
    score_grad = (weights * (weight_grad - inner)).astype(BF)
    query_grad = jnp.einsum("hqk,khd->qhd", score_grad, key, preferred_element_type=F32) * factor
    key_grad = jnp.einsum("hqk,qhd->khd", score_grad, query, preferred_element_type=F32) * factor
    return tuple(g.reshape(SLOT, -1).astype(BF) for g in (query_grad, key_grad, value_grad))


def interleave(arrays, n):
    rows = arrays[0].shape[0]
    return jnp.stack([a.reshape(rows, n, -1) for a in arrays], axis=2).reshape(rows, -1)


def apart(array, n, count):
    rows = array.shape[0]
    parts = array.reshape(rows, n, count, -1)
    return [parts[:, :, i].reshape(rows, -1) for i in range(count)]


def self_attention(plan, packed, length, n):
    if packed.shape[1] == 3 * n * LANES:
        info = jnp.stack([plan.offset, length, length])
        return attend(True, info, packed, packed, n)
    mask = build_mask(plan.positions, length, True)
    return attention_forward(*apart(packed, n, 3), mask)


def self_attention_back(plan, packed, length, n, logsum, upstream):
    if packed.shape[1] == 3 * n * LANES:
        info = jnp.stack([plan.offset, length, length])
        return attend_back(True, info, packed, packed, logsum, upstream, n)
    mask = build_mask(plan.positions, length, True)
    return interleave(attention_backward(*apart(packed, n, 3), mask, logsum, upstream), n)


def cross_attention(plan, query, memory, query_length, key_length, n):
    if query.shape[1] == n * LANES:
        info = jnp.stack([plan.offset, query_length, key_length])
        return attend(False, info, query, memory, n)
    mask = build_mask(plan.positions, key_length, False)
    return attention_forward(query, *apart(memory, n, 2), mask)


def cross_attention_back(plan, query, memory, query_length, key_length, n, logsum, upstream):
    if query.shape[1] == n * LANES:
        info = jnp.stack([plan.offset, query_length, key_length])
        return attend_back(False, info, query, memory, logsum, upstream, n)
    mask = build_mask(plan.positions, key_length, False)
    first, *rest = attention_backward(query, *apart(memory, n, 2), mask, logsum, upstream)
    return first, interleave(rest, n)


ORDER = (0, 2, 3, 1)


class Group:
    def __init__(self, weights, n):
        self.weights = weights
        self.n = n
        self.plans = []
        row = 0
        for axis, groups, local in weights:
            if axis == 0:
                tall, count = local.shape[0], local.shape[1] // n // 128
            else:
                tall, count = local.shape[0] // n, local.shape[1] // 128
            self.plans.append((row, tall, count))
            row += tall * count
        self.rows = row

    def fits(self):
        return all(
            (local.shape[1] % (groups * self.n * 128) == 0 if axis == 0 else local.shape[0] % (self.n * 128) == 0)
            for axis, groups, local in self.weights
        )

    def local_block(self, ref, at, which, block):
        axis, groups, local = self.weights[at]
        _, tall, count = self.plans[at]
        if axis == 0:
            per = count // groups
            i, b = divmod(block, per)
            return ref[:, lanes_at((i * self.n * per + b) * 128 + which * (per * 128))]
        return ref[pl.ds(pl.multiple_of(which * tall, tall), tall), block * 128 : (block + 1) * 128]

    def pack(self, me):
        def body(info, ins, outs):
            for at, (row, tall, count) in enumerate(self.plans):
                for block in range(count):
                    start = row + block * tall
                    outs[0][start : start + tall, :] = self.local_block(ins[at], at, info[0], block)

        out = jax.ShapeDtypeStruct((self.rows, 128), BF)
        return in_vmem(body, "pack", me[None], [w[2] for w in self.weights], [out])[0]

    def assemble(self, me, n_col, moved):
        half = self.rows * (n_col - 1) // 2
        count_w = len(self.weights)
        outs = []
        for axis, groups, local in self.weights:
            shape = (local.shape[0] * n_col, local.shape[1]) if axis == 0 else (local.shape[0], local.shape[1] * n_col)
            outs.append(jax.ShapeDtypeStruct(shape, BF))

        def body(info, ins, outs):
            local_refs, moved_refs = ins[:count_w], ins[count_w:]
            for at, (row, tall, count) in enumerate(self.plans):
                axis = self.weights[at][0]
                width = self.weights[at][2].shape[1]
                for place, j in enumerate(ORDER):
                    for k in range(n_col):
                        for block in range(count):
                            if k == 0:
                                value = self.local_block(local_refs[at], at, info[j], block)
                            else:
                                start = (k - 1) * self.rows + row + block * tall
                                ref = moved_refs[j]
                                if j == 3 and start >= half:
                                    ref, start = moved_refs[4], start - half
                                value = ref[start : start + tall, :]
                            if axis == 0:
                                column = (place * count + block) * 128
                                outs[at][k * tall : (k + 1) * tall, column : column + 128] = value
                            else:
                                column = k * width + block * 128
                                outs[at][place * tall : (place + 1) * tall, column : column + 128] = value

        which = jnp.stack([me ^ j for j in range(self.n)])
        return in_vmem(body, "assemble", which, [w[2] for w in self.weights] + list(moved), outs)


def pick_others(every, n_col, col):
    rows = every.shape[0] // n_col
    return pl.pallas_call(
        lambda info, source, target: target.__setitem__(Ellipsis, source[...]),
        out_shape=jax.ShapeDtypeStruct(((n_col - 1) * rows, every.shape[1]), every.dtype),
        grid_spec=pltpu.PrefetchScalarGridSpec(
            num_scalar_prefetch=1,
            grid=(n_col - 1,),
            in_specs=[
                pl.BlockSpec(
                    (rows, every.shape[1]), lambda k, info: (lax.rem(info[0] - k - 1 + n_col, n_col), 0)
                )
            ],
            out_specs=pl.BlockSpec((rows, every.shape[1]), lambda k, info: (k, 0)),
        ),
        name="pick_others",
    )(col[None], every)


class Blocks:
    def __init__(self, mesh, plan):
        self.n = mesh.shape["dp"]
        assert self.n == len(ORDER)
        self.plan = plan
        self.me = lax.axis_index("dp")

    def hop(self, values, step):
        return lax.ppermute(values, "dp", [(i, i ^ step) for i in range(self.n)])

    def own(self, values, axis, j=0, wait=0):
        shape = values.shape
        parts = values.reshape(shape[:axis] + (self.n, shape[axis] // self.n) + shape[axis + 1 :])
        return lax.dynamic_index_in_dim(parts, (self.me ^ j) + wait, axis, keepdims=False)

    def weave(self, values):
        return jnp.stack([self.own(values, values.ndim - 1, j) for j in ORDER], axis=-2)

    def unweave(self, values):
        order = jnp.array([ORDER.index(j) for j in range(self.n)])
        return jnp.concatenate(
            [
                lax.dynamic_index_in_dim(values, order[self.me ^ q], 0, keepdims=False)
                for q in range(self.n)
            ]
        )

    def others_by_shift(self, piece):
        return jnp.concatenate([self.plan.shift(piece, k) for k in range(1, self.plan.n_col)], axis=0)

    def others_by_gather(self, piece):
        every = lax.all_gather(piece, "col", axis=0, tiled=True)
        return pick_others(every, self.plan.n_col, self.plan.col)

    def hops(self, others):
        return self.hop(others, 1), self.hop(others, 2)

    def corner(self, over):
        half = over[0].shape[0] // 2
        return self.hop(over[1][:half], 1), self.hop(over[0][half:], 2)

    def whole(self, weight):
        axis, groups, local = weight
        every = self.plan.reorder(lax.all_gather(local, "col", axis=0))
        if axis == 0:
            every = every.reshape(-1, groups, local.shape[1] // groups)
            return jnp.stack([self.weave(every[:, i]) for i in range(groups)], axis=2).reshape(every.shape[0], -1)
        every = jnp.moveaxis(every, 0, 1).reshape(local.shape[0], -1)
        parts = every.reshape(self.n, -1, every.shape[1])
        picked = [lax.dynamic_index_in_dim(parts, self.me ^ j, 0, keepdims=False) for j in ORDER]
        return jnp.concatenate(picked, axis=0)

    def reduce_start(self, product, first):
        return self.hop(product(2, 4) if first == 1 else product(1, 3), first)

    def reduce_next(self, product, first, axis, got):
        got = jnp.split(got, 2, axis=axis)
        to_middle, to_base = got if first == 1 else got[::-1]
        middle = product(1, 2) if first == 1 else product(3, 4)
        return product(0, 1), to_base, self.hop(middle + to_middle, 3 - first)

    def reduce_col(self, terms, axis, offload):
        shape = terms[0].shape
        if offload and all(s % 128 == 0 for s in shape):
            parts = sum_blocks(terms, axis, self.plan.n_col, self.plan.col)
            return lax.psum_scatter(parts, "col", scatter_dimension=0, tiled=False)
        part = sum(t.astype(F32) for t in terms).astype(BF)
        parts = part.reshape(shape[:axis] + (self.plan.n_col, -1) + shape[axis + 1 :])
        if offload:
            parts = self.plan.reorder(jnp.moveaxis(parts, axis, 0))
            return lax.psum_scatter(parts, "col", scatter_dimension=0, tiled=False)
        blocks = [lax.index_in_dim(parts, k, axis, keepdims=False) for k in range(self.plan.n_col)]
        got = [blocks[0]] + [self.plan.shift(blocks[k], -k) for k in range(1, self.plan.n_col)]
        return sum(g.astype(F32) for g in got).astype(BF)

    def share_parts(self, part):
        return lax.all_gather(part, "dp", axis=0)


def total(values, mesh, axes):
    for axis in axes:
        size = mesh.shape[axis]
        step = 1
        while step < size:
            values = values + lax.ppermute(values, axis, [(i, i ^ step) for i in range(size)])
            step *= 2
    return values


def layer(mesh):
    def body(
        hidden,
        encoder,
        cotangent,
        answer_length,
        passage_length,
        self_input,
        self_output,
        cross_query,
        cross_memory,
        cross_output,
        expand_weight,
        shrink_weight,
        head_bias,
        expand_bias,
        model_bias,
        norm_gain,
        norm_shift,
    ):
        plan = Plan(mesh)
        blocks = Blocks(mesh, plan)
        n = blocks.n
        me = blocks.me
        width = model_bias.shape[1]
        heads = self_output.shape[0]
        part = heads // n
        hidden_part = expand_bias.shape[0] // n
        answers = lax.dynamic_index_in_dim(answer_length, plan.col, keepdims=False)
        passages = lax.dynamic_index_in_dim(passage_length, plan.col, keepdims=False)
        valid = (plan.own_positions < answers).astype(F32)[:, None]

        group_one = Group([(0, 3, self_input.reshape(width, -1)), (1, 1, self_output)], n)
        group_two = Group(
            [(0, 1, cross_query), (0, 2, cross_memory.reshape(width, -1)), (1, 1, cross_output)], n
        )
        group_three = Group([(0, 1, expand_weight), (1, 1, shrink_weight)], n)
        tiled = group_one.fits() and group_two.fits() and group_three.fits()
        if tiled:
            others_one = blocks.others_by_shift(group_one.pack(me))
            over_one = blocks.hops(others_one)
            corner_one = blocks.corner(over_one)
            w_self, w_self_out = group_one.assemble(me, plan.n_col, (others_one, *over_one, *corner_one))
        else:
            w_self, w_self_out = (blocks.whole(w) for w in group_one.weights)
            w_query, w_memory, w_cross_out = (blocks.whole(w) for w in group_two.weights)
            w_expand, w_shrink = (blocks.whole(w) for w in group_three.weights)
        x_takes = plan.spread(hidden)
        if tiled:
            pieces = [group_two.pack(me), group_three.pack(me)]
            x_takes, pieces = tie(x_takes, pieces)
            others_two, others_three = (blocks.others_by_gather(p) for p in pieces)
        own_norms = jnp.concatenate([model_bias, norm_gain, norm_shift])
        norms = jnp.concatenate(
            [own_norms] + [plan.shift(own_norms, k) for k in range(1, plan.n_col)], axis=1
        )
        bias_rows, gain_rows, shift_rows = norms[:3], norms[3:6], norms[6:]

        head_parts = blocks.weave(head_bias)
        none = jnp.zeros((n, part), F32)
        self_bias = jnp.stack([head_parts[0], none, head_parts[1]], axis=1).reshape(-1)
        query_bias = head_parts[2].reshape(-1)
        memory_bias = jnp.stack([none, head_parts[3]], axis=1).reshape(-1)
        hidden_bias = blocks.weave(expand_bias).reshape(-1)

        own_x = plan.spread_end(x_takes)
        full_x = plan.gather_rows(own_x)
        packed = (dot(full_x, w_self) + self_bias).astype(BF)
        if tiled:
            packed, encoder, others_two = tie(packed, encoder, others_two)
            over_two = blocks.hops(others_two)
        encoder_takes = plan.spread(encoder)
        mixture, self_logsum = self_attention(plan, packed, answers, n)
        if tiled:
            mixture, encoder_takes, over_two = tie(mixture, encoder_takes, over_two)
            corner_two = blocks.corner(over_two)
        branch = plan.scatter_product(mixture, w_self_out) + bias_rows[0]
        normed, normal_one, inverse_one = normalize(own_x.astype(F32) + branch, gain_rows[0], shift_rows[0])
        own_first = normed.astype(BF)
        if tiled:
            own_first, corner_two, others_three, cotangent = tie(
                own_first, corner_two, others_three, cotangent
            )
            over_three = blocks.hops(others_three)
        own_encoder = plan.spread_end(encoder_takes)
        full_encoder = plan.gather_rows(own_encoder)
        full_first = plan.gather_rows(own_first)
        if tiled:
            w_query, w_memory, w_cross_out = group_two.assemble(
                me, plan.n_col, (others_two, *over_two, *corner_two)
            )
        memory = (dot(full_encoder, w_memory) + memory_bias).astype(BF)
        cross_q = (dot(full_first, w_query) + query_bias).astype(BF)
        cotangent_takes = plan.spread(cotangent)
        recall, cross_logsum = cross_attention(plan, cross_q, memory, answers, passages, n)
        if tiled:
            recall, over_three, cotangent_takes = tie(recall, over_three, cotangent_takes)
            corner_three = blocks.corner(over_three)
        branch = plan.scatter_product(recall, w_cross_out) + bias_rows[1]
        normed, normal_two, inverse_two = normalize(own_first.astype(F32) + branch, gain_rows[1], shift_rows[1])
        own_second = normed.astype(BF)
        full_second = plan.gather_rows(own_second)
        if tiled:
            w_expand, w_shrink = group_three.assemble(
                me, plan.n_col, (others_three, *over_three, *corner_three)
            )
        expanded = dot(full_second, w_expand) + hidden_bias
        activated, slope = gelu_and_slope(expanded)
        branch = plan.scatter_product(activated, w_shrink) + bias_rows[2]
        normed, normal_three, inverse_three = normalize(
            own_second.astype(F32) + branch, gain_rows[2], shift_rows[2]
        )
        output_takes = plan.collect((normed * valid).astype(BF))

        def across(*entries):
            def product(a, b):
                pieces = [
                    outer_sum(left[:, a * size : b * size], right).astype(BF).reshape(b - a, size, -1)
                    for left, size, right in entries
                ]
                whole = pieces[0] if len(pieces) == 1 else jnp.concatenate(pieces, axis=1)
                return whole.reshape(-1, whole.shape[-1])

            return product

        def along(left, right, size):
            return lambda a, b: outer_sum(left, right[:, a * size : b * size]).astype(BF)

        own_cotangent = plan.spread_end(cotangent_takes)
        up_three = own_cotangent.astype(F32) * valid
        resid_three = norm_back(up_three, normal_three, inverse_three, gain_rows[2])
        own_dshrink = resid_three.astype(BF)
        full_dshrink = plan.gather_rows(own_dshrink)
        of_shrink = across((activated, hidden_part, full_dshrink))
        got_shrink = blocks.reduce_start(of_shrink, 1)
        d_expanded = (dot_flip(full_dshrink, w_shrink) * slope.astype(F32)).astype(BF)
        of_expand = along(full_second, d_expanded, hidden_part)
        got_expand = blocks.reduce_start(of_expand, 2)
        up_two = resid_three + plan.scatter_product(d_expanded, w_expand, True)
        resid_two = norm_back(up_two, normal_two, inverse_two, gain_rows[1])
        own_dcross = resid_two.astype(BF)
        full_dcross = plan.gather_rows(own_dcross)
        d_recall = dot_flip(full_dcross, w_cross_out).astype(BF)
        d_cross_q, d_memory = cross_attention_back(
            plan, cross_q, memory, answers, passages, n, cross_logsum, d_recall
        )
        d_cross_q, d_memory, got_shrink, got_expand, output_takes = tie(
            d_cross_q, d_memory, got_shrink, got_expand, output_takes
        )
        terms_shrink = blocks.reduce_next(of_shrink, 1, 0, got_shrink)
        terms_expand = blocks.reduce_next(of_expand, 2, 1, got_expand)
        up_one = resid_two + plan.scatter_product(d_cross_q, w_query, True)
        resid_one = norm_back(up_one, normal_one, inverse_one, gain_rows[0])
        own_dself = resid_one.astype(BF)
        full_dself = plan.gather_rows(own_dself)
        d_mixture = dot_flip(full_dself, w_self_out).astype(BF)
        encoder_grad_takes = plan.collect(plan.scatter_product(d_memory, w_memory, True).astype(BF))
        of_cross = across(
            (d_cross_q, part, full_first),
            (d_memory, 2 * part, full_encoder),
            (recall, part, full_dcross),
            (mixture, part, full_dself),
        )
        got_cross = blocks.reduce_start(of_cross, 1)
        d_mixture, terms_shrink, terms_expand = tie(d_mixture, terms_shrink, terms_expand)
        mine_shrink = blocks.reduce_col(terms_shrink, 1, True)
        mine_expand = blocks.reduce_col(terms_expand, 0, True)
        d_packed = self_attention_back(plan, packed, answers, n, self_logsum, d_mixture)
        d_packed, got_cross, encoder_grad_takes = tie(d_packed, got_cross, encoder_grad_takes)
        middle = full_x.shape[1] // 2
        of_low = along(full_x[:, :middle], d_packed, 3 * part)
        of_high = along(full_x[:, middle:], d_packed, 3 * part)
        got_low, got_high = blocks.reduce_start(of_low, 1), blocks.reduce_start(of_high, 2)
        hidden_takes = plan.collect(
            (resid_one + plan.scatter_product(d_packed, w_self, True)).astype(BF)
        )
        got_low, got_high, got_cross = tie(got_low, got_high, got_cross)
        terms_cross = blocks.reduce_next(of_cross, 1, 0, got_cross)
        g_shrink = blocks.share_parts(mine_shrink)
        g_expand = blocks.share_parts(mine_expand)
        halves = zip(
            blocks.reduce_next(of_low, 1, 1, got_low), blocks.reduce_next(of_high, 2, 1, got_high)
        )
        terms_self = [jnp.concatenate(h, axis=0) for h in halves]
        terms_self, terms_cross = tie(terms_self, terms_cross)
        g_cross = blocks.share_parts(blocks.reduce_col(terms_cross, 1, True))
        g_self = blocks.share_parts(blocks.reduce_col(terms_self, 0, False))
        output, g_encoder, g_hidden = (
            plan.collect_end(t) for t in (output_takes, encoder_grad_takes, hidden_takes)
        )

        def rows_of(values):
            return jnp.sum(values, axis=0, dtype=F32)

        wide = jnp.stack(
            [rows_of(v) for v in (own_dself, own_dcross, own_dshrink)]
            + [rows_of(u * v) for u, v in ((up_one, normal_one), (up_two, normal_two), (up_three, normal_three))]
            + [rows_of(v) for v in (up_one, up_two, up_three)]
        )
        packed_sums = rows_of(d_packed).reshape(n, 3, part)
        memory_sums = rows_of(d_memory).reshape(n, 2, part)
        narrow = jnp.concatenate(
            [
                blocks.unweave(v)
                for v in (
                    packed_sums[:, 0],
                    packed_sums[:, 2],
                    rows_of(d_cross_q).reshape(n, part),
                    memory_sums[:, 1],
                    rows_of(d_expanded).reshape(n, hidden_part),
                )
            ]
        )
        wide = total(wide.reshape(-1), mesh, ("row",))
        small = total(jnp.concatenate([wide, narrow]), mesh, ("dp",))
        wide = small[: wide.shape[0]].reshape(9, -1)
        narrow = total(small[wide.size :], mesh, ("col",))
        wide = sum(
            [wide[:, :width]]
            + [plan.shift(wide[:, k * width : (k + 1) * width], -k) for k in range(1, plan.n_col)]
        )

        def turned(grad, count=1):
            taken = grad.reshape(n, width, count, -1)
            return jnp.transpose(taken, (1, 2, 0, 3)).reshape(width, count, -1).astype(F32)

        def straight(grad):
            return grad.reshape(-1, width).astype(F32)

        def straight_turned(grad, count=1):
            taken = grad.reshape(n, count, -1, width)
            return jnp.transpose(taken, (3, 1, 0, 2)).reshape(width, count, -1).astype(F32)

        return (
            output,
            g_hidden,
            g_encoder,
            turned(g_self, 3),
            straight(g_cross[:, 4 * part :]),
            straight_turned(g_cross[:, :part])[:, 0],
            straight_turned(g_cross[:, part : 3 * part], 2),
            straight(g_cross[:, 3 * part : 4 * part]),
            turned(g_expand)[:, 0],
            straight(g_shrink),
            narrow[: 4 * heads].reshape(4, heads),
            narrow[4 * heads :],
            wide[:3],
            wide[3:6],
            wide[6:],
        )

    return body


def solution(mesh):
    rows = P(("dp", "row"), "col")
    weights = (
        P("col", None, "row"),
        P("row", "col"),
        P("col", "row"),
        P("col", None, "row"),
        P("row", "col"),
        P("col", "row"),
        P("row", "col"),
        P(None, "row"),
        P("row"),
        P(None, "col"),
        P(None, "col"),
        P(None, "col"),
    )
    return jax.shard_map(
        layer(mesh),
        mesh=mesh,
        in_specs=(rows, rows, rows, P("dp"), P("dp")) + weights,
        out_specs=(rows, rows, rows) + weights,
        check_vma=False,
    )
```

```python
import functools
import math

import jax
import jax.numpy as jnp
from jax import lax
from jax.experimental import pallas as pl
from jax.experimental.pallas import tpu as pltpu
from jax.sharding import PartitionSpec as P

HEAD_DIM = 64
SLOT = 1024
BF = jnp.bfloat16
F32 = jnp.float32


def tie(*values):
    return lax.optimization_barrier(values)


def dot(left, right):
    return jnp.dot(left, right, preferred_element_type=F32)


def dot_flip(left, right):
    return lax.dot_general(left, right, (((1,), (1,)), ((), ())), preferred_element_type=F32)


def outer_sum(left, right):
    return lax.dot_general(left, right, (((0,), (0,)), ((), ())), preferred_element_type=F32)

def in_vmem(body, name, scalars, arrays, outs):
    count = len(arrays)

    def kernel(info, *refs):
        body(info, refs[:count], refs[count:])

    def spec(shape):
        return pl.BlockSpec(shape, lambda i, info: (0,) * len(shape))

    def spec_in(array):
        if not isinstance(array, tuple):
            return spec(array.shape)
        whole, at = array
        rest = whole.shape[1:]
        return pl.BlockSpec((None, *rest), lambda i, info: (at,) + (0,) * len(rest))

    return pl.pallas_call(
        kernel,
        out_shape=outs,
        grid_spec=pltpu.PrefetchScalarGridSpec(
            num_scalar_prefetch=1,
            grid=(1,),
            in_specs=[spec_in(a) for a in arrays],
            out_specs=[spec(o.shape) for o in outs],
        ),
        compiler_params=pltpu.CompilerParams(vmem_limit_bytes=56 * 2**20),
        cost_estimate=small_cost(),
        name=name,
    )(scalars, *[a[0] if isinstance(a, tuple) else a for a in arrays])


def lanes_at(start):
    return pl.ds(pl.multiple_of(start, 128), 128)


def join_columns(pieces, places):
    n, rows, width = pieces.shape

    def body(info, ins, outs):
        for i in range(n):
            start = pl.multiple_of(info[i] * width, width)
            outs[0][:, pl.ds(start, width)] = ins[0][i]

    out = jax.ShapeDtypeStruct((rows, width * n), pieces.dtype)
    return in_vmem(body, "join_columns", jnp.stack(places), [pieces], [out])[0]


def cut_columns(values, n_col, col):
    rows, width = values.shape[0], values.shape[1] // n_col

    def body(info, ins, outs):
        for owner in range(n_col):
            start = pl.multiple_of(lax.rem(info[0] - owner + n_col, n_col) * width, width)
            outs[0][owner] = ins[0][:, pl.ds(start, width)]

    out = jax.ShapeDtypeStruct((n_col, rows, width), values.dtype)
    return in_vmem(body, "cut_columns", col[None], [values], [out])[0]


def join_rows(pieces, own):
    seqs, rows, width = pieces[0].shape

    def body(info, ins, outs):
        for i in range(2):
            share = info[0] if i == 0 else 1 - info[0]
            for s in range(seqs):
                start = pl.multiple_of((2 * s + share) * rows, rows)
                outs[0][pl.ds(start, rows), :] = ins[i][s].astype(F32)

    out = jax.ShapeDtypeStruct((2 * seqs * rows, width), F32)
    return in_vmem(body, "join_rows", own[None], list(pieces), [out])[0]


def as_chunk(entries, first, brought):
    return entries, (brought[0], 1 if first == 1 else 0), brought[1]


def sum_chunks(chunks, n_col, col, apart):
    operands, plans = [], []
    total_rows = 0
    for entries, got, last in chunks:
        pieces = []
        for grad, low, high in entries:
            pieces.append((len(operands), low, high))
            operands.append((grad, 0))
        plans.append((pieces, len(operands), len(operands) + 1))
        operands += [got, last]
        total_rows += sum(high - low for _, low, high in entries)
    width = chunks[0][0][0][0].shape[2] // n_col

    def body(info, ins, outs):
        for k in range(n_col):
            if apart:
                start, target = k * width, outs[k]
            else:
                start, target = lax.rem(info[0] - k + n_col, n_col) * width, outs[0].at[k]
            columns = pl.ds(pl.multiple_of(start, width), width)
            row = 0
            for pieces, got, last in plans:
                inner = 0
                for at, low, high in pieces:
                    rows = slice(inner, inner + high - low)
                    terms = [ins[at][low:high, columns], ins[got][rows, columns], ins[last][rows, columns]]
                    target[row : row + high - low, :] = sum(t.astype(F32) for t in terms).astype(BF)
                    row += high - low
                    inner += high - low

    if apart:
        outs = [jax.ShapeDtypeStruct((total_rows, width), BF)] * n_col
    else:
        outs = [jax.ShapeDtypeStruct((n_col, total_rows, width), BF)]
    return in_vmem(body, "sum_chunks", col[None], operands, outs)


def finish(which, parts, layout, size, width):
    n = len(parts)
    operands = [o for part in parts for o, _ in part]
    outs = []
    for groups, turned in layout:
        outs.append(jax.ShapeDtypeStruct((width, groups * n * size) if turned else (n * size, width), F32))

    def body(info, ins, outs):
        used = 0
        for i, part in enumerate(parts):
            refs = ins[used : used + len(part)]
            used += len(part)
            row = 0
            for (groups, turned), target in zip(layout, outs):
                for g in range(groups):
                    at = max(x for x in range(len(part)) if part[x][1] <= row)
                    block = refs[at][row - part[at][1] : row - part[at][1] + size, :].astype(F32)
                    start = pl.multiple_of(info[i] * size, size)
                    if turned:
                        target[:, pl.ds(g * n * size + start, size)] = block.T
                    else:
                        target[pl.ds(start, size), :] = block
                    row += size

    return in_vmem(body, "finish", which, operands, outs)


class Plan:
    def __init__(self, mesh):
        self.n_row = mesh.shape["row"]
        self.n_col = mesh.shape["col"]
        self.share = SLOT // self.n_row
        self.row = lax.axis_index("row")
        self.col = lax.axis_index("col")
        self.pair = self.n_row == 2
        self.offset = self.row * self.share if self.pair else jnp.int32(0)
        self.positions = (jnp.arange(SLOT, dtype=jnp.int32) + self.offset) % SLOT
        self.own_positions = self.row * self.share + jnp.arange(self.share, dtype=jnp.int32)

    def swap(self, values):
        return lax.ppermute(values, "row", [(0, 1), (1, 0)])

    def shift(self, values, k):
        n = self.n_col
        return lax.ppermute(values, "col", [(i, (i + k) % n) for i in range(n)])

    def block(self, other):
        return (self.col - other) % self.n_col

    def reorder(self, blocks):
        return jnp.stack(
            [lax.dynamic_index_in_dim(blocks, self.block(i), 0, keepdims=False) for i in range(self.n_col)]
        )

    def gather_rows(self, values):
        if self.pair:
            return jnp.concatenate([values, self.swap(values)], axis=0)
        return lax.all_gather(values, "row", axis=0, tiled=True)

    def scatter_product(self, left, right, flipped=False):
        times = dot_flip if flipped else dot
        if self.pair:
            away = self.swap(times(left[self.share :], right))
            return times(left[: self.share], right) + away
        return lax.psum_scatter(times(left, right), "row", scatter_dimension=0, tiled=True)

    def sort(self, values):
        width = values.shape[1]
        if self.pair and self.n_col == 4:
            parts = values.reshape(2, 2, self.share, width)
            keep = lax.dynamic_index_in_dim(parts, self.row, 1, keepdims=False)
            take = self.swap(lax.dynamic_index_in_dim(parts, 1 - self.row, 1, keepdims=False))
            ordered = jnp.zeros((4, self.share, width), BF)
            ordered = lax.dynamic_update_slice_in_dim(ordered, keep, 2 * self.row, axis=0)
            ordered = lax.dynamic_update_slice_in_dim(ordered, take, 2 - 2 * self.row, axis=0)
            return ordered
        whole = lax.all_gather(values, "row", axis=0, tiled=True)
        parts = whole.reshape(self.n_col, self.n_row, self.share, width)
        return lax.dynamic_index_in_dim(parts, self.row, 1, keepdims=False)

    def spread(self, ordered):
        return lax.all_to_all(ordered, "col", 0, 0, tiled=True)

    def spread_end(self, takes):
        if self.share % 128 == 0:
            return join_columns(takes, [self.block(i) for i in range(self.n_col)])
        return jnp.transpose(self.reorder(takes), (1, 0, 2)).reshape(self.share, -1)

    def collect(self, values):
        width = values.shape[1] // self.n_col
        if self.share % 128 == 0:
            blocks = cut_columns(values, self.n_col, self.col)
        else:
            blocks = self.reorder(jnp.transpose(values.reshape(self.share, self.n_col, width), (1, 0, 2)))
        return lax.all_to_all(blocks, "col", 0, 0, tiled=True)

    def collect_end(self, moved):
        if self.pair and self.n_col == 4:
            keep = lax.dynamic_slice_in_dim(moved, 2 * self.row, 2, axis=0)
            take = self.swap(lax.dynamic_slice_in_dim(moved, 2 - 2 * self.row, 2, axis=0))
            return join_rows([keep, take], self.row)
        whole = lax.all_gather(moved, "row", axis=1, tiled=True).reshape(-1, moved.shape[2])
        rows = whole.shape[0] // self.n_row
        return lax.dynamic_slice_in_dim(whole, self.row * rows, rows, axis=0).astype(F32)


def normalize(residual, gain_row, shift_row):
    center = jnp.mean(residual, axis=-1, keepdims=True)
    moved = residual - center
    inverse = lax.rsqrt(jnp.mean(moved * moved, axis=-1, keepdims=True) + 1e-05)
    normal = moved * inverse
    return normal * gain_row + shift_row, normal, inverse


def norm_back(upstream, normal, inverse, gain_row):
    scaled = upstream * gain_row
    plain = jnp.mean(scaled, axis=-1, keepdims=True)
    cross = jnp.mean(scaled * normal, axis=-1, keepdims=True)
    return inverse * (scaled - plain - normal * cross)


def gelu_and_slope(values):
    cdf = 0.5 + 0.5 * lax.erf(values * math.sqrt(0.5))
    density = jnp.exp(-0.5 * values * values) * (1.0 / math.sqrt(2.0 * math.pi))
    return (values * cdf).astype(BF), (cdf + values * density).astype(BF)


LANES = 2 * HEAD_DIM
SPAN = 256
NEVER = -1000000000.0


def dot_last(left, right):
    return lax.dot_general(left, right, (((1,), (1,)), ((), ())), preferred_element_type=F32)


def place_of(start, offset):
    return pl.multiple_of(lax.rem(start + offset, SLOT), SPAN)


def heads_apart(rows):
    low = lax.broadcasted_iota(jnp.int32, rows.shape, 1) < HEAD_DIM
    none = jnp.zeros_like(rows)
    return jnp.where(low, rows, none), jnp.where(low, none, rows)


def key_spans(count):
    if count == 1:
        return [(0, SPAN)]
    return [(0, (count - 1) * SPAN), ((count - 1) * SPAN, count * SPAN)]


def score_spans(keys_ref, query, count, limit):
    parts = []
    for start, stop in key_spans(count):
        scores = dot_last(keys_ref[start:stop, :], query)
        if stop == count * SPAN:
            places = lax.broadcasted_iota(jnp.int32, scores.shape, 0)
            if limit is None:
                allowed = places <= lax.broadcasted_iota(jnp.int32, scores.shape, 1)
            else:
                allowed = places < limit - start
            scores = jnp.where(allowed, scores, NEVER)
        parts.append(scores)
    return parts


def for_each_block(causal, query_length, key_length, run, skip):
    blocks = SLOT // SPAN
    if causal:
        for i in range(blocks):
            pl.when(i * SPAN < query_length)(functools.partial(run, i * SPAN, i + 1))
            pl.when(i * SPAN >= query_length)(functools.partial(skip, i * SPAN))
        return
    live = lax.div(query_length + (SPAN - 1), SPAN)
    spans = lax.div(key_length + (SPAN - 1), SPAN)
    for count in range(1, blocks + 1):

        @pl.when(spans == count)
        def _(count=count):
            @pl.loop(0, live)
            def _(i):
                run(pl.multiple_of(i * SPAN, SPAN), count)

    @pl.loop(live, blocks)
    def _(i):
        skip(pl.multiple_of(i * SPAN, SPAN))


def forward_kernel(causal, info, query_ref, key_ref, value_ref, out_ref, logsum_ref, keys, values_t):
    offset, query_length, key_length = info[0], info[1], info[2]
    half = SLOT // 2
    for start in (0, half):
        stored = place_of(start, offset)
        keys[start : start + half, :] = key_ref[pl.ds(stored, half), :]
        values_t[:, start : start + half] = value_ref[pl.ds(stored, half), :].T

    def run(start, count):
        stored = place_of(start, offset)
        scaled = query_ref[pl.ds(stored, SPAN), :] * (1.0 / math.sqrt(HEAD_DIM))
        outs = []
        for head, query in enumerate(heads_apart(scaled)):
            parts = score_spans(keys, query, count, None if causal else key_length)
            highest = functools.reduce(jnp.maximum, [jnp.max(s, axis=0, keepdims=True) for s in parts])
            raised = [jnp.exp(s - highest) for s in parts]
            below = sum(jnp.sum(e, axis=0, keepdims=True) for e in raised)
            mixed = sum(
                jnp.dot(
                    values_t[head * HEAD_DIM : (head + 1) * HEAD_DIM, a:b],
                    e.astype(BF),
                    preferred_element_type=F32,
                )
                for (a, b), e in zip(key_spans(count), raised)
            )
            outs.append(mixed * (1.0 / below))
            logsum_ref[0, head : head + 1, pl.ds(start, SPAN)] = highest + jnp.log(below)
        out_ref[pl.ds(stored, SPAN), :] = jnp.concatenate(outs, axis=0).T.astype(BF)

    def skip(start):
        out_ref[pl.ds(place_of(start, offset), SPAN), :] = jnp.zeros((SPAN, LANES), BF)

    for_each_block(causal, query_length, key_length, run, skip)


def backward_kernel(
    causal, info, query_ref, key_ref, value_ref, up_ref, logsum_ref, *refs
):
    if causal:
        packed_ref, keys, keys_t, values, key_sum, value_sum = refs
        query_out, other_out = packed_ref, packed_ref
        base = LANES
    else:
        query_out, other_out, keys, keys_t, values, key_sum, value_sum = refs
        base = 0
    offset, query_length, key_length = info[0], info[1], info[2]
    half = SLOT // 2
    for start in (0, half):
        stored = place_of(start, offset)
        block = key_ref[pl.ds(stored, half), :]
        keys[start : start + half, :] = block
        keys_t[:, start : start + half] = block.T
        values[start : start + half, :] = value_ref[pl.ds(stored, half), :]
    key_sum[...] = jnp.zeros_like(key_sum)
    value_sum[...] = jnp.zeros_like(value_sum)
    factor = 1.0 / math.sqrt(HEAD_DIM)

    def run(start, count):
        stored = place_of(start, offset)
        queries = heads_apart(query_ref[pl.ds(stored, SPAN), :] * factor)
        ups = heads_apart(up_ref[pl.ds(stored, SPAN), :])
        spans = key_spans(count)
        weights, grads, outs = [], [], []
        for head in range(2):
            logsum = logsum_ref[0, head : head + 1, pl.ds(start, SPAN)]
            parts = score_spans(keys, queries[head], count, None if causal else key_length)
            parts = [jnp.exp(s - logsum) for s in parts]
            pulls = [dot_last(values[a:b, :], ups[head]) for a, b in spans]
            inner = sum(jnp.sum(p * g, axis=0, keepdims=True) for p, g in zip(parts, pulls))
            pulls = [(p * (g - inner)).astype(BF) for p, g in zip(parts, pulls)]
            outs.append(
                sum(
                    jnp.dot(
                        keys_t[head * HEAD_DIM : (head + 1) * HEAD_DIM, a:b],
                        g,
                        preferred_element_type=F32,
                    )
                    for (a, b), g in zip(spans, pulls)
                )
            )
            weights.append([p.astype(BF) for p in parts])
            grads.append(pulls)
        query_out[pl.ds(stored, SPAN), 0:LANES] = (
            jnp.concatenate(outs, axis=0) * factor
        ).T.astype(BF)
        for at, (a, b) in enumerate(spans):
            for head in range(2):
                value_sum[a:b, :] += jnp.dot(weights[head][at], ups[head], preferred_element_type=F32)
                key_sum[a:b, :] += jnp.dot(grads[head][at], queries[head], preferred_element_type=F32)

    def skip(start):
        query_out[pl.ds(place_of(start, offset), SPAN), 0:LANES] = jnp.zeros((SPAN, LANES), BF)

    for_each_block(causal, query_length, key_length, run, skip)
    for start in (0, half):
        stored = place_of(start, offset)
        other_out[pl.ds(stored, half), base : base + LANES] = key_sum[start : start + half, :].astype(BF)
        other_out[pl.ds(stored, half), base + LANES : base + 2 * LANES] = value_sum[
            start : start + half, :
        ].astype(BF)


def column_block(width, of):
    return pl.BlockSpec((SLOT, width), lambda i, info: (0, of(i)))


LOGSUM_BLOCK = pl.BlockSpec((1, 2, SLOT), lambda i, info: (i, 0, 0))


def attention_cost():
    return pl.CostEstimate(flops=2 * 10**10, bytes_accessed=2**20, transcendentals=0)


def small_cost():
    return pl.CostEstimate(flops=0, bytes_accessed=2**16, transcendentals=0)


def attend(causal, info, query, keys, pairs):
    step = 3 if causal else 2
    first = 1 if causal else 0
    return pl.pallas_call(
        functools.partial(forward_kernel, causal),
        out_shape=(
            jax.ShapeDtypeStruct((SLOT, pairs * LANES), BF),
            jax.ShapeDtypeStruct((pairs, 2, SLOT), F32),
        ),
        grid_spec=pltpu.PrefetchScalarGridSpec(
            num_scalar_prefetch=1,
            grid=(pairs,),
            in_specs=[
                column_block(LANES, (lambda i: 3 * i) if causal else (lambda i: i)),
                column_block(LANES, lambda i: step * i + first),
                column_block(LANES, lambda i: step * i + first + 1),
            ],
            out_specs=(column_block(LANES, lambda i: i), LOGSUM_BLOCK),
            scratch_shapes=[pltpu.VMEM((SLOT, LANES), BF), pltpu.VMEM((LANES, SLOT), BF)],
        ),
        compiler_params=pltpu.CompilerParams(vmem_limit_bytes=48 * 2**20),
        cost_estimate=attention_cost(),
        name="attend",
    )(info, query, keys, keys)


def attend_back(causal, info, query, keys, logsum, upstream, pairs):
    step = 3 if causal else 2
    first = 1 if causal else 0
    if causal:
        out_shape = jax.ShapeDtypeStruct((SLOT, pairs * 3 * LANES), BF)
        out_specs = column_block(3 * LANES, lambda i: i)
    else:
        out_shape = (
            jax.ShapeDtypeStruct((SLOT, pairs * LANES), BF),
            jax.ShapeDtypeStruct((SLOT, pairs * 2 * LANES), BF),
        )
        out_specs = (column_block(LANES, lambda i: i), column_block(2 * LANES, lambda i: i))
    return pl.pallas_call(
        functools.partial(backward_kernel, causal),
        out_shape=out_shape,
        grid_spec=pltpu.PrefetchScalarGridSpec(
            num_scalar_prefetch=1,
            grid=(pairs,),
            in_specs=[
                column_block(LANES, (lambda i: 3 * i) if causal else (lambda i: i)),
                column_block(LANES, lambda i: step * i + first),
                column_block(LANES, lambda i: step * i + first + 1),
                column_block(LANES, lambda i: i),
                LOGSUM_BLOCK,
            ],
            out_specs=out_specs,
            scratch_shapes=[
                pltpu.VMEM((SLOT, LANES), BF),
                pltpu.VMEM((LANES, SLOT), BF),
                pltpu.VMEM((SLOT, LANES), BF),
                pltpu.VMEM((SLOT, LANES), F32),
                pltpu.VMEM((SLOT, LANES), F32),
            ],
        ),
        compiler_params=pltpu.CompilerParams(vmem_limit_bytes=48 * 2**20),
        cost_estimate=attention_cost() if causal else small_cost(),
        name="attend_back",
    )(info, query, keys, keys, upstream, logsum)


def build_mask(positions, length, causal):
    allowed = jnp.broadcast_to(positions[None, :] < length, (SLOT, SLOT))
    if causal:
        allowed = allowed & (positions[None, :] <= positions[:, None])
    return allowed


def score_block(query, key, allowed):
    factor = 1.0 / math.sqrt(HEAD_DIM)
    scores = jnp.einsum("qhd,khd->hqk", query, key, preferred_element_type=F32) * factor
    return jnp.where(allowed[None], scores, -1000000000.0)


def split_heads(values):
    return values.reshape(SLOT, -1, HEAD_DIM)


def attention_forward(query, key, value, allowed):
    query, key, value = (split_heads(v) for v in (query, key, value))
    scores = score_block(query, key, allowed)
    highest = jnp.max(scores, axis=-1, keepdims=True)
    raised = jnp.exp(scores - highest)
    denominator = jnp.sum(raised, axis=-1, keepdims=True)
    weights = (raised / denominator).astype(BF)
    mixture = jnp.einsum("hqk,khd->qhd", weights, value, preferred_element_type=F32)
    return mixture.reshape(SLOT, -1).astype(BF), highest + jnp.log(denominator)


def attention_backward(query, key, value, allowed, logsum, upstream):
    query, key, value, upstream = (split_heads(v) for v in (query, key, value, upstream))
    factor = 1.0 / math.sqrt(HEAD_DIM)
    weights = jnp.exp(score_block(query, key, allowed) - logsum)
    value_grad = jnp.einsum("hqk,qhd->khd", weights.astype(BF), upstream, preferred_element_type=F32)
    weight_grad = jnp.einsum("qhd,khd->hqk", upstream, value, preferred_element_type=F32)
    inner = jnp.sum(weights * weight_grad, axis=-1, keepdims=True)
    score_grad = (weights * (weight_grad - inner)).astype(BF)
    query_grad = jnp.einsum("hqk,khd->qhd", score_grad, key, preferred_element_type=F32) * factor
    key_grad = jnp.einsum("hqk,qhd->khd", score_grad, query, preferred_element_type=F32) * factor
    return tuple(g.reshape(SLOT, -1).astype(BF) for g in (query_grad, key_grad, value_grad))


def interleave(arrays, n):
    rows = arrays[0].shape[0]
    return jnp.stack([a.reshape(rows, n, -1) for a in arrays], axis=2).reshape(rows, -1)


def apart(array, n, count):
    rows = array.shape[0]
    parts = array.reshape(rows, n, count, -1)
    return [parts[:, :, i].reshape(rows, -1) for i in range(count)]


def self_attention(plan, packed, length, n):
    if packed.shape[1] == 3 * n * LANES:
        info = jnp.stack([plan.offset, length, length])
        return attend(True, info, packed, packed, n)
    mask = build_mask(plan.positions, length, True)
    return attention_forward(*apart(packed, n, 3), mask)


def self_attention_back(plan, packed, length, n, logsum, upstream):
    if packed.shape[1] == 3 * n * LANES:
        info = jnp.stack([plan.offset, length, length])
        return attend_back(True, info, packed, packed, logsum, upstream, n)
    mask = build_mask(plan.positions, length, True)
    return interleave(attention_backward(*apart(packed, n, 3), mask, logsum, upstream), n)


def cross_attention(plan, query, memory, query_length, key_length, n):
    if query.shape[1] == n * LANES:
        info = jnp.stack([plan.offset, query_length, key_length])
        return attend(False, info, query, memory, n)
    mask = build_mask(plan.positions, key_length, False)
    return attention_forward(query, *apart(memory, n, 2), mask)


def cross_attention_back(plan, query, memory, query_length, key_length, n, logsum, upstream):
    if query.shape[1] == n * LANES:
        info = jnp.stack([plan.offset, query_length, key_length])
        return attend_back(False, info, query, memory, logsum, upstream, n)
    mask = build_mask(plan.positions, key_length, False)
    first, *rest = attention_backward(query, *apart(memory, n, 2), mask, logsum, upstream)
    return first, interleave(rest, n)


ORDER = (0, 2, 3, 1)


class Group:
    def __init__(self, weights, n):
        self.weights = weights
        self.n = n
        self.plans = []
        row = 0
        for axis, groups, local in weights:
            if axis == 0:
                tall, count = local.shape[0], local.shape[1] // n // 128
            else:
                tall, count = local.shape[0] // n, local.shape[1] // 128
            self.plans.append((row, tall, count))
            row += tall * count
        self.rows = row

    def fits(self):
        return all(
            (local.shape[1] % (groups * self.n * 128) == 0 if axis == 0 else local.shape[0] % (self.n * 128) == 0)
            for axis, groups, local in self.weights
        )

    def local_block(self, ref, at, which, block):
        axis, groups, local = self.weights[at]
        _, tall, count = self.plans[at]
        if axis == 0:
            per = count // groups
            i, b = divmod(block, per)
            return ref[:, lanes_at((i * self.n * per + b) * 128 + which * (per * 128))]
        return ref[pl.ds(pl.multiple_of(which * tall, tall), tall), block * 128 : (block + 1) * 128]

    def pack(self, me):
        def body(info, ins, outs):
            for at, (row, tall, count) in enumerate(self.plans):
                for block in range(count):
                    start = row + block * tall
                    outs[0][start : start + tall, :] = self.local_block(ins[at], at, info[0], block)

        out = jax.ShapeDtypeStruct((self.rows, 128), BF)
        return in_vmem(body, "pack", me[None], [w[2] for w in self.weights], [out])[0]

    def assemble(self, me, n_col, moved):
        half = self.rows * (n_col - 1) // 2
        count_w = len(self.weights)
        outs = []
        for axis, groups, local in self.weights:
            shape = (local.shape[0] * n_col, local.shape[1]) if axis == 0 else (local.shape[0], local.shape[1] * n_col)
            outs.append(jax.ShapeDtypeStruct(shape, BF))

        def body(info, ins, outs):
            local_refs, moved_refs = ins[:count_w], ins[count_w:]
            for at, (row, tall, count) in enumerate(self.plans):
                axis = self.weights[at][0]
                width = self.weights[at][2].shape[1]
                for place, j in enumerate(ORDER):
                    for k in range(n_col):
                        for block in range(count):
                            if k == 0:
                                value = self.local_block(local_refs[at], at, info[j], block)
                            else:
                                start = (k - 1) * self.rows + row + block * tall
                                ref = moved_refs[j]
                                if j == 3 and start >= half:
                                    ref, start = moved_refs[4], start - half
                                value = ref[start : start + tall, :]
                            if axis == 0:
                                column = (place * count + block) * 128
                                outs[at][k * tall : (k + 1) * tall, column : column + 128] = value
                            else:
                                column = k * width + block * 128
                                outs[at][place * tall : (place + 1) * tall, column : column + 128] = value

        which = jnp.stack([me ^ j for j in range(self.n)])
        return in_vmem(body, "assemble", which, [w[2] for w in self.weights] + list(moved), outs)


def split_float(values):
    high = lax.reduce_precision(values, 8, 7)
    middle = lax.reduce_precision(values - high, 8, 7)
    low = values - high - middle
    parts = jnp.concatenate([high, middle, low], axis=0).astype(BF)
    parts = jnp.concatenate([parts[:, i : i + 128] for i in range(0, parts.shape[1], 128)], axis=0)
    return jnp.pad(parts, ((0, -parts.shape[0] % 16), (0, 0)))


def join_float(rows, shape):
    n, width = shape
    count = width // 128
    parts = rows[:, : 3 * n * count].reshape(rows.shape[0], count, 3, n, 128).astype(F32)
    whole = parts[:, :, 0] + (parts[:, :, 1] + parts[:, :, 2])
    return jnp.moveaxis(whole, 1, 2).reshape(rows.shape[0], n, width)


def pick_others(every, rows, n_col, col):
    width = every.shape[2]
    return pl.pallas_call(
        lambda info, source, target: target.__setitem__(Ellipsis, source[...]),
        out_shape=jax.ShapeDtypeStruct(((n_col - 1) * rows, width), every.dtype),
        grid_spec=pltpu.PrefetchScalarGridSpec(
            num_scalar_prefetch=1,
            grid=(n_col - 1,),
            in_specs=[
                pl.BlockSpec(
                    (None, rows, width), lambda k, info: (lax.rem(info[0] - k - 1 + n_col, n_col), 0, 0)
                )
            ],
            out_specs=pl.BlockSpec((rows, width), lambda k, info: (k, 0)),
        ),
        cost_estimate=small_cost(),
        name="pick_others",
    )(col[None], every)


class Blocks:
    def __init__(self, mesh, plan):
        self.n = mesh.shape["dp"]
        assert self.n == len(ORDER)
        self.plan = plan
        self.me = lax.axis_index("dp")

    def hop(self, values, step):
        return lax.ppermute(values, "dp", [(i, i ^ step) for i in range(self.n)])

    def own(self, values, axis, j=0, wait=0):
        shape = values.shape
        parts = values.reshape(shape[:axis] + (self.n, shape[axis] // self.n) + shape[axis + 1 :])
        return lax.dynamic_index_in_dim(parts, (self.me ^ j) + wait, axis, keepdims=False)

    def weave(self, values):
        return jnp.stack([self.own(values, values.ndim - 1, j) for j in ORDER], axis=-2)

    def unweave(self, values):
        order = jnp.array([ORDER.index(j) for j in range(self.n)])
        return jnp.concatenate(
            [
                lax.dynamic_index_in_dim(values, order[self.me ^ q], 0, keepdims=False)
                for q in range(self.n)
            ]
        )

    def others_by_shift(self, piece):
        return jnp.concatenate([self.plan.shift(piece, k) for k in range(1, self.plan.n_col)], axis=0)

    def others_by_gather(self, piece, extra):
        rows = piece.shape[0]
        if extra is not None:
            piece = jnp.concatenate([piece, extra], axis=0)
        every = lax.all_gather(piece, "col", axis=0)
        return pick_others(every, rows, self.plan.n_col, self.plan.col), every[:, rows:]

    def hops(self, others):
        return self.hop(others, 1), self.hop(others, 2)

    def corner(self, over):
        half = over[0].shape[0] // 2
        return self.hop(over[1][:half], 1), self.hop(over[0][half:], 2)

    def whole(self, weight):
        axis, groups, local = weight
        every = self.plan.reorder(lax.all_gather(local, "col", axis=0))
        if axis == 0:
            every = every.reshape(-1, groups, local.shape[1] // groups)
            return jnp.stack([self.weave(every[:, i]) for i in range(groups)], axis=2).reshape(every.shape[0], -1)
        every = jnp.moveaxis(every, 0, 1).reshape(local.shape[0], -1)
        parts = every.reshape(self.n, -1, every.shape[1])
        picked = [lax.dynamic_index_in_dim(parts, self.me ^ j, 0, keepdims=False) for j in ORDER]
        return jnp.concatenate(picked, axis=0)

    def product(self, hidden, model):
        grad = outer_sum(hidden, model).astype(BF)
        return grad.reshape(self.n, -1, grad.shape[1])

    def reduce_start(self, entries, first):
        return self.hop(self.reduce_send(entries, first), first)

    def reduce_send(self, entries, first):
        a, b = (2, 4) if first == 1 else (1, 3)
        sends = [grad[a:b, low:high] for grad, low, high in entries]
        return sends[0] if len(sends) == 1 else jnp.concatenate(sends, axis=1)

    def reduce_next(self, entries, first, got):
        to_middle, to_base = (0, 1) if first == 1 else (1, 0)
        place = 1 if first == 1 else 3
        keeps = [grad[place, low:high] for grad, low, high in entries]
        middle = keeps[0] if len(keeps) == 1 else jnp.concatenate(keeps, axis=0)
        return got, self.hop(middle + got[to_middle], 3 - first)

    def plain(self, hidden, model, groups, turned):
        plan = self.plan
        grad = outer_sum(hidden, model).astype(BF)
        parts = grad.reshape(self.n, groups, -1, grad.shape[1])
        natural = [
            lax.dynamic_index_in_dim(parts, jnp.array([ORDER.index(j) for j in range(self.n)])[self.me ^ q], 0)
            for q in range(self.n)
        ]
        grad = jnp.moveaxis(jnp.concatenate(natural, axis=0), 1, 0).reshape(grad.shape[0], plan.n_col, -1)
        grad = lax.psum(plan.reorder(jnp.moveaxis(grad, 1, 0)), "dp")
        grad = lax.psum_scatter(grad, "col", scatter_dimension=0, tiled=False).astype(F32)
        return grad.T if turned else grad


def total(values, mesh, axes):
    for axis in axes:
        size = mesh.shape[axis]
        step = 1
        while step < size:
            values = values + lax.ppermute(values, axis, [(i, i ^ step) for i in range(size)])
            step *= 2
    return values


def layer(mesh):
    def body(
        hidden,
        encoder,
        cotangent,
        answer_length,
        passage_length,
        self_input,
        self_output,
        cross_query,
        cross_memory,
        cross_output,
        expand_weight,
        shrink_weight,
        head_bias,
        expand_bias,
        model_bias,
        norm_gain,
        norm_shift,
    ):
        plan = Plan(mesh)
        blocks = Blocks(mesh, plan)
        n = blocks.n
        me = blocks.me
        width = model_bias.shape[1]
        heads = self_output.shape[0]
        part = heads // n
        hidden_part = expand_bias.shape[0] // n
        answers = lax.dynamic_index_in_dim(answer_length, plan.col, keepdims=False)
        passages = lax.dynamic_index_in_dim(passage_length, plan.col, keepdims=False)
        valid = (plan.own_positions < answers).astype(F32)[:, None]

        own_norms = jnp.concatenate([model_bias, norm_gain, norm_shift])
        group_one = Group([(0, 3, self_input.reshape(width, -1)), (1, 1, self_output)], n)
        group_two = Group(
            [(0, 1, cross_query), (0, 2, cross_memory.reshape(width, -1)), (1, 1, cross_output)], n
        )
        group_three = Group([(0, 1, expand_weight), (1, 1, shrink_weight)], n)
        tiled = group_one.fits() and group_two.fits() and group_three.fits()
        if tiled:
            others_one = blocks.others_by_shift(group_one.pack(me))
            over_one = blocks.hops(others_one)
            corner_one = blocks.corner(over_one)
            w_self, w_self_out = group_one.assemble(me, plan.n_col, (others_one, *over_one, *corner_one))
        else:
            w_self, w_self_out = (blocks.whole(w) for w in group_one.weights)
            w_query, w_memory, w_cross_out = (blocks.whole(w) for w in group_two.weights)
            w_expand, w_shrink = (blocks.whole(w) for w in group_three.weights)
        x_takes = plan.spread(plan.sort(hidden))
        encoder, cotangent = plan.sort(encoder), plan.sort(cotangent)

        if tiled:
            pieces = [group_two.pack(me), group_three.pack(me)]
            others_one, pieces, carried = tie(others_one, pieces, split_float(own_norms))
            others_two, extra = blocks.others_by_gather(pieces[0], carried)
            others_three, _ = blocks.others_by_gather(pieces[1], None)
            norms = plan.reorder(join_float(extra, own_norms.shape))
        if not tiled:
            norms = plan.reorder(lax.all_gather(own_norms, "col", axis=0))
        norms = jnp.moveaxis(norms, 0, 1).reshape(own_norms.shape[0], -1)
        bias_rows, gain_rows, shift_rows = norms[:3], norms[3:6], norms[6:]

        head_parts = blocks.weave(head_bias)
        none = jnp.zeros((n, part), F32)
        self_bias = jnp.stack([head_parts[0], none, head_parts[1]], axis=1).reshape(-1)
        query_bias = head_parts[2].reshape(-1)
        memory_bias = jnp.stack([none, head_parts[3]], axis=1).reshape(-1)
        hidden_bias = blocks.weave(expand_bias).reshape(-1)

        own_x = plan.spread_end(x_takes)
        full_x = plan.gather_rows(own_x)
        packed = (dot(full_x, w_self) + self_bias).astype(BF)
        if tiled:
            packed, others_two, encoder, cotangent = tie(packed, others_two, encoder, cotangent)
            over_two = blocks.hops(others_two)
        encoder_takes = plan.spread(encoder)
        mixture, self_logsum = self_attention(plan, packed, answers, n)
        if tiled:
            mixture, over_two, others_three = tie(mixture, over_two, others_three)
            corner_two = blocks.corner(over_two)
            over_three = blocks.hops(others_three)
        branch = plan.scatter_product(mixture, w_self_out) + bias_rows[0]
        normed, normal_one, inverse_one = normalize(own_x.astype(F32) + branch, gain_rows[0], shift_rows[0])
        own_first = normed.astype(BF)
        if tiled:
            own_first, corner_two, over_three, encoder_takes, cotangent = tie(
                own_first, corner_two, over_three, encoder_takes, cotangent
            )
            corner_three = blocks.corner(over_three)
        own_encoder = plan.spread_end(encoder_takes)
        full_encoder = plan.gather_rows(own_encoder)
        full_first = plan.gather_rows(own_first)
        if tiled:
            w_query, w_memory, w_cross_out = group_two.assemble(
                me, plan.n_col, (others_two, *over_two, *corner_two)
            )
        memory = (dot(full_encoder, w_memory) + memory_bias).astype(BF)
        cross_q = (dot(full_first, w_query) + query_bias).astype(BF)
        cotangent_takes = plan.spread(cotangent)
        if tiled:
            cross_q, memory = tie(cross_q, memory)
        recall, cross_logsum = cross_attention(plan, cross_q, memory, answers, passages, n)
        if tiled:
            recall, corner_three, cotangent_takes = tie(recall, corner_three, cotangent_takes)
        branch = plan.scatter_product(recall, w_cross_out) + bias_rows[1]
        normed, normal_two, inverse_two = normalize(own_first.astype(F32) + branch, gain_rows[1], shift_rows[1])
        own_second = normed.astype(BF)
        full_second = plan.gather_rows(own_second)
        if tiled:
            w_expand, w_shrink = group_three.assemble(
                me, plan.n_col, (others_three, *over_three, *corner_three)
            )
        expanded = dot(full_second, w_expand) + hidden_bias
        activated, slope = gelu_and_slope(expanded)
        branch = plan.scatter_product(activated, w_shrink) + bias_rows[2]
        normed, normal_three, inverse_three = normalize(
            own_second.astype(F32) + branch, gain_rows[2], shift_rows[2]
        )
        output_takes = plan.collect((normed * valid).astype(BF))

        own_cotangent = plan.spread_end(cotangent_takes)
        up_three = own_cotangent.astype(F32) * valid
        resid_three = norm_back(up_three, normal_three, inverse_three, gain_rows[2])
        own_dshrink = resid_three.astype(BF)
        full_dshrink = plan.gather_rows(own_dshrink)
        if tiled:
            of_shrink = [(blocks.product(activated, full_dshrink), 0, hidden_part)]
            got_shrink = blocks.reduce_start(of_shrink, 1)
        d_expanded = (dot_flip(full_dshrink, w_shrink) * slope.astype(F32)).astype(BF)
        (d_expanded,) = tie(d_expanded)
        if tiled:
            of_expand = [(blocks.product(d_expanded, full_second), 0, hidden_part)]
            got_expand = blocks.reduce_start(of_expand, 2)
        up_two = resid_three + plan.scatter_product(d_expanded, w_expand, True)
        resid_two = norm_back(up_two, normal_two, inverse_two, gain_rows[1])
        own_dcross = resid_two.astype(BF)
        full_dcross = plan.gather_rows(own_dcross)
        d_recall = dot_flip(full_dcross, w_cross_out).astype(BF)
        d_cross_q, d_memory = cross_attention_back(
            plan, cross_q, memory, answers, passages, n, cross_logsum, d_recall
        )
        if tiled:
            d_cross_q, d_memory, got_shrink, got_expand, output_takes = tie(
                d_cross_q, d_memory, got_shrink, got_expand, output_takes
            )
            chunk_shrink = blocks.reduce_next(of_shrink, 1, got_shrink)
            chunk_expand = blocks.reduce_next(of_expand, 2, got_expand)
            of_cross_a = [
                (blocks.product(d_cross_q, full_first), 0, part),
                (blocks.product(recall, full_dcross), 0, part),
            ]
            of_cross_b = [(blocks.product(d_memory, full_encoder), 0, 2 * part)]
            got_cross_a = blocks.reduce_start(of_cross_a, 1)
            got_cross_b = blocks.reduce_start(of_cross_b, 2)
        up_one = resid_two + plan.scatter_product(d_cross_q, w_query, True)
        resid_one = norm_back(up_one, normal_one, inverse_one, gain_rows[0])
        own_dself = resid_one.astype(BF)
        full_dself = plan.gather_rows(own_dself)
        d_mixture = dot_flip(full_dself, w_self_out).astype(BF)
        encoder_grad_takes = plan.collect(plan.scatter_product(d_memory, w_memory, True).astype(BF))
        if tiled:
            (sums,) = sum_chunks(
                [as_chunk(of_shrink, 1, chunk_shrink), as_chunk(of_expand, 2, chunk_expand)],
                plan.n_col,
                plan.col,
                False,
            )
            grad_self_out = blocks.product(mixture, full_dself)
            d_mixture, sums, got_cross_a, got_cross_b, grad_self_out = tie(
                d_mixture, sums, got_cross_a, got_cross_b, grad_self_out
            )
            mine_hidden = lax.psum_scatter(sums, "col", scatter_dimension=0, tiled=False)
            chunk_cross_a = blocks.reduce_next(of_cross_a, 1, got_cross_a)
            chunk_cross_b = blocks.reduce_next(of_cross_b, 2, got_cross_b)
        d_packed = self_attention_back(plan, packed, answers, n, self_logsum, d_mixture)
        if tiled:
            d_packed, chunk_cross_a, chunk_cross_b, mine_hidden, encoder_grad_takes = tie(
                d_packed, chunk_cross_a, chunk_cross_b, mine_hidden, encoder_grad_takes
            )
            grad_self = blocks.product(d_packed, full_x)
            of_low = [(grad_self, 0, 2 * part)]
            of_high = [(grad_self, 2 * part, 3 * part), (grad_self_out, 0, part)]
            send_low, send_high = blocks.reduce_send(of_low, 1), blocks.reduce_send(of_high, 2)
            send_low, send_high, d_packed, chunk_cross_a, chunk_cross_b = tie(
                send_low, send_high, d_packed, chunk_cross_a, chunk_cross_b
            )
            got_low, got_high = blocks.hop(send_low, 1), blocks.hop(send_high, 2)
            (sums,) = sum_chunks(
                [as_chunk(of_cross_a, 1, chunk_cross_a), as_chunk(of_cross_b, 2, chunk_cross_b)],
                plan.n_col,
                plan.col,
                False,
            )
            mine_cross = lax.psum_scatter(sums, "col", scatter_dimension=0, tiled=False)

        def rows_of(values):
            return jnp.sum(values, axis=0, dtype=F32)

        wide = jnp.stack(
            [rows_of(v) for v in (own_dself, own_dcross, own_dshrink)]
            + [rows_of(u * v) for u, v in ((up_one, normal_one), (up_two, normal_two), (up_three, normal_three))]
            + [rows_of(v) for v in (up_one, up_two, up_three)]
        )
        packed_sums = rows_of(d_packed).reshape(n, 3, part)
        memory_sums = rows_of(d_memory).reshape(n, 2, part)
        narrow = jnp.concatenate(
            [
                blocks.unweave(v)
                for v in (
                    packed_sums[:, 0],
                    packed_sums[:, 2],
                    rows_of(d_cross_q).reshape(n, part),
                    memory_sums[:, 1],
                    rows_of(d_expanded).reshape(n, hidden_part),
                )
            ]
        )
        wide = total(wide, mesh, ("row",))
        wide = plan.reorder(jnp.moveaxis(wide.reshape(9, plan.n_col, width), 1, 0))
        small = jnp.concatenate([wide.reshape(-1), narrow])

        hidden_grad = (resid_one + plan.scatter_product(d_packed, w_self, True)).astype(BF)
        if tiled:
            small = small + blocks.hop(small, 1)
        hidden_takes = plan.collect(hidden_grad)
        if not tiled:
            small = total(small, mesh, ("dp", "col"))
        if tiled:
            output, g_encoder = plan.collect_end(output_takes), plan.collect_end(encoder_grad_takes)
            got_low, got_high, small, output, g_encoder = tie(got_low, got_high, small, output, g_encoder)
            chunk_low = blocks.reduce_next(of_low, 1, got_low)
            chunk_high = blocks.reduce_next(of_high, 2, got_high)
            small = small + blocks.hop(small, 2)
            ready = lax.all_gather(mine_hidden, "dp", axis=0)
            g_shrink, g_expand = finish(
                jnp.arange(n), [[((ready, q), 0)] for q in range(n)], [(1, False), (1, True)], hidden_part, width
            )
            g_hidden = plan.collect_end(hidden_takes)
            chunk_low, chunk_high, mine_cross, g_shrink, g_expand = tie(
                chunk_low, chunk_high, mine_cross, g_shrink, g_expand
            )
            own, *rest = sum_chunks(
                [as_chunk(of_low, 1, chunk_low), as_chunk(of_high, 2, chunk_high)],
                plan.n_col,
                plan.col,
                True,
            )
            arrived = [own] + [plan.shift(r, -1 - k) for k, r in enumerate(rest)]
            small = small + lax.ppermute(small, "col", [(i, i ^ 1) for i in range(plan.n_col)])
            arrived, g_hidden = tie(arrived, g_hidden)
            mine_self = sum(r.astype(F32) for r in arrived).astype(BF)
            over_self = blocks.hops(mine_self)
            small = small + lax.ppermute(small, "col", [(i, i ^ 2) for i in range(plan.n_col)])
            ready = lax.all_gather(mine_cross, "dp", axis=0)
            g_query, g_cross_out, g_memory = finish(
                jnp.arange(n),
                [[((ready, q), 0)] for q in range(n)],
                [(1, True), (1, False), (2, True)],
                part,
                width,
            )
            over_self, g_query, g_cross_out, g_memory = tie(over_self, g_query, g_cross_out, g_memory)
            corner_self = blocks.corner(over_self)
            g_self, g_self_out = finish(
                jnp.stack([me ^ j for j in range(n)]),
                [
                    [(mine_self, 0)],
                    [(over_self[0], 0)],
                    [(over_self[1], 0)],
                    [(corner_self[0], 0), (corner_self[1], 2 * part)],
                ],
                [(3, True), (1, False)],
                part,
                width,
            )
        else:
            g_shrink = blocks.plain(activated, full_dshrink, 1, False)
            g_expand = blocks.plain(d_expanded, full_second, 1, True)
            g_query = blocks.plain(d_cross_q, full_first, 1, True)
            g_memory = blocks.plain(d_memory, full_encoder, 2, True)
            g_cross_out = blocks.plain(recall, full_dcross, 1, False)
            g_self = blocks.plain(d_packed, full_x, 3, True)
            g_self_out = blocks.plain(mixture, full_dself, 1, False)
            output, g_encoder, g_hidden = (
                plan.collect_end(t) for t in (output_takes, encoder_grad_takes, hidden_takes)
            )

        own_wide = lax.dynamic_index_in_dim(
            small[: 9 * plan.n_col * width].reshape(plan.n_col, 9, width), plan.col, keepdims=False
        )
        narrow = small[9 * plan.n_col * width :]
        return (
            output,
            g_hidden,
            g_encoder,
            g_self.reshape(self_input.shape),
            g_self_out,
            g_query,
            g_memory.reshape(cross_memory.shape),
            g_cross_out,
            g_expand,
            g_shrink,
            narrow[: 4 * heads].reshape(4, heads),
            narrow[4 * heads :],
            own_wide[:3],
            own_wide[3:6],
            own_wide[6:],
        )

    return body


def solution(mesh):
    rows = P(("dp", "row"), "col")
    weights = (
        P("col", None, "row"),
        P("row", "col"),
        P("col", "row"),
        P("col", None, "row"),
        P("row", "col"),
        P("col", "row"),
        P("row", "col"),
        P(None, "row"),
        P("row"),
        P(None, "col"),
        P(None, "col"),
        P(None, "col"),
    )
    return jax.shard_map(
        layer(mesh),
        mesh=mesh,
        in_specs=(rows, rows, rows, P("dp"), P("dp")) + weights,
        out_specs=(rows, rows, rows) + weights,
        check_vma=False,
    )
```

```python
import functools
import math

import jax
import jax.numpy as jnp
from jax import lax
from jax.experimental import pallas as pl
from jax.experimental.pallas import tpu as pltpu
from jax.sharding import PartitionSpec as P

HEAD_DIM = 64
SLOT = 1024
BF = jnp.bfloat16
F32 = jnp.float32


def tie(*values):
    return lax.optimization_barrier(values)


def dot(left, right):
    return jnp.dot(left, right, preferred_element_type=F32)


def dot_flip(left, right):
    return lax.dot_general(left, right, (((1,), (1,)), ((), ())), preferred_element_type=F32)


def outer_sum(left, right):
    return lax.dot_general(left, right, (((0,), (0,)), ((), ())), preferred_element_type=F32)

def in_vmem(body, name, scalars, arrays, outs):
    count = len(arrays)

    def kernel(info, *refs):
        body(info, refs[:count], refs[count:])

    def spec(shape):
        return pl.BlockSpec(shape, lambda i, info: (0,) * len(shape))

    def spec_in(array):
        if not isinstance(array, tuple):
            return spec(array.shape)
        whole, at = array
        rest = whole.shape[1:]
        return pl.BlockSpec((None, *rest), lambda i, info: (at,) + (0,) * len(rest))

    return pl.pallas_call(
        kernel,
        out_shape=outs,
        grid_spec=pltpu.PrefetchScalarGridSpec(
            num_scalar_prefetch=1,
            grid=(1,),
            in_specs=[spec_in(a) for a in arrays],
            out_specs=[spec(o.shape) for o in outs],
        ),
        compiler_params=pltpu.CompilerParams(vmem_limit_bytes=56 * 2**20),
        cost_estimate=small_cost(),
        name=name,
    )(scalars, *[a[0] if isinstance(a, tuple) else a for a in arrays])


def lanes_at(start):
    return pl.ds(pl.multiple_of(start, 128), 128)


def join_columns(pieces, places):
    n, rows, width = pieces.shape

    def body(info, ins, outs):
        for i in range(n):
            start = pl.multiple_of(info[i] * width, width)
            outs[0][:, pl.ds(start, width)] = ins[0][i]

    out = jax.ShapeDtypeStruct((rows, width * n), pieces.dtype)
    return in_vmem(body, "join_columns", jnp.stack(places), [pieces], [out])[0]


def cut_columns(values, n_col, col):
    rows, width = values.shape[0], values.shape[1] // n_col

    def body(info, ins, outs):
        for owner in range(n_col):
            start = pl.multiple_of(lax.rem(info[0] - owner + n_col, n_col) * width, width)
            outs[0][owner] = ins[0][:, pl.ds(start, width)]

    out = jax.ShapeDtypeStruct((n_col, rows, width), values.dtype)
    return in_vmem(body, "cut_columns", col[None], [values], [out])[0]


def join_rows(pieces, own):
    seqs, rows, width = pieces[0].shape

    def body(info, ins, outs):
        for i in range(2):
            share = info[0] if i == 0 else 1 - info[0]
            for s in range(seqs):
                start = pl.multiple_of((2 * s + share) * rows, rows)
                outs[0][pl.ds(start, rows), :] = ins[i][s].astype(F32)

    out = jax.ShapeDtypeStruct((2 * seqs * rows, width), F32)
    return in_vmem(body, "join_rows", own[None], list(pieces), [out])[0]


def as_chunk(entries, first, brought):
    return entries, (brought[0], 1 if first == 1 else 0), brought[1]


def sum_chunks(chunks, n_col, col, apart):
    operands, plans = [], []
    total_rows = 0
    for entries, got, last in chunks:
        pieces = []
        for grad, low, high in entries:
            pieces.append((len(operands), low, high))
            operands.append((grad, 0))
        plans.append((pieces, len(operands), len(operands) + 1))
        operands += [got, last]
        total_rows += sum(high - low for _, low, high in entries)
    width = chunks[0][0][0][0].shape[2] // n_col

    def body(info, ins, outs):
        for k in range(n_col):
            if apart:
                start, target = k * width, outs[k]
            else:
                start, target = lax.rem(info[0] - k + n_col, n_col) * width, outs[0].at[k]
            columns = pl.ds(pl.multiple_of(start, width), width)
            row = 0
            for pieces, got, last in plans:
                inner = 0
                for at, low, high in pieces:
                    rows = slice(inner, inner + high - low)
                    terms = [ins[at][low:high, columns], ins[got][rows, columns], ins[last][rows, columns]]
                    target[row : row + high - low, :] = sum(t.astype(F32) for t in terms).astype(BF)
                    row += high - low
                    inner += high - low

    if apart:
        outs = [jax.ShapeDtypeStruct((total_rows, width), BF)] * n_col
    else:
        outs = [jax.ShapeDtypeStruct((n_col, total_rows, width), BF)]
    return in_vmem(body, "sum_chunks", col[None], operands, outs)


def finish(which, parts, layout, size, width):
    n = len(parts)
    operands = [o for part in parts for o, _ in part]
    outs = []
    for groups, turned in layout:
        shape = (width, groups, n * size) if groups > 1 else (width, n * size)
        outs.append(jax.ShapeDtypeStruct(shape if turned else (n * size, width), F32))

    def body(info, ins, outs):
        used = 0
        for i, part in enumerate(parts):
            refs = ins[used : used + len(part)]
            used += len(part)
            row = 0
            for (groups, turned), target in zip(layout, outs):
                for g in range(groups):
                    at = max(x for x in range(len(part)) if part[x][1] <= row)
                    block = refs[at][row - part[at][1] : row - part[at][1] + size, :].astype(F32)
                    start = pl.multiple_of(info[i] * size, size)
                    if turned and groups > 1:
                        target[:, g, pl.ds(start, size)] = block.T
                    elif turned:
                        target[:, pl.ds(start, size)] = block.T
                    else:
                        target[pl.ds(start, size), :] = block
                    row += size

    return in_vmem(body, "finish", which, operands, outs)


class Plan:
    def __init__(self, mesh):
        self.n_row = mesh.shape["row"]
        self.n_col = mesh.shape["col"]
        self.share = SLOT // self.n_row
        self.row = lax.axis_index("row")
        self.col = lax.axis_index("col")
        self.pair = self.n_row == 2
        self.offset = self.row * self.share if self.pair else jnp.int32(0)
        self.positions = (jnp.arange(SLOT, dtype=jnp.int32) + self.offset) % SLOT
        self.own_positions = self.row * self.share + jnp.arange(self.share, dtype=jnp.int32)

    def swap(self, values):
        return lax.ppermute(values, "row", [(0, 1), (1, 0)])

    def shift(self, values, k):
        n = self.n_col
        return lax.ppermute(values, "col", [(i, (i + k) % n) for i in range(n)])

    def block(self, other):
        return (self.col - other) % self.n_col

    def reorder(self, blocks):
        return jnp.stack(
            [lax.dynamic_index_in_dim(blocks, self.block(i), 0, keepdims=False) for i in range(self.n_col)]
        )

    def gather_rows(self, values):
        if self.pair:
            return jnp.concatenate([values, self.swap(values)], axis=0)
        return lax.all_gather(values, "row", axis=0, tiled=True)

    def scatter_product(self, left, right, flipped=False):
        times = dot_flip if flipped else dot
        if self.pair:
            away = self.swap(times(left[self.share :], right))
            return times(left[: self.share], right) + away
        return lax.psum_scatter(times(left, right), "row", scatter_dimension=0, tiled=True)

    def sort(self, values):
        width = values.shape[1]
        if self.pair and self.n_col == 4:
            parts = values.reshape(2, 2, self.share, width)
            keep = lax.dynamic_index_in_dim(parts, self.row, 1, keepdims=False)
            take = self.swap(lax.dynamic_index_in_dim(parts, 1 - self.row, 1, keepdims=False))
            ordered = jnp.zeros((4, self.share, width), BF)
            ordered = lax.dynamic_update_slice_in_dim(ordered, keep, 2 * self.row, axis=0)
            ordered = lax.dynamic_update_slice_in_dim(ordered, take, 2 - 2 * self.row, axis=0)
            return ordered
        whole = lax.all_gather(values, "row", axis=0, tiled=True)
        parts = whole.reshape(self.n_col, self.n_row, self.share, width)
        return lax.dynamic_index_in_dim(parts, self.row, 1, keepdims=False)

    def spread(self, ordered):
        return lax.all_to_all(ordered, "col", 0, 0, tiled=True)

    def spread_end(self, takes):
        if self.share % 128 == 0:
            return join_columns(takes, [self.block(i) for i in range(self.n_col)])
        return jnp.transpose(self.reorder(takes), (1, 0, 2)).reshape(self.share, -1)

    def collect(self, values):
        return self.deal(self.cut(values))

    def cut(self, values):
        width = values.shape[1] // self.n_col
        if self.share % 128 == 0:
            return cut_columns(values, self.n_col, self.col)
        return self.reorder(jnp.transpose(values.reshape(self.share, self.n_col, width), (1, 0, 2)))

    def deal(self, blocks):
        return lax.all_to_all(blocks, "col", 0, 0, tiled=True)

    def collect_end(self, moved):
        if self.pair and self.n_col == 4:
            keep = lax.dynamic_slice_in_dim(moved, 2 * self.row, 2, axis=0)
            take = self.swap(lax.dynamic_slice_in_dim(moved, 2 - 2 * self.row, 2, axis=0))
            return join_rows([keep, take], self.row)
        whole = lax.all_gather(moved, "row", axis=1, tiled=True).reshape(-1, moved.shape[2])
        rows = whole.shape[0] // self.n_row
        return lax.dynamic_slice_in_dim(whole, self.row * rows, rows, axis=0).astype(F32)


def normalize(residual, gain_row, shift_row):
    center = jnp.mean(residual, axis=-1, keepdims=True)
    moved = residual - center
    inverse = lax.rsqrt(jnp.mean(moved * moved, axis=-1, keepdims=True) + 1e-05)
    normal = moved * inverse
    return normal * gain_row + shift_row, normal, inverse


def norm_back(upstream, normal, inverse, gain_row):
    scaled = upstream * gain_row
    plain = jnp.mean(scaled, axis=-1, keepdims=True)
    cross = jnp.mean(scaled * normal, axis=-1, keepdims=True)
    return inverse * (scaled - plain - normal * cross)


def gelu_and_slope(values):
    cdf = 0.5 + 0.5 * lax.erf(values * math.sqrt(0.5))
    density = jnp.exp(-0.5 * values * values) * (1.0 / math.sqrt(2.0 * math.pi))
    return (values * cdf).astype(BF), (cdf + values * density).astype(BF)


LANES = 2 * HEAD_DIM
SPAN = 256
NEVER = -1000000000.0


def dot_last(left, right):
    return lax.dot_general(left, right, (((1,), (1,)), ((), ())), preferred_element_type=F32)


def place_of(start, offset):
    return pl.multiple_of(lax.rem(start + offset, SLOT), SPAN)


def heads_apart(rows):
    low = lax.broadcasted_iota(jnp.int32, rows.shape, 1) < HEAD_DIM
    none = jnp.zeros_like(rows)
    return jnp.where(low, rows, none), jnp.where(low, none, rows)


def key_spans(count):
    if count == 1:
        return [(0, SPAN)]
    return [(0, (count - 1) * SPAN), ((count - 1) * SPAN, count * SPAN)]


def score_spans(keys_ref, query, count, limit):
    parts = []
    for start, stop in key_spans(count):
        scores = dot_last(keys_ref[start:stop, :], query)
        if stop == count * SPAN:
            places = lax.broadcasted_iota(jnp.int32, scores.shape, 0)
            if limit is None:
                allowed = places <= lax.broadcasted_iota(jnp.int32, scores.shape, 1)
            else:
                allowed = places < limit - start
            scores = jnp.where(allowed, scores, NEVER)
        parts.append(scores)
    return parts


def for_each_block(causal, query_length, key_length, run, skip):
    blocks = SLOT // SPAN
    if causal:
        for i in range(blocks):
            pl.when(i * SPAN < query_length)(functools.partial(run, i * SPAN, i + 1))
            pl.when(i * SPAN >= query_length)(functools.partial(skip, i * SPAN))
        return
    live = lax.div(query_length + (SPAN - 1), SPAN)
    spans = lax.div(key_length + (SPAN - 1), SPAN)
    for count in range(1, blocks + 1):

        @pl.when(spans == count)
        def _(count=count):
            @pl.loop(0, live)
            def _(i):
                run(pl.multiple_of(i * SPAN, SPAN), count)

    @pl.loop(live, blocks)
    def _(i):
        skip(pl.multiple_of(i * SPAN, SPAN))


def forward_kernel(causal, info, query_ref, key_ref, value_ref, out_ref, logsum_ref, keys, values_t):
    offset, query_length, key_length = info[0], info[1], info[2]
    half = SLOT // 2
    for start in (0, half):
        stored = place_of(start, offset)
        keys[start : start + half, :] = key_ref[pl.ds(stored, half), :]
        values_t[:, start : start + half] = value_ref[pl.ds(stored, half), :].T

    def run(start, count):
        stored = place_of(start, offset)
        scaled = query_ref[pl.ds(stored, SPAN), :] * (1.0 / math.sqrt(HEAD_DIM))
        outs = []
        for head, query in enumerate(heads_apart(scaled)):
            parts = score_spans(keys, query, count, None if causal else key_length)
            highest = functools.reduce(jnp.maximum, [jnp.max(s, axis=0, keepdims=True) for s in parts])
            raised = [jnp.exp(s - highest) for s in parts]
            below = sum(jnp.sum(e, axis=0, keepdims=True) for e in raised)
            mixed = sum(
                jnp.dot(
                    values_t[head * HEAD_DIM : (head + 1) * HEAD_DIM, a:b],
                    e.astype(BF),
                    preferred_element_type=F32,
                )
                for (a, b), e in zip(key_spans(count), raised)
            )
            outs.append(mixed * (1.0 / below))
            logsum_ref[0, head : head + 1, pl.ds(start, SPAN)] = highest + jnp.log(below)
        out_ref[pl.ds(stored, SPAN), :] = jnp.concatenate(outs, axis=0).T.astype(BF)

    def skip(start):
        out_ref[pl.ds(place_of(start, offset), SPAN), :] = jnp.zeros((SPAN, LANES), BF)

    for_each_block(causal, query_length, key_length, run, skip)


def backward_kernel(
    causal, info, query_ref, key_ref, value_ref, up_ref, logsum_ref, *refs
):
    if causal:
        packed_ref, keys, keys_t, values, key_sum, value_sum = refs
        query_out, other_out = packed_ref, packed_ref
        base = LANES
    else:
        query_out, other_out, keys, keys_t, values, key_sum, value_sum = refs
        base = 0
    offset, query_length, key_length = info[0], info[1], info[2]
    half = SLOT // 2
    for start in (0, half):
        stored = place_of(start, offset)
        block = key_ref[pl.ds(stored, half), :]
        keys[start : start + half, :] = block
        keys_t[:, start : start + half] = block.T
        values[start : start + half, :] = value_ref[pl.ds(stored, half), :]
    key_sum[...] = jnp.zeros_like(key_sum)
    value_sum[...] = jnp.zeros_like(value_sum)
    factor = 1.0 / math.sqrt(HEAD_DIM)

    def run(start, count):
        stored = place_of(start, offset)
        queries = heads_apart(query_ref[pl.ds(stored, SPAN), :] * factor)
        ups = heads_apart(up_ref[pl.ds(stored, SPAN), :])
        spans = key_spans(count)
        weights, grads, outs = [], [], []
        for head in range(2):
            logsum = logsum_ref[0, head : head + 1, pl.ds(start, SPAN)]
            parts = score_spans(keys, queries[head], count, None if causal else key_length)
            parts = [jnp.exp(s - logsum) for s in parts]
            pulls = [dot_last(values[a:b, :], ups[head]) for a, b in spans]
            inner = sum(jnp.sum(p * g, axis=0, keepdims=True) for p, g in zip(parts, pulls))
            pulls = [(p * (g - inner)).astype(BF) for p, g in zip(parts, pulls)]
            outs.append(
                sum(
                    jnp.dot(
                        keys_t[head * HEAD_DIM : (head + 1) * HEAD_DIM, a:b],
                        g,
                        preferred_element_type=F32,
                    )
                    for (a, b), g in zip(spans, pulls)
                )
            )
            weights.append([p.astype(BF) for p in parts])
            grads.append(pulls)
        query_out[pl.ds(stored, SPAN), 0:LANES] = (
            jnp.concatenate(outs, axis=0) * factor
        ).T.astype(BF)
        for at, (a, b) in enumerate(spans):
            for head in range(2):
                value_sum[a:b, :] += jnp.dot(weights[head][at], ups[head], preferred_element_type=F32)
                key_sum[a:b, :] += jnp.dot(grads[head][at], queries[head], preferred_element_type=F32)

    def skip(start):
        query_out[pl.ds(place_of(start, offset), SPAN), 0:LANES] = jnp.zeros((SPAN, LANES), BF)

    for_each_block(causal, query_length, key_length, run, skip)
    for start in (0, half):
        stored = place_of(start, offset)
        other_out[pl.ds(stored, half), base : base + LANES] = key_sum[start : start + half, :].astype(BF)
        other_out[pl.ds(stored, half), base + LANES : base + 2 * LANES] = value_sum[
            start : start + half, :
        ].astype(BF)


def column_block(width, of):
    return pl.BlockSpec((SLOT, width), lambda i, info: (0, of(i)))


LOGSUM_BLOCK = pl.BlockSpec((1, 2, SLOT), lambda i, info: (i, 0, 0))


def attention_cost():
    return pl.CostEstimate(flops=2 * 10**10, bytes_accessed=2**20, transcendentals=0)


def small_cost():
    return pl.CostEstimate(flops=0, bytes_accessed=2**16, transcendentals=0)


def attend(causal, info, query, keys, pairs):
    step = 3 if causal else 2
    first = 1 if causal else 0
    return pl.pallas_call(
        functools.partial(forward_kernel, causal),
        out_shape=(
            jax.ShapeDtypeStruct((SLOT, pairs * LANES), BF),
            jax.ShapeDtypeStruct((pairs, 2, SLOT), F32),
        ),
        grid_spec=pltpu.PrefetchScalarGridSpec(
            num_scalar_prefetch=1,
            grid=(pairs,),
            in_specs=[
                column_block(LANES, (lambda i: 3 * i) if causal else (lambda i: i)),
                column_block(LANES, lambda i: step * i + first),
                column_block(LANES, lambda i: step * i + first + 1),
            ],
            out_specs=(column_block(LANES, lambda i: i), LOGSUM_BLOCK),
            scratch_shapes=[pltpu.VMEM((SLOT, LANES), BF), pltpu.VMEM((LANES, SLOT), BF)],
        ),
        compiler_params=pltpu.CompilerParams(vmem_limit_bytes=48 * 2**20),
        cost_estimate=attention_cost(),
        name="attend",
    )(info, query, keys, keys)


def attend_back(causal, info, query, keys, logsum, upstream, pairs):
    step = 3 if causal else 2
    first = 1 if causal else 0
    if causal:
        out_shape = jax.ShapeDtypeStruct((SLOT, pairs * 3 * LANES), BF)
        out_specs = column_block(3 * LANES, lambda i: i)
    else:
        out_shape = (
            jax.ShapeDtypeStruct((SLOT, pairs * LANES), BF),
            jax.ShapeDtypeStruct((SLOT, pairs * 2 * LANES), BF),
        )
        out_specs = (column_block(LANES, lambda i: i), column_block(2 * LANES, lambda i: i))
    return pl.pallas_call(
        functools.partial(backward_kernel, causal),
        out_shape=out_shape,
        grid_spec=pltpu.PrefetchScalarGridSpec(
            num_scalar_prefetch=1,
            grid=(pairs,),
            in_specs=[
                column_block(LANES, (lambda i: 3 * i) if causal else (lambda i: i)),
                column_block(LANES, lambda i: step * i + first),
                column_block(LANES, lambda i: step * i + first + 1),
                column_block(LANES, lambda i: i),
                LOGSUM_BLOCK,
            ],
            out_specs=out_specs,
            scratch_shapes=[
                pltpu.VMEM((SLOT, LANES), BF),
                pltpu.VMEM((LANES, SLOT), BF),
                pltpu.VMEM((SLOT, LANES), BF),
                pltpu.VMEM((SLOT, LANES), F32),
                pltpu.VMEM((SLOT, LANES), F32),
            ],
        ),
        compiler_params=pltpu.CompilerParams(vmem_limit_bytes=48 * 2**20),
        cost_estimate=attention_cost() if causal else small_cost(),
        name="attend_back",
    )(info, query, keys, keys, upstream, logsum)


def build_mask(positions, length, causal):
    allowed = jnp.broadcast_to(positions[None, :] < length, (SLOT, SLOT))
    if causal:
        allowed = allowed & (positions[None, :] <= positions[:, None])
    return allowed


def score_block(query, key, allowed):
    factor = 1.0 / math.sqrt(HEAD_DIM)
    scores = jnp.einsum("qhd,khd->hqk", query, key, preferred_element_type=F32) * factor
    return jnp.where(allowed[None], scores, -1000000000.0)


def split_heads(values):
    return values.reshape(SLOT, -1, HEAD_DIM)


def attention_forward(query, key, value, allowed):
    query, key, value = (split_heads(v) for v in (query, key, value))
    scores = score_block(query, key, allowed)
    highest = jnp.max(scores, axis=-1, keepdims=True)
    raised = jnp.exp(scores - highest)
    denominator = jnp.sum(raised, axis=-1, keepdims=True)
    weights = (raised / denominator).astype(BF)
    mixture = jnp.einsum("hqk,khd->qhd", weights, value, preferred_element_type=F32)
    return mixture.reshape(SLOT, -1).astype(BF), highest + jnp.log(denominator)


def attention_backward(query, key, value, allowed, logsum, upstream):
    query, key, value, upstream = (split_heads(v) for v in (query, key, value, upstream))
    factor = 1.0 / math.sqrt(HEAD_DIM)
    weights = jnp.exp(score_block(query, key, allowed) - logsum)
    value_grad = jnp.einsum("hqk,qhd->khd", weights.astype(BF), upstream, preferred_element_type=F32)
    weight_grad = jnp.einsum("qhd,khd->hqk", upstream, value, preferred_element_type=F32)
    inner = jnp.sum(weights * weight_grad, axis=-1, keepdims=True)
    score_grad = (weights * (weight_grad - inner)).astype(BF)
    query_grad = jnp.einsum("hqk,khd->qhd", score_grad, key, preferred_element_type=F32) * factor
    key_grad = jnp.einsum("hqk,qhd->khd", score_grad, query, preferred_element_type=F32) * factor
    return tuple(g.reshape(SLOT, -1).astype(BF) for g in (query_grad, key_grad, value_grad))


def interleave(arrays, n):
    rows = arrays[0].shape[0]
    return jnp.stack([a.reshape(rows, n, -1) for a in arrays], axis=2).reshape(rows, -1)


def apart(array, n, count):
    rows = array.shape[0]
    parts = array.reshape(rows, n, count, -1)
    return [parts[:, :, i].reshape(rows, -1) for i in range(count)]


def self_attention(plan, packed, length, n):
    if packed.shape[1] == 3 * n * LANES:
        info = jnp.stack([plan.offset, length, length])
        return attend(True, info, packed, packed, n)
    mask = build_mask(plan.positions, length, True)
    return attention_forward(*apart(packed, n, 3), mask)


def self_attention_back(plan, packed, length, n, logsum, upstream):
    if packed.shape[1] == 3 * n * LANES:
        info = jnp.stack([plan.offset, length, length])
        return attend_back(True, info, packed, packed, logsum, upstream, n)
    mask = build_mask(plan.positions, length, True)
    return interleave(attention_backward(*apart(packed, n, 3), mask, logsum, upstream), n)


def cross_attention(plan, query, memory, query_length, key_length, n):
    if query.shape[1] == n * LANES:
        info = jnp.stack([plan.offset, query_length, key_length])
        return attend(False, info, query, memory, n)
    mask = build_mask(plan.positions, key_length, False)
    return attention_forward(query, *apart(memory, n, 2), mask)


def cross_attention_back(plan, query, memory, query_length, key_length, n, logsum, upstream):
    if query.shape[1] == n * LANES:
        info = jnp.stack([plan.offset, query_length, key_length])
        return attend_back(False, info, query, memory, logsum, upstream, n)
    mask = build_mask(plan.positions, key_length, False)
    first, *rest = attention_backward(query, *apart(memory, n, 2), mask, logsum, upstream)
    return first, interleave(rest, n)


ORDER = (0, 2, 3, 1)


class Group:
    def __init__(self, weights, n):
        self.weights = weights
        self.n = n
        self.plans = []
        row = 0
        for axis, groups, local in weights:
            if axis == 0:
                tall, count = local.shape[0], local.shape[1] // n // 128
            else:
                tall, count = local.shape[0] // n, local.shape[1] // 128
            self.plans.append((row, tall, count))
            row += tall * count
        self.rows = row

    def fits(self):
        return all(
            (local.shape[1] % (groups * self.n * 128) == 0 if axis == 0 else local.shape[0] % (self.n * 128) == 0)
            for axis, groups, local in self.weights
        )

    def local_block(self, ref, at, which, block):
        axis, groups, local = self.weights[at]
        _, tall, count = self.plans[at]
        if axis == 0:
            per = count // groups
            i, b = divmod(block, per)
            return ref[:, lanes_at((i * self.n * per + b) * 128 + which * (per * 128))]
        return ref[pl.ds(pl.multiple_of(which * tall, tall), tall), block * 128 : (block + 1) * 128]

    def pack(self, me):
        def body(info, ins, outs):
            for at, (row, tall, count) in enumerate(self.plans):
                for block in range(count):
                    start = row + block * tall
                    outs[0][start : start + tall, :] = self.local_block(ins[at], at, info[0], block)

        out = jax.ShapeDtypeStruct((self.rows, 128), BF)
        return in_vmem(body, "pack", me[None], [w[2] for w in self.weights], [out])[0]

    def outputs(self, n_col):
        outs = []
        for axis, groups, local in self.weights:
            shape = (local.shape[0] * n_col, local.shape[1]) if axis == 0 else (local.shape[0], local.shape[1] * n_col)
            outs.append(jax.ShapeDtypeStruct(shape, BF))
        return outs

    def fill(self, info, n_col, local_refs, moved_refs, outs):
        half = self.rows * (n_col - 1) // 2
        for at, (row, tall, count) in enumerate(self.plans):
            axis = self.weights[at][0]
            width = self.weights[at][2].shape[1]
            for place, j in enumerate(ORDER):
                for k in range(n_col):
                    for block in range(count):
                        if k == 0:
                            value = self.local_block(local_refs[at], at, info[j], block)
                        else:
                            start = (k - 1) * self.rows + row + block * tall
                            ref = moved_refs[j]
                            if j == 3 and start >= half:
                                ref, start = moved_refs[4], start - half
                            value = ref[start : start + tall, :]
                        if axis == 0:
                            column = (place * count + block) * 128
                            outs[at][k * tall : (k + 1) * tall, column : column + 128] = value
                        else:
                            column = k * width + block * 128
                            outs[at][place * tall : (place + 1) * tall, column : column + 128] = value


def assemble(me, n_col, *groups):
    operands, outs = [], []
    for group, moved in groups:
        operands += [w[2] for w in group.weights] + list(moved)
        outs += group.outputs(n_col)

    def body(info, ins, outs):
        for group, moved in groups:
            count = len(group.weights)
            group.fill(info, n_col, ins[:count], ins[count : count + len(moved)], outs[:count])
            ins, outs = ins[count + len(moved) :], outs[count:]

    which = jnp.stack([me ^ j for j in range(len(ORDER))])
    return in_vmem(body, "assemble", which, operands, outs)


def split_float(values):
    high = lax.reduce_precision(values, 8, 7)
    middle = lax.reduce_precision(values - high, 8, 7)
    low = values - high - middle
    parts = jnp.concatenate([high, middle, low], axis=0).astype(BF)
    parts = jnp.concatenate([parts[:, i : i + 128] for i in range(0, parts.shape[1], 128)], axis=0)
    return jnp.pad(parts, ((0, -parts.shape[0] % 16), (0, 0)))


def join_float(rows, shape):
    n, width = shape
    count = width // 128
    parts = rows[:, : 3 * n * count].reshape(rows.shape[0], count, 3, n, 128).astype(F32)
    whole = parts[:, :, 0] + (parts[:, :, 1] + parts[:, :, 2])
    return jnp.moveaxis(whole, 1, 2).reshape(rows.shape[0], n, width)


def pick_others(every, at, rows, n_col, col):
    width = every.shape[2]
    return pl.pallas_call(
        lambda info, source, target: target.__setitem__(Ellipsis, source[...]),
        out_shape=jax.ShapeDtypeStruct(((n_col - 1) * rows, width), every.dtype),
        grid_spec=pltpu.PrefetchScalarGridSpec(
            num_scalar_prefetch=1,
            grid=(n_col - 1,),
            in_specs=[
                pl.BlockSpec(
                    (None, rows, width), lambda k, info: (lax.rem(info[0] - k - 1 + n_col, n_col), at, 0)
                )
            ],
            out_specs=pl.BlockSpec((rows, width), lambda k, info: (k, 0)),
        ),
        cost_estimate=small_cost(),
        name="pick_others",
    )(col[None], every)


class Blocks:
    def __init__(self, mesh, plan):
        self.n = mesh.shape["dp"]
        assert self.n == len(ORDER)
        self.plan = plan
        self.me = lax.axis_index("dp")

    def hop(self, values, step):
        return lax.ppermute(values, "dp", [(i, i ^ step) for i in range(self.n)])

    def own(self, values, axis, j=0, wait=0):
        shape = values.shape
        parts = values.reshape(shape[:axis] + (self.n, shape[axis] // self.n) + shape[axis + 1 :])
        return lax.dynamic_index_in_dim(parts, (self.me ^ j) + wait, axis, keepdims=False)

    def weave(self, values):
        return jnp.stack([self.own(values, values.ndim - 1, j) for j in ORDER], axis=-2)

    def unweave(self, values):
        order = jnp.array([ORDER.index(j) for j in range(self.n)])
        return jnp.concatenate(
            [
                lax.dynamic_index_in_dim(values, order[self.me ^ q], 0, keepdims=False)
                for q in range(self.n)
            ]
        )

    def others_by_shift(self, piece):
        return jnp.concatenate([self.plan.shift(piece, k) for k in range(1, self.plan.n_col)], axis=0)

    def others_by_gather(self, piece, count, extra):
        total_rows = piece.shape[0]
        if extra is not None:
            piece = jnp.concatenate([piece, extra], axis=0)
        every = lax.all_gather(piece, "col", axis=0)
        rows = total_rows // count
        picked = [pick_others(every, i, rows, self.plan.n_col, self.plan.col) for i in range(count)]
        return picked, every[:, total_rows:]

    def hops(self, others):
        return self.hop(others, 1), self.hop(others, 2)

    def corner(self, over):
        half = over[0].shape[0] // 2
        return self.hop(over[1][:half], 1), self.hop(over[0][half:], 2)

    def whole(self, weight):
        axis, groups, local = weight
        every = self.plan.reorder(lax.all_gather(local, "col", axis=0))
        if axis == 0:
            every = every.reshape(-1, groups, local.shape[1] // groups)
            return jnp.stack([self.weave(every[:, i]) for i in range(groups)], axis=2).reshape(every.shape[0], -1)
        every = jnp.moveaxis(every, 0, 1).reshape(local.shape[0], -1)
        parts = every.reshape(self.n, -1, every.shape[1])
        picked = [lax.dynamic_index_in_dim(parts, self.me ^ j, 0, keepdims=False) for j in ORDER]
        return jnp.concatenate(picked, axis=0)

    def product(self, hidden, model):
        grad = outer_sum(hidden, model).astype(BF)
        return grad.reshape(self.n, -1, grad.shape[1])

    def reduce_start(self, entries, first):
        return self.hop(self.reduce_send(entries, first), first)

    def reduce_send(self, entries, first):
        a, b = (2, 4) if first == 1 else (1, 3)
        sends = [grad[a:b, low:high] for grad, low, high in entries]
        return sends[0] if len(sends) == 1 else jnp.concatenate(sends, axis=1)

    def reduce_next(self, entries, first, got):
        to_middle, to_base = (0, 1) if first == 1 else (1, 0)
        place = 1 if first == 1 else 3
        keeps = [grad[place, low:high] for grad, low, high in entries]
        middle = keeps[0] if len(keeps) == 1 else jnp.concatenate(keeps, axis=0)
        return got, self.hop(middle + got[to_middle], 3 - first)

    def plain(self, hidden, model, groups, turned):
        plan = self.plan
        grad = outer_sum(hidden, model).astype(BF)
        parts = grad.reshape(self.n, groups, -1, grad.shape[1])
        natural = [
            lax.dynamic_index_in_dim(parts, jnp.array([ORDER.index(j) for j in range(self.n)])[self.me ^ q], 0)
            for q in range(self.n)
        ]
        grad = jnp.moveaxis(jnp.concatenate(natural, axis=0), 1, 0).reshape(grad.shape[0], plan.n_col, -1)
        grad = lax.psum(plan.reorder(jnp.moveaxis(grad, 1, 0)), "dp")
        grad = lax.psum_scatter(grad, "col", scatter_dimension=0, tiled=False).astype(F32)
        return grad.T if turned else grad


def total(values, mesh, axes):
    for axis in axes:
        size = mesh.shape[axis]
        step = 1
        while step < size:
            values = values + lax.ppermute(values, axis, [(i, i ^ step) for i in range(size)])
            step *= 2
    return values


def layer(mesh):
    def body(
        hidden,
        encoder,
        cotangent,
        answer_length,
        passage_length,
        self_input,
        self_output,
        cross_query,
        cross_memory,
        cross_output,
        expand_weight,
        shrink_weight,
        head_bias,
        expand_bias,
        model_bias,
        norm_gain,
        norm_shift,
    ):
        plan = Plan(mesh)
        blocks = Blocks(mesh, plan)
        n = blocks.n
        me = blocks.me
        width = model_bias.shape[1]
        heads = self_output.shape[0]
        part = heads // n
        hidden_part = expand_bias.shape[0] // n
        answers = lax.dynamic_index_in_dim(answer_length, plan.col, keepdims=False)
        passages = lax.dynamic_index_in_dim(passage_length, plan.col, keepdims=False)
        valid = (plan.own_positions < answers).astype(F32)[:, None]

        own_norms = jnp.concatenate([model_bias, norm_gain, norm_shift])
        group_one = Group([(0, 3, self_input.reshape(width, -1)), (1, 1, self_output)], n)
        group_two = Group(
            [(0, 1, cross_query), (0, 2, cross_memory.reshape(width, -1)), (1, 1, cross_output)], n
        )
        group_three = Group([(0, 1, expand_weight), (1, 1, shrink_weight)], n)
        group_expand, group_shrink = Group([(0, 1, expand_weight)], n), Group([(1, 1, shrink_weight)], n)
        tiled = plan.pair and all(g.fits() for g in (group_one, group_two, group_expand, group_shrink))
        if tiled:
            others_one = blocks.others_by_shift(group_one.pack(me))
            hidden = plan.sort(hidden)
            over_one = blocks.hops(others_one)
            corner_one = blocks.corner(over_one)
            w_self, w_self_out = assemble(me, plan.n_col, (group_one, (others_one, *over_one, *corner_one)))
        else:
            hidden = plan.sort(hidden)
            w_self, w_self_out = (blocks.whole(w) for w in group_one.weights)
            w_query, w_memory, w_cross_out = (blocks.whole(w) for w in group_two.weights)
            w_expand, w_shrink = (blocks.whole(g.weights[0]) for g in (group_expand, group_shrink))
        x_takes = plan.spread(hidden)
        encoder, cotangent = plan.sort(encoder), plan.sort(cotangent)

        if tiled:
            pieces = [group_two.pack(me), group_three.pack(me)]
            others_one, pieces, carried = tie(others_one, pieces, split_float(own_norms))
            (others_two,), extra = blocks.others_by_gather(pieces[0], 1, carried)
            (others_a, others_b), _ = blocks.others_by_gather(pieces[1], 2, None)
            norms = plan.reorder(join_float(extra, own_norms.shape))
        if not tiled:
            norms = plan.reorder(lax.all_gather(own_norms, "col", axis=0))
        norms = jnp.moveaxis(norms, 0, 1).reshape(own_norms.shape[0], -1)
        bias_rows, gain_rows, shift_rows = norms[:3], norms[3:6], norms[6:]

        head_parts = blocks.weave(head_bias)
        none = jnp.zeros((n, part), F32)
        self_bias = jnp.stack([head_parts[0], none, head_parts[1]], axis=1).reshape(-1)
        query_bias = head_parts[2].reshape(-1)
        memory_bias = jnp.stack([none, head_parts[3]], axis=1).reshape(-1)
        hidden_bias = blocks.weave(expand_bias).reshape(-1)

        own_x = plan.spread_end(x_takes)
        full_x = plan.gather_rows(own_x)
        packed = (dot(full_x, w_self) + self_bias).astype(BF)
        if tiled:
            packed, others_two, encoder, cotangent = tie(packed, others_two, encoder, cotangent)
            over_two = blocks.hops(others_two)
        encoder_takes = plan.spread(encoder)
        mixture, self_logsum = self_attention(plan, packed, answers, n)
        if tiled:
            mixture, over_two = tie(mixture, over_two)
            corner_two = blocks.corner(over_two)
        branch = plan.scatter_product(mixture, w_self_out) + bias_rows[0]
        if tiled:
            branch, others_a = tie(branch, others_a)
            over_a = blocks.hops(others_a)
        normed, normal_one, inverse_one = normalize(own_x.astype(F32) + branch, gain_rows[0], shift_rows[0])
        own_first = normed.astype(BF)
        if tiled:
            own_first, corner_two, over_a, others_b, encoder_takes, cotangent = tie(
                own_first, corner_two, over_a, others_b, encoder_takes, cotangent
            )
            corner_a = blocks.corner(over_a)
            over_b = blocks.hops(others_b)
        own_encoder = plan.spread_end(encoder_takes)
        full_encoder = plan.gather_rows(own_encoder)
        full_first = plan.gather_rows(own_first)
        if tiled:
            w_query, w_memory, w_cross_out = assemble(
                me, plan.n_col, (group_two, (others_two, *over_two, *corner_two))
            )
        memory = (dot(full_encoder, w_memory) + memory_bias).astype(BF)
        cross_q = (dot(full_first, w_query) + query_bias).astype(BF)
        cotangent_takes = plan.spread(cotangent)
        if tiled:
            cross_q, memory, over_b, corner_a = tie(cross_q, memory, over_b, corner_a)
            corner_b = blocks.corner(over_b)
        recall, cross_logsum = cross_attention(plan, cross_q, memory, answers, passages, n)
        if tiled:
            recall, corner_b, cotangent_takes = tie(recall, corner_b, cotangent_takes)
        branch = plan.scatter_product(recall, w_cross_out) + bias_rows[1]
        normed, normal_two, inverse_two = normalize(own_first.astype(F32) + branch, gain_rows[1], shift_rows[1])
        own_second = normed.astype(BF)
        full_second = plan.gather_rows(own_second)
        if tiled:
            w_expand, w_shrink = assemble(
                me,
                plan.n_col,
                (group_expand, (others_a, *over_a, *corner_a)),
                (group_shrink, (others_b, *over_b, *corner_b)),
            )
        expanded = dot(full_second, w_expand) + hidden_bias
        activated, slope = gelu_and_slope(expanded)
        branch = plan.scatter_product(activated, w_shrink) + bias_rows[2]
        normed, normal_three, inverse_three = normalize(
            own_second.astype(F32) + branch, gain_rows[2], shift_rows[2]
        )
        output_takes = plan.collect((normed * valid).astype(BF))

        own_cotangent = plan.spread_end(cotangent_takes)
        up_three = own_cotangent.astype(F32) * valid
        resid_three = norm_back(up_three, normal_three, inverse_three, gain_rows[2])
        own_dshrink = resid_three.astype(BF)
        full_dshrink = plan.gather_rows(own_dshrink)
        if tiled:
            of_shrink = [(blocks.product(activated, full_dshrink), 0, hidden_part)]
            send_shrink = blocks.reduce_send(of_shrink, 1)
            full_dshrink, send_shrink = tie(full_dshrink, send_shrink)
            got_shrink = blocks.hop(send_shrink, 1)
        d_expanded = (dot_flip(full_dshrink, w_shrink) * slope.astype(F32)).astype(BF)
        (d_expanded,) = tie(d_expanded)
        if tiled:
            of_expand = [(blocks.product(d_expanded, full_second), 0, hidden_part)]
            got_expand = blocks.reduce_start(of_expand, 2)
        up_two = resid_three + plan.scatter_product(d_expanded, w_expand, True)
        resid_two = norm_back(up_two, normal_two, inverse_two, gain_rows[1])
        own_dcross = resid_two.astype(BF)
        full_dcross = plan.gather_rows(own_dcross)
        d_recall = dot_flip(full_dcross, w_cross_out).astype(BF)
        d_cross_q, d_memory = cross_attention_back(
            plan, cross_q, memory, answers, passages, n, cross_logsum, d_recall
        )
        if tiled:
            d_cross_q, d_memory, got_shrink, got_expand, output_takes = tie(
                d_cross_q, d_memory, got_shrink, got_expand, output_takes
            )
            chunk_shrink = blocks.reduce_next(of_shrink, 1, got_shrink)
            chunk_expand = blocks.reduce_next(of_expand, 2, got_expand)
            of_cross_a = [
                (blocks.product(d_cross_q, full_first), 0, part),
                (blocks.product(recall, full_dcross), 0, part),
            ]
            of_cross_b = [(blocks.product(d_memory, full_encoder), 0, 2 * part)]
            got_cross_a = blocks.reduce_start(of_cross_a, 1)
            got_cross_b = blocks.reduce_start(of_cross_b, 2)
        up_one = resid_two + plan.scatter_product(d_cross_q, w_query, True)
        resid_one = norm_back(up_one, normal_one, inverse_one, gain_rows[0])
        own_dself = resid_one.astype(BF)
        full_dself = plan.gather_rows(own_dself)
        d_mixture = dot_flip(full_dself, w_self_out).astype(BF)
        encoder_grad_takes = plan.collect(plan.scatter_product(d_memory, w_memory, True).astype(BF))
        if tiled:
            (sums,) = sum_chunks(
                [as_chunk(of_shrink, 1, chunk_shrink), as_chunk(of_expand, 2, chunk_expand)],
                plan.n_col,
                plan.col,
                False,
            )
            grad_self_out = blocks.product(mixture, full_dself)
            d_mixture, sums, got_cross_a, got_cross_b, grad_self_out = tie(
                d_mixture, sums, got_cross_a, got_cross_b, grad_self_out
            )
            mine_hidden = lax.psum_scatter(sums, "col", scatter_dimension=0, tiled=False)
            chunk_cross_a = blocks.reduce_next(of_cross_a, 1, got_cross_a)
            chunk_cross_b = blocks.reduce_next(of_cross_b, 2, got_cross_b)
        d_packed = self_attention_back(plan, packed, answers, n, self_logsum, d_mixture)
        if tiled:
            d_packed, chunk_cross_a, chunk_cross_b, mine_hidden, encoder_grad_takes = tie(
                d_packed, chunk_cross_a, chunk_cross_b, mine_hidden, encoder_grad_takes
            )
            grad_self = blocks.product(d_packed, full_x)
            of_low = [(grad_self, 0, 2 * part)]
            of_high = [(grad_self, 2 * part, 3 * part), (grad_self_out, 0, part)]
            send_low, send_high = blocks.reduce_send(of_low, 1), blocks.reduce_send(of_high, 2)
            send_low, send_high, d_packed, chunk_cross_a, chunk_cross_b = tie(
                send_low, send_high, d_packed, chunk_cross_a, chunk_cross_b
            )
            got_low, got_high = blocks.hop(send_low, 1), blocks.hop(send_high, 2)
            (sums,) = sum_chunks(
                [as_chunk(of_cross_a, 1, chunk_cross_a), as_chunk(of_cross_b, 2, chunk_cross_b)],
                plan.n_col,
                plan.col,
                False,
            )
            mine_cross = lax.psum_scatter(sums, "col", scatter_dimension=0, tiled=False)

        def rows_of(values):
            return jnp.sum(values, axis=0, dtype=F32)

        wide = jnp.stack(
            [rows_of(v) for v in (own_dself, own_dcross, own_dshrink)]
            + [rows_of(u * v) for u, v in ((up_one, normal_one), (up_two, normal_two), (up_three, normal_three))]
            + [rows_of(v) for v in (up_one, up_two, up_three)]
        )
        packed_sums = rows_of(d_packed).reshape(n, 3, part)
        memory_sums = rows_of(d_memory).reshape(n, 2, part)
        narrow = jnp.concatenate(
            [
                blocks.unweave(v)
                for v in (
                    packed_sums[:, 0],
                    packed_sums[:, 2],
                    rows_of(d_cross_q).reshape(n, part),
                    memory_sums[:, 1],
                    rows_of(d_expanded).reshape(n, hidden_part),
                )
            ]
        )
        wide = total(wide, mesh, ("row",))
        wide = plan.reorder(jnp.moveaxis(wide.reshape(9, plan.n_col, width), 1, 0))
        small = jnp.concatenate([wide.reshape(-1), narrow])

        hidden_grad = (resid_one + plan.scatter_product(d_packed, w_self, True)).astype(BF)
        if tiled:
            small = small + blocks.hop(small, 1)
        hidden_grad = plan.cut(hidden_grad)
        if tiled:
            hidden_grad, got_low, got_high = tie(hidden_grad, got_low, got_high)
        hidden_takes = plan.deal(hidden_grad)
        if not tiled:
            small = total(small, mesh, ("dp", "col"))
        if tiled:
            g_encoder = plan.collect_end(encoder_grad_takes)
            small, output_takes, g_encoder = tie(small, output_takes, g_encoder)
            chunk_low = blocks.reduce_next(of_low, 1, got_low)
            chunk_high = blocks.reduce_next(of_high, 2, got_high)
            small = small + blocks.hop(small, 2)
            output = plan.collect_end(output_takes)
            ready = lax.all_gather(mine_hidden, "dp", axis=0)
            g_shrink, g_expand = finish(
                jnp.arange(n), [[((ready, q), 0)] for q in range(n)], [(1, False), (1, True)], hidden_part, width
            )
            chunk_low, chunk_high, small, output, hidden_takes = tie(
                chunk_low, chunk_high, small, output, hidden_takes
            )
            own, *rest = sum_chunks(
                [as_chunk(of_low, 1, chunk_low), as_chunk(of_high, 2, chunk_high)],
                plan.n_col,
                plan.col,
                True,
            )
            arrived = [own] + [plan.shift(r, -1 - k) for k, r in enumerate(rest)]
            small = small + lax.ppermute(small, "col", [(i, i ^ 1) for i in range(plan.n_col)])
            g_hidden = plan.collect_end(hidden_takes)
            ready = lax.all_gather(mine_cross, "dp", axis=0)
            arrived, g_hidden, g_shrink, g_expand, small, ready = tie(
                arrived, g_hidden, g_shrink, g_expand, small, ready
            )
            mine_self = sum(r.astype(F32) for r in arrived).astype(BF)
            over_self = blocks.hops(mine_self)
            small = small + lax.ppermute(small, "col", [(i, i ^ 2) for i in range(plan.n_col)])
            g_query, g_cross_out, g_memory = finish(
                jnp.arange(n),
                [[((ready, q), 0)] for q in range(n)],
                [(1, True), (1, False), (2, True)],
                part,
                width,
            )
            over_self, g_query, g_cross_out, g_memory = tie(over_self, g_query, g_cross_out, g_memory)
            corner_self = blocks.corner(over_self)
            g_self, g_self_out = finish(
                jnp.stack([me ^ j for j in range(n)]),
                [
                    [(mine_self, 0)],
                    [(over_self[0], 0)],
                    [(over_self[1], 0)],
                    [(corner_self[0], 0), (corner_self[1], 2 * part)],
                ],
                [(3, True), (1, False)],
                part,
                width,
            )
        else:
            g_shrink = blocks.plain(activated, full_dshrink, 1, False)
            g_expand = blocks.plain(d_expanded, full_second, 1, True)
            g_query = blocks.plain(d_cross_q, full_first, 1, True)
            g_memory = blocks.plain(d_memory, full_encoder, 2, True)
            g_cross_out = blocks.plain(recall, full_dcross, 1, False)
            g_self = blocks.plain(d_packed, full_x, 3, True)
            g_self_out = blocks.plain(mixture, full_dself, 1, False)
            output, g_encoder, g_hidden = (
                plan.collect_end(t) for t in (output_takes, encoder_grad_takes, hidden_takes)
            )

        own_wide = lax.dynamic_index_in_dim(
            small[: 9 * plan.n_col * width].reshape(plan.n_col, 9, width), plan.col, keepdims=False
        )
        narrow = small[9 * plan.n_col * width :]
        return (
            output,
            g_hidden,
            g_encoder,
            g_self.reshape(self_input.shape),
            g_self_out,
            g_query,
            g_memory.reshape(cross_memory.shape),
            g_cross_out,
            g_expand,
            g_shrink,
            narrow[: 4 * heads].reshape(4, heads),
            narrow[4 * heads :],
            own_wide[:3],
            own_wide[3:6],
            own_wide[6:],
        )

    return body


def solution(mesh):
    rows = P(("dp", "row"), "col")
    weights = (
        P("col", None, "row"),
        P("row", "col"),
        P("col", "row"),
        P("col", None, "row"),
        P("row", "col"),
        P("col", "row"),
        P("row", "col"),
        P(None, "row"),
        P("row"),
        P(None, "col"),
        P(None, "col"),
        P(None, "col"),
    )
    return jax.shard_map(
        layer(mesh),
        mesh=mesh,
        in_specs=(rows, rows, rows, P("dp"), P("dp")) + weights,
        out_specs=(rows, rows, rows) + weights,
        check_vma=False,
    )
```

```python
import functools
import math

import jax
import jax.numpy as jnp
from jax import lax
from jax.experimental import pallas as pl
from jax.experimental.pallas import tpu as pltpu
from jax.sharding import PartitionSpec as P

HEAD_DIM = 64
SLOT = 1024
BF = jnp.bfloat16
F32 = jnp.float32


def tie(*values):
    return lax.optimization_barrier(values)


def dot(left, right):
    return jnp.dot(left, right, preferred_element_type=F32)


def dot_flip(left, right):
    return lax.dot_general(left, right, (((1,), (1,)), ((), ())), preferred_element_type=F32)


def outer_sum(left, right):
    return lax.dot_general(left, right, (((0,), (0,)), ((), ())), preferred_element_type=F32)

def in_vmem(body, name, scalars, arrays, outs):
    count = len(arrays)

    def kernel(info, *refs):
        body(info, refs[:count], refs[count:])

    def spec(shape):
        return pl.BlockSpec(shape, lambda i, info: (0,) * len(shape))

    def spec_in(array):
        if not isinstance(array, tuple):
            return spec(array.shape)
        whole, at = array
        rest = whole.shape[1:]
        return pl.BlockSpec((None, *rest), lambda i, info: (at,) + (0,) * len(rest))

    return pl.pallas_call(
        kernel,
        out_shape=outs,
        grid_spec=pltpu.PrefetchScalarGridSpec(
            num_scalar_prefetch=1,
            grid=(1,),
            in_specs=[spec_in(a) for a in arrays],
            out_specs=[spec(o.shape) for o in outs],
        ),
        compiler_params=pltpu.CompilerParams(vmem_limit_bytes=56 * 2**20),
        cost_estimate=small_cost(),
        name=name,
    )(scalars, *[a[0] if isinstance(a, tuple) else a for a in arrays])


def lanes_at(start):
    return pl.ds(pl.multiple_of(start, 128), 128)


def join_columns(pieces, places):
    n, rows, width = pieces.shape

    def body(info, ins, outs):
        for i in range(n):
            start = pl.multiple_of(info[i] * width, width)
            outs[0][:, pl.ds(start, width)] = ins[0][i]

    out = jax.ShapeDtypeStruct((rows, width * n), pieces.dtype)
    return in_vmem(body, "join_columns", jnp.stack(places), [pieces], [out])[0]


def cut_columns(values, n_col, col):
    rows, width = values.shape[0], values.shape[1] // n_col

    def body(info, ins, outs):
        for owner in range(n_col):
            start = pl.multiple_of(lax.rem(info[0] - owner + n_col, n_col) * width, width)
            outs[0][owner] = ins[0][:, pl.ds(start, width)]

    out = jax.ShapeDtypeStruct((n_col, rows, width), values.dtype)
    return in_vmem(body, "cut_columns", col[None], [values], [out])[0]


def join_rows(pieces, own):
    seqs, rows, width = pieces[0].shape

    def body(info, ins, outs):
        for i in range(2):
            share = info[0] if i == 0 else 1 - info[0]
            for s in range(seqs):
                start = pl.multiple_of((2 * s + share) * rows, rows)
                outs[0][pl.ds(start, rows), :] = ins[i][s].astype(F32)

    out = jax.ShapeDtypeStruct((2 * seqs * rows, width), F32)
    return in_vmem(body, "join_rows", own[None], list(pieces), [out])[0]


def as_chunk(entries, first, brought):
    return entries, (brought[0], 1 if first == 1 else 0), brought[1]


def sum_chunks(chunks, n_col, col, apart):
    operands, plans = [], []
    total_rows = 0
    for entries, got, last in chunks:
        pieces = []
        for grad, low, high in entries:
            pieces.append((len(operands), low, high))
            operands.append((grad, 0))
        plans.append((pieces, len(operands), len(operands) + 1))
        operands += [got, last]
        total_rows += sum(high - low for _, low, high in entries)
    width = chunks[0][0][0][0].shape[2] // n_col

    def body(info, ins, outs):
        for k in range(n_col):
            if apart:
                start, target = k * width, outs[k]
            else:
                start, target = lax.rem(info[0] - k + n_col, n_col) * width, outs[0].at[k]
            columns = pl.ds(pl.multiple_of(start, width), width)
            row = 0
            for pieces, got, last in plans:
                inner = 0
                for at, low, high in pieces:
                    rows = slice(inner, inner + high - low)
                    terms = [ins[at][low:high, columns], ins[got][rows, columns], ins[last][rows, columns]]
                    target[row : row + high - low, :] = sum(t.astype(F32) for t in terms).astype(BF)
                    row += high - low
                    inner += high - low

    if apart:
        outs = [jax.ShapeDtypeStruct((total_rows, width), BF)] * n_col
    else:
        outs = [jax.ShapeDtypeStruct((n_col, total_rows, width), BF)]
    return in_vmem(body, "sum_chunks", col[None], operands, outs)


def finish(which, parts, layout, size, width):
    n = len(parts)
    operands = [o for part in parts for o, _ in part]
    outs = []
    for groups, turned in layout:
        shape = (width, groups, n * size) if groups > 1 else (width, n * size)
        outs.append(jax.ShapeDtypeStruct(shape if turned else (n * size, width), F32))

    def body(info, ins, outs):
        used = 0
        for i, part in enumerate(parts):
            refs = ins[used : used + len(part)]
            used += len(part)
            row = 0
            for (groups, turned), target in zip(layout, outs):
                for g in range(groups):
                    at = max(x for x in range(len(part)) if part[x][1] <= row)
                    block = refs[at][row - part[at][1] : row - part[at][1] + size, :].astype(F32)
                    start = pl.multiple_of(info[i] * size, size)
                    if turned and groups > 1:
                        target[:, g, pl.ds(start, size)] = block.T
                    elif turned:
                        target[:, pl.ds(start, size)] = block.T
                    else:
                        target[pl.ds(start, size), :] = block
                    row += size

    return in_vmem(body, "finish", which, operands, outs)


class Plan:
    def __init__(self, mesh):
        self.n_row = mesh.shape["row"]
        self.n_col = mesh.shape["col"]
        self.share = SLOT // self.n_row
        self.row = lax.axis_index("row")
        self.col = lax.axis_index("col")
        self.pair = self.n_row == 2
        self.offset = self.row * self.share if self.pair else jnp.int32(0)
        self.positions = (jnp.arange(SLOT, dtype=jnp.int32) + self.offset) % SLOT
        self.own_positions = self.row * self.share + jnp.arange(self.share, dtype=jnp.int32)

    def swap(self, values):
        return lax.ppermute(values, "row", [(0, 1), (1, 0)])

    def shift(self, values, k):
        n = self.n_col
        return lax.ppermute(values, "col", [(i, (i + k) % n) for i in range(n)])

    def block(self, other):
        return (self.col - other) % self.n_col

    def reorder(self, blocks):
        return jnp.stack(
            [lax.dynamic_index_in_dim(blocks, self.block(i), 0, keepdims=False) for i in range(self.n_col)]
        )

    def gather_rows(self, values):
        if self.pair:
            return jnp.concatenate([values, self.swap(values)], axis=0)
        return lax.all_gather(values, "row", axis=0, tiled=True)

    def scatter_product(self, left, right, flipped=False):
        times = dot_flip if flipped else dot
        if self.pair:
            away = self.swap(times(left[self.share :], right))
            return times(left[: self.share], right) + away
        return lax.psum_scatter(times(left, right), "row", scatter_dimension=0, tiled=True)

    def sort(self, values):
        width = values.shape[1]
        if self.pair and self.n_col == 4:
            parts = values.reshape(2, 2, self.share, width)
            keep = lax.dynamic_index_in_dim(parts, self.row, 1, keepdims=False)
            take = self.swap(lax.dynamic_index_in_dim(parts, 1 - self.row, 1, keepdims=False))
            ordered = jnp.zeros((4, self.share, width), BF)
            ordered = lax.dynamic_update_slice_in_dim(ordered, keep, 2 * self.row, axis=0)
            ordered = lax.dynamic_update_slice_in_dim(ordered, take, 2 - 2 * self.row, axis=0)
            return ordered
        whole = lax.all_gather(values, "row", axis=0, tiled=True)
        parts = whole.reshape(self.n_col, self.n_row, self.share, width)
        return lax.dynamic_index_in_dim(parts, self.row, 1, keepdims=False)

    def spread(self, ordered):
        return lax.all_to_all(ordered, "col", 0, 0, tiled=True)

    def spread_end(self, takes):
        if self.share % 128 == 0:
            return join_columns(takes, [self.block(i) for i in range(self.n_col)])
        return jnp.transpose(self.reorder(takes), (1, 0, 2)).reshape(self.share, -1)

    def collect(self, values):
        return self.deal(self.cut(values))

    def cut(self, values):
        width = values.shape[1] // self.n_col
        if self.share % 128 == 0:
            return cut_columns(values, self.n_col, self.col)
        return self.reorder(jnp.transpose(values.reshape(self.share, self.n_col, width), (1, 0, 2)))

    def deal(self, blocks):
        return lax.all_to_all(blocks, "col", 0, 0, tiled=True)

    def collect_end(self, moved):
        if self.pair and self.n_col == 4:
            keep = lax.dynamic_slice_in_dim(moved, 2 * self.row, 2, axis=0)
            take = self.swap(lax.dynamic_slice_in_dim(moved, 2 - 2 * self.row, 2, axis=0))
            return join_rows([keep, take], self.row)
        whole = lax.all_gather(moved, "row", axis=1, tiled=True).reshape(-1, moved.shape[2])
        rows = whole.shape[0] // self.n_row
        return lax.dynamic_slice_in_dim(whole, self.row * rows, rows, axis=0).astype(F32)


def normalize(residual, gain_row, shift_row):
    center = jnp.mean(residual, axis=-1, keepdims=True)
    moved = residual - center
    inverse = lax.rsqrt(jnp.mean(moved * moved, axis=-1, keepdims=True) + 1e-05)
    normal = moved * inverse
    return normal * gain_row + shift_row, normal, inverse


def norm_back(upstream, normal, inverse, gain_row):
    scaled = upstream * gain_row
    plain = jnp.mean(scaled, axis=-1, keepdims=True)
    cross = jnp.mean(scaled * normal, axis=-1, keepdims=True)
    return inverse * (scaled - plain - normal * cross)


def gelu_and_slope(values):
    cdf = 0.5 + 0.5 * lax.erf(values * math.sqrt(0.5))
    density = jnp.exp(-0.5 * values * values) * (1.0 / math.sqrt(2.0 * math.pi))
    return (values * cdf).astype(BF), (cdf + values * density).astype(BF)


LANES = 2 * HEAD_DIM
SPAN = 256
NEVER = -1000000000.0


def dot_last(left, right):
    return lax.dot_general(left, right, (((1,), (1,)), ((), ())), preferred_element_type=F32)


def place_of(start, offset):
    return pl.multiple_of(lax.rem(start + offset, SLOT), SPAN)


def heads_apart(rows):
    low = lax.broadcasted_iota(jnp.int32, rows.shape, 1) < HEAD_DIM
    none = jnp.zeros_like(rows)
    return jnp.where(low, rows, none), jnp.where(low, none, rows)


def key_spans(count):
    if count == 1:
        return [(0, SPAN)]
    return [(0, (count - 1) * SPAN), ((count - 1) * SPAN, count * SPAN)]


def score_spans(keys_ref, query, count, limit):
    parts = []
    for start, stop in key_spans(count):
        scores = dot_last(keys_ref[start:stop, :], query)
        if stop == count * SPAN:
            places = lax.broadcasted_iota(jnp.int32, scores.shape, 0)
            if limit is None:
                allowed = places <= lax.broadcasted_iota(jnp.int32, scores.shape, 1)
            else:
                allowed = places < limit - start
            scores = jnp.where(allowed, scores, NEVER)
        parts.append(scores)
    return parts


def for_each_block(causal, whole, query_length, key_length, run, skip):
    blocks = SLOT // SPAN
    half = blocks // 2
    spans = lax.div(key_length + (SPAN - 1), SPAN)
    short = query_length <= half * SPAN
    for count in (None,) if causal else range(1, blocks + 1):
        chosen = True if causal else spans == count
        items = [(i * SPAN, i + 1 if causal else count) for i in range(blocks)]
        if whole:
            pl.when(short & chosen)(functools.partial(run, *items[:half]))
            pl.when(jnp.logical_not(short) & chosen)(functools.partial(run, *items))
            continue

        @pl.when(chosen)
        def _(count=count):
            @pl.loop(0, jnp.where(short, 1, 2))
            def _(i):
                run(*[(pl.multiple_of((2 * i + k) * SPAN, SPAN), count) for k in range(2)])

    @pl.when(short)
    def _():
        for i in range(half, blocks):
            skip(i * SPAN)


def forward_kernel(causal, info, query_ref, key_ref, value_ref, out_ref, logsum_ref, keys, values_t):
    offset, query_length, key_length = info[0], info[1], info[2]
    half = SLOT // 2
    for start in (0, half):
        stored = place_of(start, offset)
        keys[start : start + half, :] = key_ref[pl.ds(stored, half), :]
        values_t[:, start : start + half] = value_ref[pl.ds(stored, half), :].T

    def run(*items):
        tasks = []
        for start, count in items:
            scaled = query_ref[pl.ds(place_of(start, offset), SPAN), :] * (1.0 / math.sqrt(HEAD_DIM))
            tasks += [(start, count, head, query) for head, query in enumerate(heads_apart(scaled))]

        def scores_of(task):
            return score_spans(keys, task[3], task[1], None if causal else key_length)

        outs = []
        ahead = scores_of(tasks[0])
        for at, (start, count, head, _) in enumerate(tasks):
            parts = ahead
            if at + 1 < len(tasks):
                ahead = scores_of(tasks[at + 1])
            highest = functools.reduce(jnp.maximum, [jnp.max(s, axis=0, keepdims=True) for s in parts])
            raised = [jnp.exp(s - highest) for s in parts]
            below = sum(jnp.sum(e, axis=0, keepdims=True) for e in raised)
            mixed = sum(
                jnp.dot(
                    values_t[head * HEAD_DIM : (head + 1) * HEAD_DIM, a:b],
                    e.astype(BF),
                    preferred_element_type=F32,
                )
                for (a, b), e in zip(key_spans(count), raised)
            )
            outs.append(mixed * (1.0 / below))
            logsum_ref[0, head : head + 1, pl.ds(start, SPAN)] = highest + jnp.log(below)
            if head == 1:
                both = jnp.concatenate(outs[at - 1 : at + 1], axis=0)
                out_ref[pl.ds(place_of(start, offset), SPAN), :] = both.T.astype(BF)

    def skip(start):
        out_ref[pl.ds(place_of(start, offset), SPAN), :] = jnp.zeros((SPAN, LANES), BF)

    for_each_block(causal, True, query_length, key_length, run, skip)


def backward_kernel(
    causal, info, query_ref, key_ref, value_ref, up_ref, logsum_ref, *refs
):
    if causal:
        packed_ref, keys, keys_t, values, key_sum, value_sum = refs
        query_out, other_out = packed_ref, packed_ref
        base = LANES
    else:
        query_out, other_out, keys, keys_t, values, key_sum, value_sum = refs
        base = 0
    offset, query_length, key_length = info[0], info[1], info[2]
    half = SLOT // 2
    for start in (0, half):
        stored = place_of(start, offset)
        block = key_ref[pl.ds(stored, half), :]
        keys[start : start + half, :] = block
        keys_t[:, start : start + half] = block.T
        values[start : start + half, :] = value_ref[pl.ds(stored, half), :]
    key_sum[...] = jnp.zeros_like(key_sum)
    value_sum[...] = jnp.zeros_like(value_sum)
    factor = 1.0 / math.sqrt(HEAD_DIM)

    def run(*items):
        tasks = []
        for start, count in items:
            stored = place_of(start, offset)
            queries = heads_apart(query_ref[pl.ds(stored, SPAN), :] * factor)
            ups = heads_apart(up_ref[pl.ds(stored, SPAN), :])
            tasks += [(start, count, head, queries[head], ups[head]) for head in range(2)]

        def products_of(task):
            _, count, _, query, up = task
            parts = score_spans(keys, query, count, None if causal else key_length)
            return parts, [dot_last(values[a:b, :], up) for a, b in key_spans(count)]

        outs, weights, grads = [], [], []
        ahead = products_of(tasks[0])
        for at, (start, count, head, _, _) in enumerate(tasks):
            parts, pulls = ahead
            if at + 1 < len(tasks):
                ahead = products_of(tasks[at + 1])
            logsum = logsum_ref[0, head : head + 1, pl.ds(start, SPAN)]
            parts = [jnp.exp(s - logsum) for s in parts]
            inner = sum(jnp.sum(p * g, axis=0, keepdims=True) for p, g in zip(parts, pulls))
            pulls = [(p * (g - inner)).astype(BF) for p, g in zip(parts, pulls)]
            outs.append(
                sum(
                    jnp.dot(
                        keys_t[head * HEAD_DIM : (head + 1) * HEAD_DIM, a:b],
                        g,
                        preferred_element_type=F32,
                    )
                    for (a, b), g in zip(key_spans(count), pulls)
                )
            )
            weights.append([p.astype(BF) for p in parts])
            grads.append(pulls)
            if head == 0:
                continue
            both = jnp.concatenate(outs[at - 1 : at + 1], axis=0) * factor
            query_out[pl.ds(place_of(start, offset), SPAN), 0:LANES] = both.T.astype(BF)
            for part, (a, b) in enumerate(key_spans(count)):
                value_sum[a:b, :] += sum(
                    jnp.dot(weights[t][part], tasks[t][4], preferred_element_type=F32) for t in (at - 1, at)
                )
                key_sum[a:b, :] += sum(
                    jnp.dot(grads[t][part], tasks[t][3], preferred_element_type=F32) for t in (at - 1, at)
                )

    def skip(start):
        query_out[pl.ds(place_of(start, offset), SPAN), 0:LANES] = jnp.zeros((SPAN, LANES), BF)

    for_each_block(causal, causal, query_length, key_length, run, skip)
    for start in (0, half):
        stored = place_of(start, offset)
        other_out[pl.ds(stored, half), base : base + LANES] = key_sum[start : start + half, :].astype(BF)
        other_out[pl.ds(stored, half), base + LANES : base + 2 * LANES] = value_sum[
            start : start + half, :
        ].astype(BF)


def column_block(width, of):
    return pl.BlockSpec((SLOT, width), lambda i, info: (0, of(i)))


LOGSUM_BLOCK = pl.BlockSpec((1, 2, SLOT), lambda i, info: (i, 0, 0))


def attention_cost():
    return pl.CostEstimate(flops=2 * 10**10, bytes_accessed=2**20, transcendentals=0)


def small_cost():
    return pl.CostEstimate(flops=0, bytes_accessed=2**16, transcendentals=0)


def attend(causal, info, query, keys, pairs):
    step = 3 if causal else 2
    first = 1 if causal else 0
    return pl.pallas_call(
        functools.partial(forward_kernel, causal),
        out_shape=(
            jax.ShapeDtypeStruct((SLOT, pairs * LANES), BF),
            jax.ShapeDtypeStruct((pairs, 2, SLOT), F32),
        ),
        grid_spec=pltpu.PrefetchScalarGridSpec(
            num_scalar_prefetch=1,
            grid=(pairs,),
            in_specs=[
                column_block(LANES, (lambda i: 3 * i) if causal else (lambda i: i)),
                column_block(LANES, lambda i: step * i + first),
                column_block(LANES, lambda i: step * i + first + 1),
            ],
            out_specs=(column_block(LANES, lambda i: i), LOGSUM_BLOCK),
            scratch_shapes=[pltpu.VMEM((SLOT, LANES), BF), pltpu.VMEM((LANES, SLOT), BF)],
        ),
        compiler_params=pltpu.CompilerParams(vmem_limit_bytes=48 * 2**20),
        cost_estimate=attention_cost(),
        name="attend",
    )(info, query, keys, keys)


def attend_back(causal, info, query, keys, logsum, upstream, pairs):
    step = 3 if causal else 2
    first = 1 if causal else 0
    if causal:
        out_shape = jax.ShapeDtypeStruct((SLOT, pairs * 3 * LANES), BF)
        out_specs = column_block(3 * LANES, lambda i: i)
    else:
        out_shape = (
            jax.ShapeDtypeStruct((SLOT, pairs * LANES), BF),
            jax.ShapeDtypeStruct((SLOT, pairs * 2 * LANES), BF),
        )
        out_specs = (column_block(LANES, lambda i: i), column_block(2 * LANES, lambda i: i))
    return pl.pallas_call(
        functools.partial(backward_kernel, causal),
        out_shape=out_shape,
        grid_spec=pltpu.PrefetchScalarGridSpec(
            num_scalar_prefetch=1,
            grid=(pairs,),
            in_specs=[
                column_block(LANES, (lambda i: 3 * i) if causal else (lambda i: i)),
                column_block(LANES, lambda i: step * i + first),
                column_block(LANES, lambda i: step * i + first + 1),
                column_block(LANES, lambda i: i),
                LOGSUM_BLOCK,
            ],
            out_specs=out_specs,
            scratch_shapes=[
                pltpu.VMEM((SLOT, LANES), BF),
                pltpu.VMEM((LANES, SLOT), BF),
                pltpu.VMEM((SLOT, LANES), BF),
                pltpu.VMEM((SLOT, LANES), F32),
                pltpu.VMEM((SLOT, LANES), F32),
            ],
        ),
        compiler_params=pltpu.CompilerParams(vmem_limit_bytes=48 * 2**20),
        cost_estimate=attention_cost() if causal else small_cost(),
        name="attend_back",
    )(info, query, keys, keys, upstream, logsum)


def build_mask(positions, length, causal):
    allowed = jnp.broadcast_to(positions[None, :] < length, (SLOT, SLOT))
    if causal:
        allowed = allowed & (positions[None, :] <= positions[:, None])
    return allowed


def score_block(query, key, allowed):
    factor = 1.0 / math.sqrt(HEAD_DIM)
    scores = jnp.einsum("qhd,khd->hqk", query, key, preferred_element_type=F32) * factor
    return jnp.where(allowed[None], scores, -1000000000.0)


def split_heads(values):
    return values.reshape(SLOT, -1, HEAD_DIM)


def attention_forward(query, key, value, allowed):
    query, key, value = (split_heads(v) for v in (query, key, value))
    scores = score_block(query, key, allowed)
    highest = jnp.max(scores, axis=-1, keepdims=True)
    raised = jnp.exp(scores - highest)
    denominator = jnp.sum(raised, axis=-1, keepdims=True)
    weights = (raised / denominator).astype(BF)
    mixture = jnp.einsum("hqk,khd->qhd", weights, value, preferred_element_type=F32)
    return mixture.reshape(SLOT, -1).astype(BF), highest + jnp.log(denominator)


def attention_backward(query, key, value, allowed, logsum, upstream):
    query, key, value, upstream = (split_heads(v) for v in (query, key, value, upstream))
    factor = 1.0 / math.sqrt(HEAD_DIM)
    weights = jnp.exp(score_block(query, key, allowed) - logsum)
    value_grad = jnp.einsum("hqk,qhd->khd", weights.astype(BF), upstream, preferred_element_type=F32)
    weight_grad = jnp.einsum("qhd,khd->hqk", upstream, value, preferred_element_type=F32)
    inner = jnp.sum(weights * weight_grad, axis=-1, keepdims=True)
    score_grad = (weights * (weight_grad - inner)).astype(BF)
    query_grad = jnp.einsum("hqk,khd->qhd", score_grad, key, preferred_element_type=F32) * factor
    key_grad = jnp.einsum("hqk,qhd->khd", score_grad, query, preferred_element_type=F32) * factor
    return tuple(g.reshape(SLOT, -1).astype(BF) for g in (query_grad, key_grad, value_grad))


def interleave(arrays, n):
    rows = arrays[0].shape[0]
    return jnp.stack([a.reshape(rows, n, -1) for a in arrays], axis=2).reshape(rows, -1)


def apart(array, n, count):
    rows = array.shape[0]
    parts = array.reshape(rows, n, count, -1)
    return [parts[:, :, i].reshape(rows, -1) for i in range(count)]


def self_attention(plan, packed, length, n):
    if packed.shape[1] == 3 * n * LANES:
        info = jnp.stack([plan.offset, length, length])
        return attend(True, info, packed, packed, n)
    mask = build_mask(plan.positions, length, True)
    return attention_forward(*apart(packed, n, 3), mask)


def self_attention_back(plan, packed, length, n, logsum, upstream):
    if packed.shape[1] == 3 * n * LANES:
        info = jnp.stack([plan.offset, length, length])
        return attend_back(True, info, packed, packed, logsum, upstream, n)
    mask = build_mask(plan.positions, length, True)
    return interleave(attention_backward(*apart(packed, n, 3), mask, logsum, upstream), n)


def cross_attention(plan, query, memory, query_length, key_length, n):
    if query.shape[1] == n * LANES:
        info = jnp.stack([plan.offset, query_length, key_length])
        return attend(False, info, query, memory, n)
    mask = build_mask(plan.positions, key_length, False)
    return attention_forward(query, *apart(memory, n, 2), mask)


def cross_attention_back(plan, query, memory, query_length, key_length, n, logsum, upstream):
    if query.shape[1] == n * LANES:
        info = jnp.stack([plan.offset, query_length, key_length])
        return attend_back(False, info, query, memory, logsum, upstream, n)
    mask = build_mask(plan.positions, key_length, False)
    first, *rest = attention_backward(query, *apart(memory, n, 2), mask, logsum, upstream)
    return first, interleave(rest, n)


ORDER = (0, 2, 3, 1)


class Group:
    def __init__(self, weights, n):
        self.weights = weights
        self.n = n
        self.plans = []
        row = 0
        for axis, groups, local in weights:
            if axis == 0:
                tall, count = local.shape[0], local.shape[1] // n // 128
            else:
                tall, count = local.shape[0] // n, local.shape[1] // 128
            self.plans.append((row, tall, count))
            row += tall * count
        self.rows = row

    def fits(self):
        return all(
            (local.shape[1] % (groups * self.n * 128) == 0 if axis == 0 else local.shape[0] % (self.n * 128) == 0)
            for axis, groups, local in self.weights
        )

    def local_block(self, ref, at, which, block):
        axis, groups, local = self.weights[at]
        _, tall, count = self.plans[at]
        if axis == 0:
            per = count // groups
            i, b = divmod(block, per)
            return ref[:, lanes_at((i * self.n * per + b) * 128 + which * (per * 128))]
        return ref[pl.ds(pl.multiple_of(which * tall, tall), tall), block * 128 : (block + 1) * 128]

    def pack(self, me):
        def body(info, ins, outs):
            for at, (row, tall, count) in enumerate(self.plans):
                for block in range(count):
                    start = row + block * tall
                    outs[0][start : start + tall, :] = self.local_block(ins[at], at, info[0], block)

        out = jax.ShapeDtypeStruct((self.rows, 128), BF)
        return in_vmem(body, "pack", me[None], [w[2] for w in self.weights], [out])[0]

    def outputs(self, n_col):
        outs = []
        for axis, groups, local in self.weights:
            shape = (local.shape[0] * n_col, local.shape[1]) if axis == 0 else (local.shape[0], local.shape[1] * n_col)
            outs.append(jax.ShapeDtypeStruct(shape, BF))
        return outs

    def fill(self, info, n_col, local_refs, moved_refs, outs):
        half = self.rows * (n_col - 1) // 2
        for at, (row, tall, count) in enumerate(self.plans):
            axis = self.weights[at][0]
            width = self.weights[at][2].shape[1]
            for place, j in enumerate(ORDER):
                for k in range(n_col):
                    for block in range(count):
                        if k == 0:
                            value = self.local_block(local_refs[at], at, info[j], block)
                        else:
                            start = (k - 1) * self.rows + row + block * tall
                            ref = moved_refs[j]
                            if j == 3 and start >= half:
                                ref, start = moved_refs[4], start - half
                            value = ref[start : start + tall, :]
                        if axis == 0:
                            column = (place * count + block) * 128
                            outs[at][k * tall : (k + 1) * tall, column : column + 128] = value
                        else:
                            column = k * width + block * 128
                            outs[at][place * tall : (place + 1) * tall, column : column + 128] = value


def assemble(me, n_col, *groups):
    operands, outs = [], []
    for group, moved in groups:
        operands += [w[2] for w in group.weights] + list(moved)
        outs += group.outputs(n_col)

    def body(info, ins, outs):
        for group, moved in groups:
            count = len(group.weights)
            group.fill(info, n_col, ins[:count], ins[count : count + len(moved)], outs[:count])
            ins, outs = ins[count + len(moved) :], outs[count:]

    which = jnp.stack([me ^ j for j in range(len(ORDER))])
    return in_vmem(body, "assemble", which, operands, outs)


def split_float(values):
    high = lax.reduce_precision(values, 8, 7)
    middle = lax.reduce_precision(values - high, 8, 7)
    low = values - high - middle
    parts = jnp.concatenate([high, middle, low], axis=0).astype(BF)
    parts = jnp.concatenate([parts[:, i : i + 128] for i in range(0, parts.shape[1], 128)], axis=0)
    return jnp.pad(parts, ((0, -parts.shape[0] % 16), (0, 0)))


def join_float(rows, shape):
    n, width = shape
    count = width // 128
    parts = rows[:, : 3 * n * count].reshape(rows.shape[0], count, 3, n, 128).astype(F32)
    whole = parts[:, :, 0] + (parts[:, :, 1] + parts[:, :, 2])
    return jnp.moveaxis(whole, 1, 2).reshape(rows.shape[0], n, width)


def pick_others(every, at, rows, n_col, col):
    width = every.shape[2]
    return pl.pallas_call(
        lambda info, source, target: target.__setitem__(Ellipsis, source[...]),
        out_shape=jax.ShapeDtypeStruct(((n_col - 1) * rows, width), every.dtype),
        grid_spec=pltpu.PrefetchScalarGridSpec(
            num_scalar_prefetch=1,
            grid=(n_col - 1,),
            in_specs=[
                pl.BlockSpec(
                    (None, rows, width), lambda k, info: (lax.rem(info[0] - k - 1 + n_col, n_col), at, 0)
                )
            ],
            out_specs=pl.BlockSpec((rows, width), lambda k, info: (k, 0)),
        ),
        cost_estimate=small_cost(),
        name="pick_others",
    )(col[None], every)


class Blocks:
    def __init__(self, mesh, plan):
        self.n = mesh.shape["dp"]
        assert self.n == len(ORDER)
        self.plan = plan
        self.me = lax.axis_index("dp")

    def hop(self, values, step):
        return lax.ppermute(values, "dp", [(i, i ^ step) for i in range(self.n)])

    def own(self, values, axis, j=0, wait=0):
        shape = values.shape
        parts = values.reshape(shape[:axis] + (self.n, shape[axis] // self.n) + shape[axis + 1 :])
        return lax.dynamic_index_in_dim(parts, (self.me ^ j) + wait, axis, keepdims=False)

    def weave(self, values):
        return jnp.stack([self.own(values, values.ndim - 1, j) for j in ORDER], axis=-2)

    def unweave(self, values):
        order = jnp.array([ORDER.index(j) for j in range(self.n)])
        return jnp.concatenate(
            [
                lax.dynamic_index_in_dim(values, order[self.me ^ q], 0, keepdims=False)
                for q in range(self.n)
            ]
        )

    def others_by_shift(self, piece):
        return jnp.concatenate([self.plan.shift(piece, k) for k in range(1, self.plan.n_col)], axis=0)

    def others_by_gather(self, piece, count, extra):
        total_rows = piece.shape[0]
        if extra is not None:
            piece = jnp.concatenate([piece, extra], axis=0)
        every = lax.all_gather(piece, "col", axis=0)
        rows = total_rows // count
        picked = [pick_others(every, i, rows, self.plan.n_col, self.plan.col) for i in range(count)]
        return picked, every[:, total_rows:]

    def hops(self, others):
        return self.hop(others, 1), self.hop(others, 2)

    def corner(self, over):
        half = over[0].shape[0] // 2
        return self.hop(over[1][:half], 1), self.hop(over[0][half:], 2)

    def whole(self, weight):
        axis, groups, local = weight
        every = self.plan.reorder(lax.all_gather(local, "col", axis=0))
        if axis == 0:
            every = every.reshape(-1, groups, local.shape[1] // groups)
            return jnp.stack([self.weave(every[:, i]) for i in range(groups)], axis=2).reshape(every.shape[0], -1)
        every = jnp.moveaxis(every, 0, 1).reshape(local.shape[0], -1)
        parts = every.reshape(self.n, -1, every.shape[1])
        picked = [lax.dynamic_index_in_dim(parts, self.me ^ j, 0, keepdims=False) for j in ORDER]
        return jnp.concatenate(picked, axis=0)

    def product(self, hidden, model):
        grad = outer_sum(hidden, model).astype(BF)
        return grad.reshape(self.n, -1, grad.shape[1])

    def reduce_start(self, entries, first):
        return self.hop(self.reduce_send(entries, first), first)

    def reduce_send(self, entries, first):
        a, b = (2, 4) if first == 1 else (1, 3)
        sends = [grad[a:b, low:high] for grad, low, high in entries]
        return sends[0] if len(sends) == 1 else jnp.concatenate(sends, axis=1)

    def reduce_next(self, entries, first, got):
        to_middle, to_base = (0, 1) if first == 1 else (1, 0)
        place = 1 if first == 1 else 3
        keeps = [grad[place, low:high] for grad, low, high in entries]
        middle = keeps[0] if len(keeps) == 1 else jnp.concatenate(keeps, axis=0)
        return got, self.hop(middle + got[to_middle], 3 - first)

    def plain(self, hidden, model, groups, turned):
        plan = self.plan
        grad = outer_sum(hidden, model).astype(BF)
        parts = grad.reshape(self.n, groups, -1, grad.shape[1])
        natural = [
            lax.dynamic_index_in_dim(parts, jnp.array([ORDER.index(j) for j in range(self.n)])[self.me ^ q], 0)
            for q in range(self.n)
        ]
        grad = jnp.moveaxis(jnp.concatenate(natural, axis=0), 1, 0).reshape(grad.shape[0], plan.n_col, -1)
        grad = lax.psum(plan.reorder(jnp.moveaxis(grad, 1, 0)), "dp")
        grad = lax.psum_scatter(grad, "col", scatter_dimension=0, tiled=False).astype(F32)
        return grad.T if turned else grad


def total(values, mesh, axes):
    for axis in axes:
        size = mesh.shape[axis]
        step = 1
        while step < size:
            values = values + lax.ppermute(values, axis, [(i, i ^ step) for i in range(size)])
            step *= 2
    return values


def layer(mesh):
    def body(
        hidden,
        encoder,
        cotangent,
        answer_length,
        passage_length,
        self_input,
        self_output,
        cross_query,
        cross_memory,
        cross_output,
        expand_weight,
        shrink_weight,
        head_bias,
        expand_bias,
        model_bias,
        norm_gain,
        norm_shift,
    ):
        plan = Plan(mesh)
        blocks = Blocks(mesh, plan)
        n = blocks.n
        me = blocks.me
        width = model_bias.shape[1]
        heads = self_output.shape[0]
        part = heads // n
        hidden_part = expand_bias.shape[0] // n
        answers = lax.dynamic_index_in_dim(answer_length, plan.col, keepdims=False)
        passages = lax.dynamic_index_in_dim(passage_length, plan.col, keepdims=False)
        valid = (plan.own_positions < answers).astype(F32)[:, None]

        own_norms = jnp.concatenate([model_bias, norm_gain, norm_shift])
        group_one = Group([(0, 3, self_input.reshape(width, -1)), (1, 1, self_output)], n)
        group_two = Group(
            [(0, 1, cross_query), (0, 2, cross_memory.reshape(width, -1)), (1, 1, cross_output)], n
        )
        group_three = Group([(0, 1, expand_weight), (1, 1, shrink_weight)], n)
        group_expand, group_shrink = Group([(0, 1, expand_weight)], n), Group([(1, 1, shrink_weight)], n)
        tiled = plan.pair and all(g.fits() for g in (group_one, group_two, group_expand, group_shrink))
        if tiled:
            others_one = blocks.others_by_shift(group_one.pack(me))
            hidden = plan.sort(hidden)
            over_one = blocks.hops(others_one)
            corner_one = blocks.corner(over_one)
            w_self, w_self_out = assemble(me, plan.n_col, (group_one, (others_one, *over_one, *corner_one)))
        else:
            hidden = plan.sort(hidden)
            w_self, w_self_out = (blocks.whole(w) for w in group_one.weights)
            w_query, w_memory, w_cross_out = (blocks.whole(w) for w in group_two.weights)
            w_expand, w_shrink = (blocks.whole(g.weights[0]) for g in (group_expand, group_shrink))
        x_takes = plan.spread(hidden)
        encoder, cotangent = plan.sort(encoder), plan.sort(cotangent)

        if tiled:
            pieces = [group_two.pack(me), group_three.pack(me)]
            others_one, pieces, carried = tie(others_one, pieces, split_float(own_norms))
            (others_two,), extra = blocks.others_by_gather(pieces[0], 1, carried)
            (others_a, others_b), _ = blocks.others_by_gather(pieces[1], 2, None)
            norms = plan.reorder(join_float(extra, own_norms.shape))
        if not tiled:
            norms = plan.reorder(lax.all_gather(own_norms, "col", axis=0))
        norms = jnp.moveaxis(norms, 0, 1).reshape(own_norms.shape[0], -1)
        bias_rows, gain_rows, shift_rows = norms[:3], norms[3:6], norms[6:]

        head_parts = blocks.weave(head_bias)
        none = jnp.zeros((n, part), F32)
        self_bias = jnp.stack([head_parts[0], none, head_parts[1]], axis=1).reshape(-1)
        query_bias = head_parts[2].reshape(-1)
        memory_bias = jnp.stack([none, head_parts[3]], axis=1).reshape(-1)
        hidden_bias = blocks.weave(expand_bias).reshape(-1)

        own_x = plan.spread_end(x_takes)
        full_x = plan.gather_rows(own_x)
        packed = (dot(full_x, w_self) + self_bias).astype(BF)
        if tiled:
            packed, others_two, encoder, cotangent = tie(packed, others_two, encoder, cotangent)
            over_two = blocks.hops(others_two)
        encoder_takes = plan.spread(encoder)
        mixture, self_logsum = self_attention(plan, packed, answers, n)
        if tiled:
            mixture, over_two = tie(mixture, over_two)
            corner_two = blocks.corner(over_two)
        branch = plan.scatter_product(mixture, w_self_out) + bias_rows[0]
        if tiled:
            branch, others_a = tie(branch, others_a)
            over_a = blocks.hops(others_a)
        normed, normal_one, inverse_one = normalize(own_x.astype(F32) + branch, gain_rows[0], shift_rows[0])
        own_first = normed.astype(BF)
        if tiled:
            own_first, corner_two, over_a, others_b, encoder_takes, cotangent = tie(
                own_first, corner_two, over_a, others_b, encoder_takes, cotangent
            )
            corner_a = blocks.corner(over_a)
            over_b = blocks.hops(others_b)
        own_encoder = plan.spread_end(encoder_takes)
        full_encoder = plan.gather_rows(own_encoder)
        full_first = plan.gather_rows(own_first)
        if tiled:
            w_query, w_memory, w_cross_out = assemble(
                me, plan.n_col, (group_two, (others_two, *over_two, *corner_two))
            )
        memory = (dot(full_encoder, w_memory) + memory_bias).astype(BF)
        cross_q = (dot(full_first, w_query) + query_bias).astype(BF)
        cotangent_takes = plan.spread(cotangent)
        if tiled:
            cross_q, memory, over_b, corner_a = tie(cross_q, memory, over_b, corner_a)
            corner_b = blocks.corner(over_b)
        recall, cross_logsum = cross_attention(plan, cross_q, memory, answers, passages, n)
        if tiled:
            recall, corner_b, cotangent_takes = tie(recall, corner_b, cotangent_takes)
        branch = plan.scatter_product(recall, w_cross_out) + bias_rows[1]
        normed, normal_two, inverse_two = normalize(own_first.astype(F32) + branch, gain_rows[1], shift_rows[1])
        own_second = normed.astype(BF)
        full_second = plan.gather_rows(own_second)
        if tiled:
            w_expand, w_shrink = assemble(
                me,
                plan.n_col,
                (group_expand, (others_a, *over_a, *corner_a)),
                (group_shrink, (others_b, *over_b, *corner_b)),
            )
        expanded = dot(full_second, w_expand) + hidden_bias
        activated, slope = gelu_and_slope(expanded)
        branch = plan.scatter_product(activated, w_shrink) + bias_rows[2]
        normed, normal_three, inverse_three = normalize(
            own_second.astype(F32) + branch, gain_rows[2], shift_rows[2]
        )
        output_takes = plan.collect((normed * valid).astype(BF))

        own_cotangent = plan.spread_end(cotangent_takes)
        up_three = own_cotangent.astype(F32) * valid
        resid_three = norm_back(up_three, normal_three, inverse_three, gain_rows[2])
        own_dshrink = resid_three.astype(BF)
        full_dshrink = plan.gather_rows(own_dshrink)
        if tiled:
            of_shrink = [(blocks.product(activated, full_dshrink), 0, hidden_part)]
            send_shrink = blocks.reduce_send(of_shrink, 1)
            full_dshrink, send_shrink = tie(full_dshrink, send_shrink)
            got_shrink = blocks.hop(send_shrink, 1)
        d_expanded = (dot_flip(full_dshrink, w_shrink) * slope.astype(F32)).astype(BF)
        (d_expanded,) = tie(d_expanded)
        if tiled:
            of_expand = [(blocks.product(d_expanded, full_second), 0, hidden_part)]
            got_expand = blocks.reduce_start(of_expand, 2)
        up_two = resid_three + plan.scatter_product(d_expanded, w_expand, True)
        resid_two = norm_back(up_two, normal_two, inverse_two, gain_rows[1])
        own_dcross = resid_two.astype(BF)
        full_dcross = plan.gather_rows(own_dcross)
        d_recall = dot_flip(full_dcross, w_cross_out).astype(BF)
        d_cross_q, d_memory = cross_attention_back(
            plan, cross_q, memory, answers, passages, n, cross_logsum, d_recall
        )
        if tiled:
            d_cross_q, d_memory, got_shrink, got_expand, output_takes = tie(
                d_cross_q, d_memory, got_shrink, got_expand, output_takes
            )
            chunk_shrink = blocks.reduce_next(of_shrink, 1, got_shrink)
            chunk_expand = blocks.reduce_next(of_expand, 2, got_expand)
            of_cross_a = [
                (blocks.product(d_cross_q, full_first), 0, part),
                (blocks.product(recall, full_dcross), 0, part),
            ]
            of_cross_b = [(blocks.product(d_memory, full_encoder), 0, 2 * part)]
            got_cross_a = blocks.reduce_start(of_cross_a, 1)
            got_cross_b = blocks.reduce_start(of_cross_b, 2)
        up_one = resid_two + plan.scatter_product(d_cross_q, w_query, True)
        resid_one = norm_back(up_one, normal_one, inverse_one, gain_rows[0])
        own_dself = resid_one.astype(BF)
        full_dself = plan.gather_rows(own_dself)
        d_mixture = dot_flip(full_dself, w_self_out).astype(BF)
        encoder_grad_takes = plan.collect(plan.scatter_product(d_memory, w_memory, True).astype(BF))
        if tiled:
            (sums,) = sum_chunks(
                [as_chunk(of_shrink, 1, chunk_shrink), as_chunk(of_expand, 2, chunk_expand)],
                plan.n_col,
                plan.col,
                False,
            )
            grad_self_out = blocks.product(mixture, full_dself)
            d_mixture, sums, got_cross_a, got_cross_b, grad_self_out = tie(
                d_mixture, sums, got_cross_a, got_cross_b, grad_self_out
            )
            mine_hidden = lax.psum_scatter(sums, "col", scatter_dimension=0, tiled=False)
            chunk_cross_a = blocks.reduce_next(of_cross_a, 1, got_cross_a)
            chunk_cross_b = blocks.reduce_next(of_cross_b, 2, got_cross_b)
        d_packed = self_attention_back(plan, packed, answers, n, self_logsum, d_mixture)
        if tiled:
            d_packed, chunk_cross_a, chunk_cross_b, mine_hidden, encoder_grad_takes = tie(
                d_packed, chunk_cross_a, chunk_cross_b, mine_hidden, encoder_grad_takes
            )
            grad_self = blocks.product(d_packed, full_x)
            of_low = [(grad_self, 0, 2 * part)]
            of_high = [(grad_self, 2 * part, 3 * part), (grad_self_out, 0, part)]
            send_low, send_high = blocks.reduce_send(of_low, 1), blocks.reduce_send(of_high, 2)
            send_low, send_high, d_packed, chunk_cross_a, chunk_cross_b = tie(
                send_low, send_high, d_packed, chunk_cross_a, chunk_cross_b
            )
            got_low, got_high = blocks.hop(send_low, 1), blocks.hop(send_high, 2)
            (sums,) = sum_chunks(
                [as_chunk(of_cross_a, 1, chunk_cross_a), as_chunk(of_cross_b, 2, chunk_cross_b)],
                plan.n_col,
                plan.col,
                False,
            )
            mine_cross = lax.psum_scatter(sums, "col", scatter_dimension=0, tiled=False)

        def rows_of(values):
            return jnp.sum(values, axis=0, dtype=F32)

        wide = jnp.stack(
            [rows_of(v) for v in (own_dself, own_dcross, own_dshrink)]
            + [rows_of(u * v) for u, v in ((up_one, normal_one), (up_two, normal_two), (up_three, normal_three))]
            + [rows_of(v) for v in (up_one, up_two, up_three)]
        )
        packed_sums = rows_of(d_packed).reshape(n, 3, part)
        memory_sums = rows_of(d_memory).reshape(n, 2, part)
        narrow = jnp.concatenate(
            [
                blocks.unweave(v)
                for v in (
                    packed_sums[:, 0],
                    packed_sums[:, 2],
                    rows_of(d_cross_q).reshape(n, part),
                    memory_sums[:, 1],
                    rows_of(d_expanded).reshape(n, hidden_part),
                )
            ]
        )
        wide = total(wide, mesh, ("row",))
        wide = plan.reorder(jnp.moveaxis(wide.reshape(9, plan.n_col, width), 1, 0))
        small = jnp.concatenate([wide.reshape(-1), narrow])

        hidden_grad = (resid_one + plan.scatter_product(d_packed, w_self, True)).astype(BF)
        if tiled:
            small = small + blocks.hop(small, 1)
        hidden_grad = plan.cut(hidden_grad)
        if tiled:
            hidden_grad, got_low, got_high = tie(hidden_grad, got_low, got_high)
        hidden_takes = plan.deal(hidden_grad)
        if not tiled:
            small = total(small, mesh, ("dp", "col"))
        if tiled:
            g_encoder = plan.collect_end(encoder_grad_takes)
            small, output_takes, g_encoder = tie(small, output_takes, g_encoder)
            chunk_low = blocks.reduce_next(of_low, 1, got_low)
            chunk_high = blocks.reduce_next(of_high, 2, got_high)
            small = small + blocks.hop(small, 2)
            output = plan.collect_end(output_takes)
            ready = lax.all_gather(mine_hidden, "dp", axis=0)
            g_shrink, g_expand = finish(
                jnp.arange(n), [[((ready, q), 0)] for q in range(n)], [(1, False), (1, True)], hidden_part, width
            )
            chunk_low, chunk_high, small, output, hidden_takes = tie(
                chunk_low, chunk_high, small, output, hidden_takes
            )
            own, *rest = sum_chunks(
                [as_chunk(of_low, 1, chunk_low), as_chunk(of_high, 2, chunk_high)],
                plan.n_col,
                plan.col,
                True,
            )
            arrived = [own] + [plan.shift(r, -1 - k) for k, r in enumerate(rest)]
            small = small + lax.ppermute(small, "col", [(i, i ^ 1) for i in range(plan.n_col)])
            g_hidden = plan.collect_end(hidden_takes)
            ready = lax.all_gather(mine_cross, "dp", axis=0)
            arrived, g_hidden, g_shrink, g_expand, small, ready = tie(
                arrived, g_hidden, g_shrink, g_expand, small, ready
            )
            mine_self = sum(r.astype(F32) for r in arrived).astype(BF)
            over_self = blocks.hops(mine_self)
            small = small + lax.ppermute(small, "col", [(i, i ^ 2) for i in range(plan.n_col)])
            g_query, g_cross_out, g_memory = finish(
                jnp.arange(n),
                [[((ready, q), 0)] for q in range(n)],
                [(1, True), (1, False), (2, True)],
                part,
                width,
            )
            over_self, g_query, g_cross_out, g_memory = tie(over_self, g_query, g_cross_out, g_memory)
            corner_self = blocks.corner(over_self)
            g_self, g_self_out = finish(
                jnp.stack([me ^ j for j in range(n)]),
                [
                    [(mine_self, 0)],
                    [(over_self[0], 0)],
                    [(over_self[1], 0)],
                    [(corner_self[0], 0), (corner_self[1], 2 * part)],
                ],
                [(3, True), (1, False)],
                part,
                width,
            )
        else:
            g_shrink = blocks.plain(activated, full_dshrink, 1, False)
            g_expand = blocks.plain(d_expanded, full_second, 1, True)
            g_query = blocks.plain(d_cross_q, full_first, 1, True)
            g_memory = blocks.plain(d_memory, full_encoder, 2, True)
            g_cross_out = blocks.plain(recall, full_dcross, 1, False)
            g_self = blocks.plain(d_packed, full_x, 3, True)
            g_self_out = blocks.plain(mixture, full_dself, 1, False)
            output, g_encoder, g_hidden = (
                plan.collect_end(t) for t in (output_takes, encoder_grad_takes, hidden_takes)
            )

        own_wide = lax.dynamic_index_in_dim(
            small[: 9 * plan.n_col * width].reshape(plan.n_col, 9, width), plan.col, keepdims=False
        )
        narrow = small[9 * plan.n_col * width :]
        return (
            output,
            g_hidden,
            g_encoder,
            g_self.reshape(self_input.shape),
            g_self_out,
            g_query,
            g_memory.reshape(cross_memory.shape),
            g_cross_out,
            g_expand,
            g_shrink,
            narrow[: 4 * heads].reshape(4, heads),
            narrow[4 * heads :],
            own_wide[:3],
            own_wide[3:6],
            own_wide[6:],
        )

    return body


def solution(mesh):
    rows = P(("dp", "row"), "col")
    weights = (
        P("col", None, "row"),
        P("row", "col"),
        P("col", "row"),
        P("col", None, "row"),
        P("row", "col"),
        P("col", "row"),
        P("row", "col"),
        P(None, "row"),
        P("row"),
        P(None, "col"),
        P(None, "col"),
        P(None, "col"),
    )
    return jax.shard_map(
        layer(mesh),
        mesh=mesh,
        in_specs=(rows, rows, rows, P("dp"), P("dp")) + weights,
        out_specs=(rows, rows, rows) + weights,
        check_vma=False,
    )
```

```python
import functools
import math

import jax
import jax.numpy as jnp
from jax import lax
from jax.experimental import pallas as pl
from jax.experimental.pallas import tpu as pltpu
from jax.sharding import PartitionSpec as P

HEAD_DIM = 64
SLOT = 1024
BF = jnp.bfloat16
F32 = jnp.float32


def tie(*values):
    return lax.optimization_barrier(values)


def dot(left, right):
    return jnp.dot(left, right, preferred_element_type=F32)


def dot_flip(left, right):
    return lax.dot_general(left, right, (((1,), (1,)), ((), ())), preferred_element_type=F32)


def outer_sum(left, right):
    return lax.dot_general(left, right, (((0,), (0,)), ((), ())), preferred_element_type=F32)

def in_vmem(body, name, scalars, arrays, outs):
    count = len(arrays)

    def kernel(info, *refs):
        body(info, refs[:count], refs[count:])

    def spec(shape):
        return pl.BlockSpec(shape, lambda i, info: (0,) * len(shape))

    def spec_in(array):
        if not isinstance(array, tuple):
            return spec(array.shape)
        whole, at = array
        rest = whole.shape[1:]
        return pl.BlockSpec((None, *rest), lambda i, info: (at,) + (0,) * len(rest))

    return pl.pallas_call(
        kernel,
        out_shape=outs,
        grid_spec=pltpu.PrefetchScalarGridSpec(
            num_scalar_prefetch=1,
            grid=(1,),
            in_specs=[spec_in(a) for a in arrays],
            out_specs=[spec(o.shape) for o in outs],
        ),
        compiler_params=pltpu.CompilerParams(vmem_limit_bytes=56 * 2**20),
        cost_estimate=small_cost(),
        name=name,
    )(scalars, *[a[0] if isinstance(a, tuple) else a for a in arrays])


def lanes_at(start):
    return pl.ds(pl.multiple_of(start, 128), 128)


def join_columns(pieces, places):
    n, rows, width = pieces.shape

    def body(info, ins, outs):
        for i in range(n):
            start = pl.multiple_of(info[i] * width, width)
            outs[0][:, pl.ds(start, width)] = ins[0][i]

    out = jax.ShapeDtypeStruct((rows, width * n), pieces.dtype)
    return in_vmem(body, "join_columns", jnp.stack(places), [pieces], [out])[0]


def cut_columns(values, n_col, col):
    rows, width = values.shape[0], values.shape[1] // n_col

    def body(info, ins, outs):
        for owner in range(n_col):
            start = pl.multiple_of(lax.rem(info[0] - owner + n_col, n_col) * width, width)
            outs[0][owner] = ins[0][:, pl.ds(start, width)]

    out = jax.ShapeDtypeStruct((n_col, rows, width), values.dtype)
    return in_vmem(body, "cut_columns", col[None], [values], [out])[0]


def join_rows(pieces, own):
    seqs, rows, width = pieces[0].shape

    def body(info, ins, outs):
        for i in range(2):
            share = info[0] if i == 0 else 1 - info[0]
            for s in range(seqs):
                start = pl.multiple_of((2 * s + share) * rows, rows)
                outs[0][pl.ds(start, rows), :] = ins[i][s].astype(F32)

    out = jax.ShapeDtypeStruct((2 * seqs * rows, width), F32)
    return in_vmem(body, "join_rows", own[None], list(pieces), [out])[0]


def as_chunk(entries, first, brought):
    return entries, (brought[0], 1 if first == 1 else 0), brought[1]


def sum_chunks(chunks, n_col, col, apart):
    operands, plans = [], []
    total_rows = 0
    for entries, got, last in chunks:
        pieces = []
        for grad, low, high in entries:
            pieces.append((len(operands), low, high))
            operands.append((grad, 0))
        plans.append((pieces, len(operands), len(operands) + 1))
        operands += [got, last]
        total_rows += sum(high - low for _, low, high in entries)
    width = chunks[0][0][0][0].shape[2] // n_col

    def body(info, ins, outs):
        for k in range(n_col):
            if apart:
                start, target = k * width, outs[k]
            else:
                start, target = lax.rem(info[0] - k + n_col, n_col) * width, outs[0].at[k]
            columns = pl.ds(pl.multiple_of(start, width), width)
            row = 0
            for pieces, got, last in plans:
                inner = 0
                for at, low, high in pieces:
                    rows = slice(inner, inner + high - low)
                    terms = [ins[at][low:high, columns], ins[got][rows, columns], ins[last][rows, columns]]
                    target[row : row + high - low, :] = sum(t.astype(F32) for t in terms).astype(BF)
                    row += high - low
                    inner += high - low

    if apart:
        outs = [jax.ShapeDtypeStruct((total_rows, width), BF)] * n_col
    else:
        outs = [jax.ShapeDtypeStruct((n_col, total_rows, width), BF)]
    return in_vmem(body, "sum_chunks", col[None], operands, outs)


def finish(which, parts, layout, size, width):
    n = len(parts)
    operands = [o for part in parts for o, _ in part]
    outs = []
    for groups, turned in layout:
        shape = (width, groups, n * size) if groups > 1 else (width, n * size)
        outs.append(jax.ShapeDtypeStruct(shape if turned else (n * size, width), F32))

    def body(info, ins, outs):
        used = 0
        for i, part in enumerate(parts):
            refs = ins[used : used + len(part)]
            used += len(part)
            row = 0
            for (groups, turned), target in zip(layout, outs):
                for g in range(groups):
                    at = max(x for x in range(len(part)) if part[x][1] <= row)
                    block = refs[at][row - part[at][1] : row - part[at][1] + size, :].astype(F32)
                    start = pl.multiple_of(info[i] * size, size)
                    if turned and groups > 1:
                        target[:, g, pl.ds(start, size)] = block.T
                    elif turned:
                        target[:, pl.ds(start, size)] = block.T
                    else:
                        target[pl.ds(start, size), :] = block
                    row += size

    return in_vmem(body, "finish", which, operands, outs)


class Plan:
    def __init__(self, mesh):
        self.n_row = mesh.shape["row"]
        self.n_col = mesh.shape["col"]
        self.share = SLOT // self.n_row
        self.row = lax.axis_index("row")
        self.col = lax.axis_index("col")
        self.pair = self.n_row == 2
        self.offset = self.row * self.share if self.pair else jnp.int32(0)
        self.positions = (jnp.arange(SLOT, dtype=jnp.int32) + self.offset) % SLOT
        self.own_positions = self.row * self.share + jnp.arange(self.share, dtype=jnp.int32)

    def swap(self, values):
        return lax.ppermute(values, "row", [(0, 1), (1, 0)])

    def shift(self, values, k):
        n = self.n_col
        return lax.ppermute(values, "col", [(i, (i + k) % n) for i in range(n)])

    def block(self, other):
        return (self.col - other) % self.n_col

    def reorder(self, blocks):
        return jnp.stack(
            [lax.dynamic_index_in_dim(blocks, self.block(i), 0, keepdims=False) for i in range(self.n_col)]
        )

    def gather_rows(self, values):
        if self.pair:
            return jnp.concatenate([values, self.swap(values)], axis=0)
        return lax.all_gather(values, "row", axis=0, tiled=True)

    def scatter_product(self, left, right, flipped=False):
        times = dot_flip if flipped else dot
        if self.pair:
            away = self.swap(times(left[self.share :], right))
            return times(left[: self.share], right) + away
        return lax.psum_scatter(times(left, right), "row", scatter_dimension=0, tiled=True)

    def sort(self, values):
        width = values.shape[1]
        if self.pair and self.n_col == 4:
            parts = values.reshape(2, 2, self.share, width)
            keep = lax.dynamic_index_in_dim(parts, self.row, 1, keepdims=False)
            take = self.swap(lax.dynamic_index_in_dim(parts, 1 - self.row, 1, keepdims=False))
            ordered = jnp.zeros((4, self.share, width), BF)
            ordered = lax.dynamic_update_slice_in_dim(ordered, keep, 2 * self.row, axis=0)
            ordered = lax.dynamic_update_slice_in_dim(ordered, take, 2 - 2 * self.row, axis=0)
            return ordered
        whole = lax.all_gather(values, "row", axis=0, tiled=True)
        parts = whole.reshape(self.n_col, self.n_row, self.share, width)
        return lax.dynamic_index_in_dim(parts, self.row, 1, keepdims=False)

    def spread(self, ordered):
        return lax.all_to_all(ordered, "col", 0, 0, tiled=True)

    def spread_end(self, takes):
        if self.share % 128 == 0:
            return join_columns(takes, [self.block(i) for i in range(self.n_col)])
        return jnp.transpose(self.reorder(takes), (1, 0, 2)).reshape(self.share, -1)

    def collect(self, values):
        return self.deal(self.cut(values))

    def cut(self, values):
        width = values.shape[1] // self.n_col
        if self.share % 128 == 0:
            return cut_columns(values, self.n_col, self.col)
        return self.reorder(jnp.transpose(values.reshape(self.share, self.n_col, width), (1, 0, 2)))

    def deal(self, blocks):
        return lax.all_to_all(blocks, "col", 0, 0, tiled=True)

    def collect_end(self, moved):
        if self.pair and self.n_col == 4:
            keep = lax.dynamic_slice_in_dim(moved, 2 * self.row, 2, axis=0)
            take = self.swap(lax.dynamic_slice_in_dim(moved, 2 - 2 * self.row, 2, axis=0))
            return join_rows([keep, take], self.row)
        whole = lax.all_gather(moved, "row", axis=1, tiled=True).reshape(-1, moved.shape[2])
        rows = whole.shape[0] // self.n_row
        return lax.dynamic_slice_in_dim(whole, self.row * rows, rows, axis=0).astype(F32)


def normalize(residual, gain_row, shift_row):
    center = jnp.mean(residual, axis=-1, keepdims=True)
    moved = residual - center
    inverse = lax.rsqrt(jnp.mean(moved * moved, axis=-1, keepdims=True) + 1e-05)
    normal = moved * inverse
    return normal * gain_row + shift_row, normal, inverse


def norm_back(upstream, normal, inverse, gain_row):
    scaled = upstream * gain_row
    plain = jnp.mean(scaled, axis=-1, keepdims=True)
    cross = jnp.mean(scaled * normal, axis=-1, keepdims=True)
    return inverse * (scaled - plain - normal * cross)


def gelu_and_slope(values):
    cdf = 0.5 + 0.5 * lax.erf(values * math.sqrt(0.5))
    density = jnp.exp(-0.5 * values * values) * (1.0 / math.sqrt(2.0 * math.pi))
    return (values * cdf).astype(BF), (cdf + values * density).astype(BF)


LANES = 2 * HEAD_DIM
SPAN = 256
NEVER = -1000000000.0


def dot_last(left, right):
    return lax.dot_general(left, right, (((1,), (1,)), ((), ())), preferred_element_type=F32)


def place_of(start, offset):
    return pl.multiple_of(lax.rem(start + offset, SLOT), SPAN)


def heads_apart(rows):
    low = lax.broadcasted_iota(jnp.int32, rows.shape, 1) < HEAD_DIM
    none = jnp.zeros_like(rows)
    return jnp.where(low, rows, none), jnp.where(low, none, rows)


def key_spans(count):
    if count == 1:
        return [(0, SPAN)]
    return [(0, (count - 1) * SPAN), ((count - 1) * SPAN, count * SPAN)]


def score_spans(keys_ref, query, count, limit):
    parts = []
    for start, stop in key_spans(count):
        scores = dot_last(keys_ref[start:stop, :], query)
        if stop == count * SPAN:
            places = lax.broadcasted_iota(jnp.int32, scores.shape, 0)
            if limit is None:
                allowed = places <= lax.broadcasted_iota(jnp.int32, scores.shape, 1)
            else:
                allowed = places < limit - start
            scores = jnp.where(allowed, scores, NEVER)
        parts.append(scores)
    return parts


def for_each_block(causal, whole, query_length, key_length, run, skip):
    blocks = SLOT // SPAN
    half = blocks // 2
    spans = lax.div(key_length + (SPAN - 1), SPAN)
    short = query_length <= half * SPAN
    for count in (None,) if causal else range(1, blocks + 1):
        chosen = True if causal else spans == count
        items = [(i * SPAN, i + 1 if causal else count) for i in range(blocks)]
        if whole:
            pl.when(short & chosen)(functools.partial(run, *items[:half]))
            pl.when(jnp.logical_not(short) & chosen)(functools.partial(run, *items))
            continue

        @pl.when(chosen)
        def _(count=count):
            @pl.loop(0, jnp.where(short, 1, 2))
            def _(i):
                run(*[(pl.multiple_of((2 * i + k) * SPAN, SPAN), count) for k in range(2)])

    @pl.when(short)
    def _():
        for i in range(half, blocks):
            skip(i * SPAN)


def forward_kernel(causal, info, query_ref, key_ref, value_ref, out_ref, logsum_ref, keys, values_t):
    offset, query_length, key_length = info[0], info[1], info[2]
    half = SLOT // 2
    for start in (0, half):
        stored = place_of(start, offset)
        keys[start : start + half, :] = key_ref[pl.ds(stored, half), :]
        values_t[:, start : start + half] = value_ref[pl.ds(stored, half), :].T

    def run(*items):
        tasks = []
        for start, count in items:
            scaled = query_ref[pl.ds(place_of(start, offset), SPAN), :] * (1.0 / math.sqrt(HEAD_DIM))
            tasks += [(start, count, head, query) for head, query in enumerate(heads_apart(scaled))]

        def scores_of(task):
            return score_spans(keys, task[3], task[1], None if causal else key_length)

        outs = []
        ahead = scores_of(tasks[0])
        for at, (start, count, head, _) in enumerate(tasks):
            parts = ahead
            if at + 1 < len(tasks):
                ahead = scores_of(tasks[at + 1])
            highest = functools.reduce(jnp.maximum, [jnp.max(s, axis=0, keepdims=True) for s in parts])
            raised = [jnp.exp(s - highest) for s in parts]
            below = sum(jnp.sum(e, axis=0, keepdims=True) for e in raised)
            mixed = sum(
                jnp.dot(
                    values_t[head * HEAD_DIM : (head + 1) * HEAD_DIM, a:b],
                    e.astype(BF),
                    preferred_element_type=F32,
                )
                for (a, b), e in zip(key_spans(count), raised)
            )
            outs.append(mixed * (1.0 / below))
            logsum_ref[0, head : head + 1, pl.ds(start, SPAN)] = highest + jnp.log(below)
            if head == 1:
                both = jnp.concatenate(outs[at - 1 : at + 1], axis=0)
                out_ref[pl.ds(place_of(start, offset), SPAN), :] = both.T.astype(BF)

    def skip(start):
        out_ref[pl.ds(place_of(start, offset), SPAN), :] = jnp.zeros((SPAN, LANES), BF)

    for_each_block(causal, True, query_length, key_length, run, skip)


def backward_kernel(
    causal, info, query_ref, key_ref, value_ref, up_ref, logsum_ref, *refs
):
    if causal:
        packed_ref, keys, keys_t, values, key_sum, value_sum = refs
        query_out, other_out = packed_ref, packed_ref
        base = LANES
    else:
        query_out, other_out, keys, keys_t, values, key_sum, value_sum = refs
        base = 0
    offset, query_length, key_length = info[0], info[1], info[2]
    half = SLOT // 2
    for start in (0, half):
        stored = place_of(start, offset)
        block = key_ref[pl.ds(stored, half), :]
        keys[start : start + half, :] = block
        keys_t[:, start : start + half] = block.T
        values[start : start + half, :] = value_ref[pl.ds(stored, half), :]
    key_sum[...] = jnp.zeros_like(key_sum)
    value_sum[...] = jnp.zeros_like(value_sum)
    factor = 1.0 / math.sqrt(HEAD_DIM)

    def run(*items):
        tasks = []
        for start, count in items:
            stored = place_of(start, offset)
            queries = heads_apart(query_ref[pl.ds(stored, SPAN), :] * factor)
            ups = heads_apart(up_ref[pl.ds(stored, SPAN), :])
            tasks += [(start, count, head, queries[head], ups[head]) for head in range(2)]

        def products_of(task):
            _, count, _, query, up = task
            parts = score_spans(keys, query, count, None if causal else key_length)
            return parts, [dot_last(values[a:b, :], up) for a, b in key_spans(count)]

        outs, weights, grads = [], [], []
        ahead = products_of(tasks[0])
        for at, (start, count, head, _, _) in enumerate(tasks):
            parts, pulls = ahead
            if at + 1 < len(tasks):
                ahead = products_of(tasks[at + 1])
            logsum = logsum_ref[0, head : head + 1, pl.ds(start, SPAN)]
            parts = [jnp.exp(s - logsum) for s in parts]
            inner = sum(jnp.sum(p * g, axis=0, keepdims=True) for p, g in zip(parts, pulls))
            pulls = [(p * (g - inner)).astype(BF) for p, g in zip(parts, pulls)]
            outs.append(
                sum(
                    jnp.dot(
                        keys_t[head * HEAD_DIM : (head + 1) * HEAD_DIM, a:b],
                        g,
                        preferred_element_type=F32,
                    )
                    for (a, b), g in zip(key_spans(count), pulls)
                )
            )
            weights.append([p.astype(BF) for p in parts])
            grads.append(pulls)
            if head == 0:
                continue
            both = jnp.concatenate(outs[at - 1 : at + 1], axis=0) * factor
            query_out[pl.ds(place_of(start, offset), SPAN), 0:LANES] = both.T.astype(BF)
            for part, (a, b) in enumerate(key_spans(count)):
                value_sum[a:b, :] += sum(
                    jnp.dot(weights[t][part], tasks[t][4], preferred_element_type=F32) for t in (at - 1, at)
                )
                key_sum[a:b, :] += sum(
                    jnp.dot(grads[t][part], tasks[t][3], preferred_element_type=F32) for t in (at - 1, at)
                )

    def skip(start):
        query_out[pl.ds(place_of(start, offset), SPAN), 0:LANES] = jnp.zeros((SPAN, LANES), BF)

    for_each_block(causal, causal, query_length, key_length, run, skip)
    for start in (0, half):
        stored = place_of(start, offset)
        other_out[pl.ds(stored, half), base : base + LANES] = key_sum[start : start + half, :].astype(BF)
        other_out[pl.ds(stored, half), base + LANES : base + 2 * LANES] = value_sum[
            start : start + half, :
        ].astype(BF)


def column_block(width, of):
    return pl.BlockSpec((SLOT, width), lambda i, info: (0, of(i)))


LOGSUM_BLOCK = pl.BlockSpec((1, 2, SLOT), lambda i, info: (i, 0, 0))


def attention_cost():
    return pl.CostEstimate(flops=2 * 10**10, bytes_accessed=2**20, transcendentals=0)


def small_cost():
    return pl.CostEstimate(flops=0, bytes_accessed=2**16, transcendentals=0)


def attend(causal, info, query, keys, pairs):
    step = 3 if causal else 2
    first = 1 if causal else 0
    return pl.pallas_call(
        functools.partial(forward_kernel, causal),
        out_shape=(
            jax.ShapeDtypeStruct((SLOT, pairs * LANES), BF),
            jax.ShapeDtypeStruct((pairs, 2, SLOT), F32),
        ),
        grid_spec=pltpu.PrefetchScalarGridSpec(
            num_scalar_prefetch=1,
            grid=(pairs,),
            in_specs=[
                column_block(LANES, (lambda i: 3 * i) if causal else (lambda i: i)),
                column_block(LANES, lambda i: step * i + first),
                column_block(LANES, lambda i: step * i + first + 1),
            ],
            out_specs=(column_block(LANES, lambda i: i), LOGSUM_BLOCK),
            scratch_shapes=[pltpu.VMEM((SLOT, LANES), BF), pltpu.VMEM((LANES, SLOT), BF)],
        ),
        compiler_params=pltpu.CompilerParams(vmem_limit_bytes=48 * 2**20),
        cost_estimate=attention_cost(),
        name="attend",
    )(info, query, keys, keys)


def attend_back(causal, info, query, keys, logsum, upstream, pairs):
    step = 3 if causal else 2
    first = 1 if causal else 0
    if causal:
        out_shape = jax.ShapeDtypeStruct((SLOT, pairs * 3 * LANES), BF)
        out_specs = column_block(3 * LANES, lambda i: i)
    else:
        out_shape = (
            jax.ShapeDtypeStruct((SLOT, pairs * LANES), BF),
            jax.ShapeDtypeStruct((SLOT, pairs * 2 * LANES), BF),
        )
        out_specs = (column_block(LANES, lambda i: i), column_block(2 * LANES, lambda i: i))
    return pl.pallas_call(
        functools.partial(backward_kernel, causal),
        out_shape=out_shape,
        grid_spec=pltpu.PrefetchScalarGridSpec(
            num_scalar_prefetch=1,
            grid=(pairs,),
            in_specs=[
                column_block(LANES, (lambda i: 3 * i) if causal else (lambda i: i)),
                column_block(LANES, lambda i: step * i + first),
                column_block(LANES, lambda i: step * i + first + 1),
                column_block(LANES, lambda i: i),
                LOGSUM_BLOCK,
            ],
            out_specs=out_specs,
            scratch_shapes=[
                pltpu.VMEM((SLOT, LANES), BF),
                pltpu.VMEM((LANES, SLOT), BF),
                pltpu.VMEM((SLOT, LANES), BF),
                pltpu.VMEM((SLOT, LANES), F32),
                pltpu.VMEM((SLOT, LANES), F32),
            ],
        ),
        compiler_params=pltpu.CompilerParams(vmem_limit_bytes=48 * 2**20),
        cost_estimate=attention_cost() if causal else small_cost(),
        name="attend_back",
    )(info, query, keys, keys, upstream, logsum)


def build_mask(positions, length, causal):
    allowed = jnp.broadcast_to(positions[None, :] < length, (SLOT, SLOT))
    if causal:
        allowed = allowed & (positions[None, :] <= positions[:, None])
    return allowed


def score_block(query, key, allowed):
    factor = 1.0 / math.sqrt(HEAD_DIM)
    scores = jnp.einsum("qhd,khd->hqk", query, key, preferred_element_type=F32) * factor
    return jnp.where(allowed[None], scores, -1000000000.0)


def split_heads(values):
    return values.reshape(SLOT, -1, HEAD_DIM)


def attention_forward(query, key, value, allowed):
    query, key, value = (split_heads(v) for v in (query, key, value))
    scores = score_block(query, key, allowed)
    highest = jnp.max(scores, axis=-1, keepdims=True)
    raised = jnp.exp(scores - highest)
    denominator = jnp.sum(raised, axis=-1, keepdims=True)
    weights = (raised / denominator).astype(BF)
    mixture = jnp.einsum("hqk,khd->qhd", weights, value, preferred_element_type=F32)
    return mixture.reshape(SLOT, -1).astype(BF), highest + jnp.log(denominator)


def attention_backward(query, key, value, allowed, logsum, upstream):
    query, key, value, upstream = (split_heads(v) for v in (query, key, value, upstream))
    factor = 1.0 / math.sqrt(HEAD_DIM)
    weights = jnp.exp(score_block(query, key, allowed) - logsum)
    value_grad = jnp.einsum("hqk,qhd->khd", weights.astype(BF), upstream, preferred_element_type=F32)
    weight_grad = jnp.einsum("qhd,khd->hqk", upstream, value, preferred_element_type=F32)
    inner = jnp.sum(weights * weight_grad, axis=-1, keepdims=True)
    score_grad = (weights * (weight_grad - inner)).astype(BF)
    query_grad = jnp.einsum("hqk,khd->qhd", score_grad, key, preferred_element_type=F32) * factor
    key_grad = jnp.einsum("hqk,qhd->khd", score_grad, query, preferred_element_type=F32) * factor
    return tuple(g.reshape(SLOT, -1).astype(BF) for g in (query_grad, key_grad, value_grad))


def interleave(arrays, n):
    rows = arrays[0].shape[0]
    return jnp.stack([a.reshape(rows, n, -1) for a in arrays], axis=2).reshape(rows, -1)


def apart(array, n, count):
    rows = array.shape[0]
    parts = array.reshape(rows, n, count, -1)
    return [parts[:, :, i].reshape(rows, -1) for i in range(count)]


def self_attention(plan, packed, length, n):
    if packed.shape[1] == 3 * n * LANES:
        info = jnp.stack([plan.offset, length, length])
        return attend(True, info, packed, packed, n)
    mask = build_mask(plan.positions, length, True)
    return attention_forward(*apart(packed, n, 3), mask)


def self_attention_back(plan, packed, length, n, logsum, upstream):
    if packed.shape[1] == 3 * n * LANES:
        info = jnp.stack([plan.offset, length, length])
        return attend_back(True, info, packed, packed, logsum, upstream, n)
    mask = build_mask(plan.positions, length, True)
    return interleave(attention_backward(*apart(packed, n, 3), mask, logsum, upstream), n)


def cross_attention(plan, query, memory, query_length, key_length, n):
    if query.shape[1] == n * LANES:
        info = jnp.stack([plan.offset, query_length, key_length])
        return attend(False, info, query, memory, n)
    mask = build_mask(plan.positions, key_length, False)
    return attention_forward(query, *apart(memory, n, 2), mask)


def cross_attention_back(plan, query, memory, query_length, key_length, n, logsum, upstream):
    if query.shape[1] == n * LANES:
        info = jnp.stack([plan.offset, query_length, key_length])
        return attend_back(False, info, query, memory, logsum, upstream, n)
    mask = build_mask(plan.positions, key_length, False)
    first, *rest = attention_backward(query, *apart(memory, n, 2), mask, logsum, upstream)
    return first, interleave(rest, n)


ORDER = (0, 2, 3, 1)


class Group:
    def __init__(self, weights, n):
        self.weights = weights
        self.n = n
        self.plans = []
        row = 0
        for axis, groups, local in weights:
            if axis == 0:
                tall, count = local.shape[0], local.shape[1] // n // 128
            else:
                tall, count = local.shape[0] // n, local.shape[1] // 128
            self.plans.append((row, tall, count))
            row += tall * count
        self.rows = row

    def fits(self):
        return all(
            (local.shape[1] % (groups * self.n * 128) == 0 if axis == 0 else local.shape[0] % (self.n * 128) == 0)
            for axis, groups, local in self.weights
        )

    def local_block(self, ref, at, which, block):
        axis, groups, local = self.weights[at]
        _, tall, count = self.plans[at]
        if axis == 0:
            per = count // groups
            i, b = divmod(block, per)
            return ref[:, lanes_at((i * self.n * per + b) * 128 + which * (per * 128))]
        return ref[pl.ds(pl.multiple_of(which * tall, tall), tall), block * 128 : (block + 1) * 128]

    def pack(self, me):
        def body(info, ins, outs):
            for at, (row, tall, count) in enumerate(self.plans):
                for block in range(count):
                    start = row + block * tall
                    outs[0][start : start + tall, :] = self.local_block(ins[at], at, info[0], block)

        out = jax.ShapeDtypeStruct((self.rows, 128), BF)
        return in_vmem(body, "pack", me[None], [w[2] for w in self.weights], [out])[0]

    def outputs(self, n_col):
        outs = []
        for axis, groups, local in self.weights:
            shape = (local.shape[0] * n_col, local.shape[1]) if axis == 0 else (local.shape[0], local.shape[1] * n_col)
            outs.append(jax.ShapeDtypeStruct(shape, BF))
        return outs

    def fill(self, info, n_col, local_refs, moved_refs, outs):
        half = self.rows * (n_col - 1) // 2
        for at, (row, tall, count) in enumerate(self.plans):
            axis = self.weights[at][0]
            width = self.weights[at][2].shape[1]
            for place, j in enumerate(ORDER):
                for k in range(n_col):
                    for block in range(count):
                        if k == 0:
                            value = self.local_block(local_refs[at], at, info[j], block)
                        else:
                            start = (k - 1) * self.rows + row + block * tall
                            ref = moved_refs[j]
                            if j == 3 and start >= half:
                                ref, start = moved_refs[4], start - half
                            value = ref[start : start + tall, :]
                        if axis == 0:
                            column = (place * count + block) * 128
                            outs[at][k * tall : (k + 1) * tall, column : column + 128] = value
                        else:
                            column = k * width + block * 128
                            outs[at][place * tall : (place + 1) * tall, column : column + 128] = value


def assemble(me, n_col, *groups):
    operands, outs = [], []
    for group, moved in groups:
        operands += [w[2] for w in group.weights] + list(moved)
        outs += group.outputs(n_col)

    def body(info, ins, outs):
        for group, moved in groups:
            count = len(group.weights)
            group.fill(info, n_col, ins[:count], ins[count : count + len(moved)], outs[:count])
            ins, outs = ins[count + len(moved) :], outs[count:]

    which = jnp.stack([me ^ j for j in range(len(ORDER))])
    return in_vmem(body, "assemble", which, operands, outs)


def split_float(values):
    high = lax.reduce_precision(values, 8, 7)
    middle = lax.reduce_precision(values - high, 8, 7)
    low = values - high - middle
    parts = jnp.concatenate([high, middle, low], axis=0).astype(BF)
    parts = jnp.concatenate([parts[:, i : i + 128] for i in range(0, parts.shape[1], 128)], axis=0)
    return jnp.pad(parts, ((0, -parts.shape[0] % 16), (0, 0)))


def join_float(rows, shape):
    n, width = shape
    count = width // 128
    parts = rows[:, : 3 * n * count].reshape(rows.shape[0], count, 3, n, 128).astype(F32)
    whole = parts[:, :, 0] + (parts[:, :, 1] + parts[:, :, 2])
    return jnp.moveaxis(whole, 1, 2).reshape(rows.shape[0], n, width)


def pick_others(every, at, rows, n_col, col):
    width = every.shape[2]
    return pl.pallas_call(
        lambda info, source, target: target.__setitem__(Ellipsis, source[...]),
        out_shape=jax.ShapeDtypeStruct(((n_col - 1) * rows, width), every.dtype),
        grid_spec=pltpu.PrefetchScalarGridSpec(
            num_scalar_prefetch=1,
            grid=(n_col - 1,),
            in_specs=[
                pl.BlockSpec(
                    (None, rows, width), lambda k, info: (lax.rem(info[0] - k - 1 + n_col, n_col), at, 0)
                )
            ],
            out_specs=pl.BlockSpec((rows, width), lambda k, info: (k, 0)),
        ),
        cost_estimate=small_cost(),
        name="pick_others",
    )(col[None], every)


class Blocks:
    def __init__(self, mesh, plan):
        self.n = mesh.shape["dp"]
        assert self.n == len(ORDER)
        self.plan = plan
        self.me = lax.axis_index("dp")

    def hop(self, values, step):
        return lax.ppermute(values, "dp", [(i, i ^ step) for i in range(self.n)])

    def own(self, values, axis, j=0, wait=0):
        shape = values.shape
        parts = values.reshape(shape[:axis] + (self.n, shape[axis] // self.n) + shape[axis + 1 :])
        return lax.dynamic_index_in_dim(parts, (self.me ^ j) + wait, axis, keepdims=False)

    def weave(self, values):
        return jnp.stack([self.own(values, values.ndim - 1, j) for j in ORDER], axis=-2)

    def unweave(self, values):
        order = jnp.array([ORDER.index(j) for j in range(self.n)])
        return jnp.concatenate(
            [
                lax.dynamic_index_in_dim(values, order[self.me ^ q], 0, keepdims=False)
                for q in range(self.n)
            ]
        )

    def others_by_shift(self, piece):
        return jnp.concatenate([self.plan.shift(piece, k) for k in range(1, self.plan.n_col)], axis=0)

    def others_by_gather(self, piece, count, extra):
        total_rows = piece.shape[0]
        if extra is not None:
            piece = jnp.concatenate([piece, extra], axis=0)
        every = lax.all_gather(piece, "col", axis=0)
        rows = total_rows // count
        picked = [pick_others(every, i, rows, self.plan.n_col, self.plan.col) for i in range(count)]
        return picked, every[:, total_rows:]

    def hops(self, others):
        return self.hop(others, 1), self.hop(others, 2)

    def corner(self, over):
        half = over[0].shape[0] // 2
        return self.hop(over[1][:half], 1), self.hop(over[0][half:], 2)

    def whole(self, weight):
        axis, groups, local = weight
        every = self.plan.reorder(lax.all_gather(local, "col", axis=0))
        if axis == 0:
            every = every.reshape(-1, groups, local.shape[1] // groups)
            return jnp.stack([self.weave(every[:, i]) for i in range(groups)], axis=2).reshape(every.shape[0], -1)
        every = jnp.moveaxis(every, 0, 1).reshape(local.shape[0], -1)
        parts = every.reshape(self.n, -1, every.shape[1])
        picked = [lax.dynamic_index_in_dim(parts, self.me ^ j, 0, keepdims=False) for j in ORDER]
        return jnp.concatenate(picked, axis=0)

    def product(self, hidden, model):
        grad = outer_sum(hidden, model).astype(BF)
        return grad.reshape(self.n, -1, grad.shape[1])

    def reduce_start(self, entries, first):
        return self.hop(self.reduce_send(entries, first), first)

    def reduce_send(self, entries, first):
        a, b = (2, 4) if first == 1 else (1, 3)
        sends = [grad[a:b, low:high] for grad, low, high in entries]
        return sends[0] if len(sends) == 1 else jnp.concatenate(sends, axis=1)

    def reduce_next(self, entries, first, got):
        to_middle, to_base = (0, 1) if first == 1 else (1, 0)
        place = 1 if first == 1 else 3
        keeps = [grad[place, low:high] for grad, low, high in entries]
        middle = keeps[0] if len(keeps) == 1 else jnp.concatenate(keeps, axis=0)
        return got, self.hop(middle + got[to_middle], 3 - first)

    def plain(self, hidden, model, groups, turned):
        plan = self.plan
        grad = outer_sum(hidden, model).astype(BF)
        parts = grad.reshape(self.n, groups, -1, grad.shape[1])
        natural = [
            lax.dynamic_index_in_dim(parts, jnp.array([ORDER.index(j) for j in range(self.n)])[self.me ^ q], 0)
            for q in range(self.n)
        ]
        grad = jnp.moveaxis(jnp.concatenate(natural, axis=0), 1, 0).reshape(grad.shape[0], plan.n_col, -1)
        grad = lax.psum(plan.reorder(jnp.moveaxis(grad, 1, 0)), "dp")
        grad = lax.psum_scatter(grad, "col", scatter_dimension=0, tiled=False).astype(F32)
        return grad.T if turned else grad


def total(values, mesh, axes):
    for axis in axes:
        size = mesh.shape[axis]
        step = 1
        while step < size:
            values = values + lax.ppermute(values, axis, [(i, i ^ step) for i in range(size)])
            step *= 2
    return values


def layer(mesh):
    def body(
        hidden,
        encoder,
        cotangent,
        answer_length,
        passage_length,
        self_input,
        self_output,
        cross_query,
        cross_memory,
        cross_output,
        expand_weight,
        shrink_weight,
        head_bias,
        expand_bias,
        model_bias,
        norm_gain,
        norm_shift,
    ):
        plan = Plan(mesh)
        blocks = Blocks(mesh, plan)
        n = blocks.n
        me = blocks.me
        width = model_bias.shape[1]
        heads = self_output.shape[0]
        part = heads // n
        hidden_part = expand_bias.shape[0] // n
        answers = lax.dynamic_index_in_dim(answer_length, plan.col, keepdims=False)
        passages = lax.dynamic_index_in_dim(passage_length, plan.col, keepdims=False)
        valid = (plan.own_positions < answers).astype(F32)[:, None]

        own_norms = jnp.concatenate([model_bias, norm_gain, norm_shift])
        group_one = Group([(0, 3, self_input.reshape(width, -1)), (1, 1, self_output)], n)
        group_two = Group(
            [(0, 1, cross_query), (0, 2, cross_memory.reshape(width, -1)), (1, 1, cross_output)], n
        )
        group_three = Group([(0, 1, expand_weight), (1, 1, shrink_weight)], n)
        group_expand, group_shrink = Group([(0, 1, expand_weight)], n), Group([(1, 1, shrink_weight)], n)
        tiled = plan.pair and all(g.fits() for g in (group_one, group_two, group_expand, group_shrink))
        if tiled:
            others_one = blocks.others_by_shift(group_one.pack(me))
            hidden = plan.sort(hidden)
            over_one = blocks.hops(others_one)
            corner_one = blocks.corner(over_one)
            w_self, w_self_out = assemble(me, plan.n_col, (group_one, (others_one, *over_one, *corner_one)))
        else:
            hidden = plan.sort(hidden)
            w_self, w_self_out = (blocks.whole(w) for w in group_one.weights)
            w_query, w_memory, w_cross_out = (blocks.whole(w) for w in group_two.weights)
            w_expand, w_shrink = (blocks.whole(g.weights[0]) for g in (group_expand, group_shrink))
        x_takes = plan.spread(hidden)
        encoder, cotangent = plan.sort(encoder), plan.sort(cotangent)

        if tiled:
            pieces = [group_two.pack(me), group_three.pack(me)]
            others_one, pieces, carried = tie(others_one, pieces, split_float(own_norms))
            (others_two,), extra = blocks.others_by_gather(pieces[0], 1, carried)
            (others_a, others_b), _ = blocks.others_by_gather(pieces[1], 2, None)
            norms = plan.reorder(join_float(extra, own_norms.shape))
        if not tiled:
            norms = plan.reorder(lax.all_gather(own_norms, "col", axis=0))
        norms = jnp.moveaxis(norms, 0, 1).reshape(own_norms.shape[0], -1)
        bias_rows, gain_rows, shift_rows = norms[:3], norms[3:6], norms[6:]

        head_parts = blocks.weave(head_bias)
        none = jnp.zeros((n, part), F32)
        self_bias = jnp.stack([head_parts[0], none, head_parts[1]], axis=1).reshape(-1)
        query_bias = head_parts[2].reshape(-1)
        memory_bias = jnp.stack([none, head_parts[3]], axis=1).reshape(-1)
        hidden_bias = blocks.weave(expand_bias).reshape(-1)

        own_x = plan.spread_end(x_takes)
        full_x = plan.gather_rows(own_x)
        packed = (dot(full_x, w_self) + self_bias).astype(BF)
        if tiled:
            packed, others_two, encoder, cotangent = tie(packed, others_two, encoder, cotangent)
            over_two = blocks.hops(others_two)
        encoder_takes = plan.spread(encoder)
        mixture, self_logsum = self_attention(plan, packed, answers, n)
        if tiled:
            mixture, over_two = tie(mixture, over_two)
            corner_two = blocks.corner(over_two)
        branch = plan.scatter_product(mixture, w_self_out) + bias_rows[0]
        if tiled:
            branch, others_a = tie(branch, others_a)
            over_a = blocks.hops(others_a)
        normed, normal_one, inverse_one = normalize(own_x.astype(F32) + branch, gain_rows[0], shift_rows[0])
        own_first = normed.astype(BF)
        if tiled:
            own_first, corner_two, others_b, encoder_takes, cotangent = tie(
                own_first, corner_two, others_b, encoder_takes, cotangent
            )
            over_b = blocks.hops(others_b)
        own_encoder = plan.spread_end(encoder_takes)
        full_encoder = plan.gather_rows(own_encoder)
        full_first = plan.gather_rows(own_first)
        if tiled:
            w_query, w_memory, w_cross_out = assemble(
                me, plan.n_col, (group_two, (others_two, *over_two, *corner_two))
            )
        memory = (dot(full_encoder, w_memory) + memory_bias).astype(BF)
        cross_q = (dot(full_first, w_query) + query_bias).astype(BF)
        cotangent_takes = plan.spread(cotangent)
        if tiled:
            cross_q, memory, over_a, over_b = tie(cross_q, memory, over_a, over_b)
            corner_a = blocks.corner(over_a)
            corner_b = blocks.corner(over_b)
        recall, cross_logsum = cross_attention(plan, cross_q, memory, answers, passages, n)
        if tiled:
            recall, corner_a, corner_b, cotangent_takes = tie(recall, corner_a, corner_b, cotangent_takes)
        branch = plan.scatter_product(recall, w_cross_out) + bias_rows[1]
        normed, normal_two, inverse_two = normalize(own_first.astype(F32) + branch, gain_rows[1], shift_rows[1])
        own_second = normed.astype(BF)
        full_second = plan.gather_rows(own_second)
        if tiled:
            w_expand, w_shrink = assemble(
                me,
                plan.n_col,
                (group_expand, (others_a, *over_a, *corner_a)),
                (group_shrink, (others_b, *over_b, *corner_b)),
            )
        expanded = dot(full_second, w_expand) + hidden_bias
        activated, slope = gelu_and_slope(expanded)
        branch = plan.scatter_product(activated, w_shrink) + bias_rows[2]
        normed, normal_three, inverse_three = normalize(
            own_second.astype(F32) + branch, gain_rows[2], shift_rows[2]
        )
        output_takes = plan.collect((normed * valid).astype(BF))

        own_cotangent = plan.spread_end(cotangent_takes)
        up_three = own_cotangent.astype(F32) * valid
        resid_three = norm_back(up_three, normal_three, inverse_three, gain_rows[2])
        own_dshrink = resid_three.astype(BF)
        full_dshrink = plan.gather_rows(own_dshrink)
        if tiled:
            of_shrink = [(blocks.product(activated, full_dshrink), 0, hidden_part)]
            send_shrink = blocks.reduce_send(of_shrink, 1)
            full_dshrink, send_shrink = tie(full_dshrink, send_shrink)
            got_shrink = blocks.hop(send_shrink, 1)
        d_expanded = (dot_flip(full_dshrink, w_shrink) * slope.astype(F32)).astype(BF)
        (d_expanded,) = tie(d_expanded)
        if tiled:
            of_expand = [(blocks.product(d_expanded, full_second), 0, hidden_part)]
            got_expand = blocks.reduce_start(of_expand, 2)
        up_two = resid_three + plan.scatter_product(d_expanded, w_expand, True)
        resid_two = norm_back(up_two, normal_two, inverse_two, gain_rows[1])
        own_dcross = resid_two.astype(BF)
        full_dcross = plan.gather_rows(own_dcross)
        d_recall = dot_flip(full_dcross, w_cross_out).astype(BF)
        d_cross_q, d_memory = cross_attention_back(
            plan, cross_q, memory, answers, passages, n, cross_logsum, d_recall
        )
        if tiled:
            d_cross_q, d_memory, got_shrink, got_expand, output_takes = tie(
                d_cross_q, d_memory, got_shrink, got_expand, output_takes
            )
            chunk_shrink = blocks.reduce_next(of_shrink, 1, got_shrink)
            chunk_expand = blocks.reduce_next(of_expand, 2, got_expand)
            of_cross_a = [
                (blocks.product(d_cross_q, full_first), 0, part),
                (blocks.product(recall, full_dcross), 0, part),
            ]
            of_cross_b = [(blocks.product(d_memory, full_encoder), 0, 2 * part)]
            got_cross_a = blocks.reduce_start(of_cross_a, 1)
            got_cross_b = blocks.reduce_start(of_cross_b, 2)
        up_one = resid_two + plan.scatter_product(d_cross_q, w_query, True)
        resid_one = norm_back(up_one, normal_one, inverse_one, gain_rows[0])
        own_dself = resid_one.astype(BF)
        full_dself = plan.gather_rows(own_dself)
        d_mixture = dot_flip(full_dself, w_self_out).astype(BF)
        encoder_grad_takes = plan.collect(plan.scatter_product(d_memory, w_memory, True).astype(BF))
        if tiled:
            (sums,) = sum_chunks(
                [as_chunk(of_shrink, 1, chunk_shrink), as_chunk(of_expand, 2, chunk_expand)],
                plan.n_col,
                plan.col,
                False,
            )
            grad_self_out = blocks.product(mixture, full_dself)
            d_mixture, sums, grad_self_out = tie(d_mixture, sums, grad_self_out)
            mine_hidden = lax.psum_scatter(sums, "col", scatter_dimension=0, tiled=False)
            chunk_cross_a = blocks.reduce_next(of_cross_a, 1, got_cross_a)
            chunk_cross_b = blocks.reduce_next(of_cross_b, 2, got_cross_b)
        d_packed = self_attention_back(plan, packed, answers, n, self_logsum, d_mixture)
        if tiled:
            d_packed, chunk_cross_a, chunk_cross_b, mine_hidden, encoder_grad_takes = tie(
                d_packed, chunk_cross_a, chunk_cross_b, mine_hidden, encoder_grad_takes
            )
            grad_self = blocks.product(d_packed, full_x)
            of_low = [(grad_self, 0, 2 * part)]
            of_high = [(grad_self, 2 * part, 3 * part), (grad_self_out, 0, part)]
            send_low, send_high = blocks.reduce_send(of_low, 1), blocks.reduce_send(of_high, 2)
            send_low, send_high, d_packed, chunk_cross_a, chunk_cross_b = tie(
                send_low, send_high, d_packed, chunk_cross_a, chunk_cross_b
            )
            got_low, got_high = blocks.hop(send_low, 1), blocks.hop(send_high, 2)
            (sums,) = sum_chunks(
                [as_chunk(of_cross_a, 1, chunk_cross_a), as_chunk(of_cross_b, 2, chunk_cross_b)],
                plan.n_col,
                plan.col,
                False,
            )
            mine_cross = lax.psum_scatter(sums, "col", scatter_dimension=0, tiled=False)

        def rows_of(values):
            return jnp.sum(values, axis=0, dtype=F32)

        wide = jnp.stack(
            [rows_of(v) for v in (own_dself, own_dcross, own_dshrink)]
            + [rows_of(u * v) for u, v in ((up_one, normal_one), (up_two, normal_two), (up_three, normal_three))]
            + [rows_of(v) for v in (up_one, up_two, up_three)]
        )
        packed_sums = rows_of(d_packed).reshape(n, 3, part)
        memory_sums = rows_of(d_memory).reshape(n, 2, part)
        narrow = jnp.concatenate(
            [
                blocks.unweave(v)
                for v in (
                    packed_sums[:, 0],
                    packed_sums[:, 2],
                    rows_of(d_cross_q).reshape(n, part),
                    memory_sums[:, 1],
                    rows_of(d_expanded).reshape(n, hidden_part),
                )
            ]
        )
        wide = total(wide, mesh, ("row",))
        wide = plan.reorder(jnp.moveaxis(wide.reshape(9, plan.n_col, width), 1, 0))
        small = jnp.concatenate([wide.reshape(-1), narrow])

        hidden_grad = (resid_one + plan.scatter_product(d_packed, w_self, True)).astype(BF)
        if tiled:
            small = small + blocks.hop(small, 1)
        hidden_grad = plan.cut(hidden_grad)
        if tiled:
            hidden_grad, got_low, got_high = tie(hidden_grad, got_low, got_high)
        hidden_takes = plan.deal(hidden_grad)
        if not tiled:
            small = total(small, mesh, ("dp", "col"))
        if tiled:
            g_encoder = plan.collect_end(encoder_grad_takes)
            small, output_takes, g_encoder = tie(small, output_takes, g_encoder)
            chunk_low = blocks.reduce_next(of_low, 1, got_low)
            chunk_high = blocks.reduce_next(of_high, 2, got_high)
            small = small + blocks.hop(small, 2)
            output = plan.collect_end(output_takes)
            ready = lax.all_gather(mine_hidden, "dp", axis=0)
            g_shrink, g_expand = finish(
                jnp.arange(n), [[((ready, q), 0)] for q in range(n)], [(1, False), (1, True)], hidden_part, width
            )
            chunk_low, chunk_high, small, output, hidden_takes = tie(
                chunk_low, chunk_high, small, output, hidden_takes
            )
            own, *rest = sum_chunks(
                [as_chunk(of_low, 1, chunk_low), as_chunk(of_high, 2, chunk_high)],
                plan.n_col,
                plan.col,
                True,
            )
            arrived = [own] + [plan.shift(r, -1 - k) for k, r in enumerate(rest)]
            small = small + lax.ppermute(small, "col", [(i, i ^ 1) for i in range(plan.n_col)])
            g_hidden = plan.collect_end(hidden_takes)
            ready = lax.all_gather(mine_cross, "dp", axis=0)
            arrived, g_hidden, g_shrink, g_expand, small, ready = tie(
                arrived, g_hidden, g_shrink, g_expand, small, ready
            )
            mine_self = sum(r.astype(F32) for r in arrived).astype(BF)
            over_self = blocks.hops(mine_self)
            small = small + lax.ppermute(small, "col", [(i, i ^ 2) for i in range(plan.n_col)])
            g_query, g_cross_out, g_memory = finish(
                jnp.arange(n),
                [[((ready, q), 0)] for q in range(n)],
                [(1, True), (1, False), (2, True)],
                part,
                width,
            )
            over_self, g_query, g_cross_out, g_memory = tie(over_self, g_query, g_cross_out, g_memory)
            corner_self = blocks.corner(over_self)
            g_self, g_self_out = finish(
                jnp.stack([me ^ j for j in range(n)]),
                [
                    [(mine_self, 0)],
                    [(over_self[0], 0)],
                    [(over_self[1], 0)],
                    [(corner_self[0], 0), (corner_self[1], 2 * part)],
                ],
                [(3, True), (1, False)],
                part,
                width,
            )
        else:
            g_shrink = blocks.plain(activated, full_dshrink, 1, False)
            g_expand = blocks.plain(d_expanded, full_second, 1, True)
            g_query = blocks.plain(d_cross_q, full_first, 1, True)
            g_memory = blocks.plain(d_memory, full_encoder, 2, True)
            g_cross_out = blocks.plain(recall, full_dcross, 1, False)
            g_self = blocks.plain(d_packed, full_x, 3, True)
            g_self_out = blocks.plain(mixture, full_dself, 1, False)
            output, g_encoder, g_hidden = (
                plan.collect_end(t) for t in (output_takes, encoder_grad_takes, hidden_takes)
            )

        own_wide = lax.dynamic_index_in_dim(
            small[: 9 * plan.n_col * width].reshape(plan.n_col, 9, width), plan.col, keepdims=False
        )
        narrow = small[9 * plan.n_col * width :]
        return (
            output,
            g_hidden,
            g_encoder,
            g_self.reshape(self_input.shape),
            g_self_out,
            g_query,
            g_memory.reshape(cross_memory.shape),
            g_cross_out,
            g_expand,
            g_shrink,
            narrow[: 4 * heads].reshape(4, heads),
            narrow[4 * heads :],
            own_wide[:3],
            own_wide[3:6],
            own_wide[6:],
        )

    return body


def solution(mesh):
    rows = P(("dp", "row"), "col")
    weights = (
        P("col", None, "row"),
        P("row", "col"),
        P("col", "row"),
        P("col", None, "row"),
        P("row", "col"),
        P("col", "row"),
        P("row", "col"),
        P(None, "row"),
        P("row"),
        P(None, "col"),
        P(None, "col"),
        P(None, "col"),
    )
    return jax.shard_map(
        layer(mesh),
        mesh=mesh,
        in_specs=(rows, rows, rows, P("dp"), P("dp")) + weights,
        out_specs=(rows, rows, rows) + weights,
        check_vma=False,
    )
```
